32 devices in a mesh: pair: 2 (over x), gx: 4 (over y, core), gy: 4 (over z).
Axes of the slice: x: 2, y: 2, z: 4, core: 2. Of those that a mesh axis runs over, the one named last changes fastest.
Arguments:
- sound_speed_sq: float32 [32, 32, 1024], P('gx', 'gy'), may hold values from 0.5 to 2
- wind_profile: float32 [3, 1024], replicated, may hold values from -0.6 to 0.6
- forward_field: bfloat16 [4, 4, 32, 32, 1024], P(None, None, 'gx', 'gy'), may hold values from -6 to 6
- adjoint_state: float32 [2, 4, 32, 32, 1024], P('pair', None, 'gx', 'gy'), may hold values from -0.3125 to 0.3125
- pair_counts: int32 [2], P('pair'), may hold values from 64 to 256, as said below
- source_cells: int32 [512, 3], P('pair'), may hold values from 0 to 1023, as said below
- receiver_cells: int32 [512, 3], P('pair'), may hold values from 0 to 1023, as said below
- residuals: float32 [512, 4], P('pair'), may hold values from -16 to 16
Outputs:
- kernels: float32 [4, 32, 32, 1024], P(None, 'gx', 'gy', 'pair')
- final_state: float32 [2, 4, 32, 32, 1024], P('pair', None, 'gx', 'gy')
The draws below stay inside these ranges and needn't reach their ends.
Inputs may be any that keep to these rules, and one draw needn't show every extreme that they name: `pair_counts`: one group in every draw has exactly 256 live pairs. `source_cells`: columns are the cell along the first, second and third dimension, each within the grid. `receiver_cells`: columns are the cell along the first, second and third dimension, each within the grid; several pairs may share a cell.
All inputs are finite; a program needn't handle non-finite values.
Results may differ from the reference program's by a relative error of at most 0.00115.
Values may be sent and summed in bfloat16 or wider, within the bound.
No kernel may reach another device: no remote copies, remote signals or barrier semaphores. Data moves between devices by JAX's collectives and lax.ppermute only.
A program may use at most 128 MiB of HBM per device.

```python
import math
import jax
import jax.numpy as jnp

NZ = 1024
PMAX = 256
STEPS = 4
GROUPS = 2
PAIRS = 512
NX = 32
NY = 32


def draw_pair_counts(key, part):
    counts = jax.random.randint(key, (GROUPS,), PMAX // 4, PMAX + 1)
    chosen = jax.random.randint(jax.random.fold_in(key, 7), (), 0, GROUPS)
    return jnp.where(jnp.arange(GROUPS) == chosen, PMAX, counts).astype(jnp.int32)


def station_cells(key):
    first = jax.random.randint(jax.random.fold_in(key, 1), (PAIRS,), 0, NX)
    second = jax.random.randint(jax.random.fold_in(key, 2), (PAIRS,), 0, NY)
    third = jax.random.randint(jax.random.fold_in(key, 3), (PAIRS,), 0, NZ)
    slot = jnp.arange(PAIRS, dtype=jnp.int32)
    first = jnp.where(slot == 0, NX - 1, jnp.where(slot == 1, 0, first))
    second = jnp.where(slot == 0, NY - 1, jnp.where(slot == 1, 0, second))
    third = jnp.where(slot == 0, NZ - 1, jnp.where(slot == 1, 0, third))
    return jnp.stack([first, second, third], axis=1).astype(jnp.int32)


def draw_source_cells(key, part):
    return station_cells(jax.random.fold_in(key, 11))


def draw_receiver_cells(key, part):
    return station_cells(jax.random.fold_in(key, 13))


def level_of(stream_key, extent, cuts, least, largest):
    gain = 1.0
    for dim, parts in cuts:
        heights = jax.random.uniform(jax.random.fold_in(jax.random.fold_in(stream_key, 6), dim), (parts,), jnp.float32, least / len(cuts), largest / len(cuts))
        gain = gain * jnp.repeat(jnp.exp(heights), extent[dim] // parts).reshape((-1,) + (1,) * (len(extent) - 1 - dim))
    return gain


def noise(rng, shape, spread, reach, cuts=(), held_as=jnp.bfloat16):
    entries = spread * jax.random.normal(rng, shape, jnp.float32)
    if cuts:
        entries = entries * level_of(rng, shape, cuts, -0.22, 0.18)
    return jnp.clip(entries, -reach, reach).astype(held_as)


def setup_inputs(seed: int = 0) -> dict:
    splits = jax.random.split(jax.random.key(seed), 9)
    sound_speed_sq = jnp.clip(jnp.exp(math.log(2.0) - 1.3862944 * jax.random.uniform(splits[0], (NX, NY, NZ), jnp.float32) ** level_of(splits[0], (NX, NY, NZ), ((0, 4), (1, 4)), -0.2, 0.2)), 0.5, 2.0)
    wind_profile = jnp.clip(jax.random.uniform(splits[1], (3, NZ), jnp.float32, -0.6, 0.6), -0.6, 0.6)
    forward_field = noise(splits[2], (STEPS, 4, NX, NY, NZ), 1.0, 6.0, ((2, 4), (3, 4)))
    adjoint_state = noise(splits[3], (GROUPS, 4, NX, NY, NZ), 0.05, 0.3125, ((0, 2), (2, 4), (3, 4)), jnp.float32)
    pair_counts = draw_pair_counts(jax.random.fold_in(splits[8], 71), 0)
    source_cells = draw_source_cells(jax.random.fold_in(splits[8], 71), 0)
    receiver_cells = draw_receiver_cells(jax.random.fold_in(splits[8], 71), 0)
    residuals = noise(splits[7], (PAIRS, STEPS), 3.0, 16.0, ((0, 2),), jnp.float32)
    return {"sound_speed_sq": sound_speed_sq, "wind_profile": wind_profile, "forward_field": forward_field, "adjoint_state": adjoint_state, "pair_counts": pair_counts, "source_cells": source_cells, "receiver_cells": receiver_cells, "residuals": residuals}


step_length = 0.25


def central(field):
    dims = field.ndim
    wide = [(0, 0)] * (dims - 3) + [(1, 1), (1, 1), (0, 0)]
    padded = jnp.pad(field, wide)
    east_diff = (padded[..., 2:, 1:-1, :] - padded[..., :-2, 1:-1, :]) * 0.5
    north_diff = (padded[..., 1:-1, 2:, :] - padded[..., 1:-1, :-2, :]) * 0.5
    center = padded[..., 1:-1, 1:-1, :]
    vertical = jnp.pad(center, [(0, 0)] * (dims - 1) + [(1, 1)])
    up_diff = (vertical[..., 2:] - vertical[..., :-2]) * 0.5
    return east_diff, north_diff, up_diff


def reference(sound_speed_sq, wind_profile, forward_field, adjoint_state, pair_counts, source_cells, receiver_cells, residuals):
    east_wind = wind_profile[0]
    north_wind = wind_profile[1]
    vertical_wind = wind_profile[2]
    kernel_total = jnp.zeros((4, NX, NY, NZ), jnp.float32)
    states = []
    for group in range(GROUPS):
        lower = group * PMAX
        src = source_cells[lower:lower + PMAX]
        rcv = receiver_cells[lower:lower + PMAX]
        misfit = residuals[lower:lower + PMAX]
        live = (jnp.arange(PMAX, dtype=jnp.int32) < pair_counts[group]).astype(jnp.float32)
        src_flat = (src[:, 0] * NY + src[:, 1]) * NZ + src[:, 2]
        rcv_flat = (rcv[:, 0] * NY + rcv[:, 1]) * NZ + rcv[:, 2]
        state = adjoint_state[group]
        for step in range(STEPS):
            snap = STEPS - 1 - step
            forward = forward_field[snap].astype(jnp.float32)
            sample = forward[0].reshape(-1)[src_flat]
            amplitude = misfit[:, snap] * sample * live
            injected = jnp.zeros((NX * NY * NZ,), jnp.float32).at[rcv_flat].add(amplitude).reshape(NX, NY, NZ)
            east_diff, north_diff, up_diff = central(state)
            pressure = state[0]
            velocity = state[1:]
            divergence = east_diff[1] + north_diff[2] + up_diff[3]
            p_new = pressure + step_length * (sound_speed_sq * divergence + east_wind * east_diff[0] + north_wind * north_diff[0] + vertical_wind * up_diff[0]) + injected
            p_east, p_north, p_up = central(p_new)
            gradient = jnp.stack([p_east, p_north, p_up])
            a_new = velocity + step_length * (gradient + east_wind * east_diff[1:] + north_wind * north_diff[1:] + vertical_wind * up_diff[1:])
            f_east, f_north, f_up = central(forward)
            pieces = [p_new * (f_east[1] + f_north[2] + f_up[3])]
            for along in (f_east, f_north, f_up):
                pieces.append(p_new * along[0] + a_new[0] * along[1] + a_new[1] * along[2] + a_new[2] * along[3])
            kernel_total = kernel_total + jnp.stack(pieces)
            state = jnp.concatenate([p_new[None], a_new], axis=0)
        states.append(state)
    return kernel_total, jnp.stack(states)
```

```python
import jax
import jax.numpy as jnp
from jax import lax
from jax.experimental import pallas as pl
from jax.experimental.pallas import tpu as pltpu
from jax.sharding import PartitionSpec as P

step_length = 0.25
SCALE = 0.5 * step_length
HALO = 4
PER_ROUND = 2
LANES = 128
ROWS = 8
VMEM = pltpu.VMEM
CORNER = [(i, j) for i in range(1, HALO) for j in range(1, HALO) if i + j <= HALO]
BF = jnp.bfloat16
F32 = jnp.float32


def swap_pairs(size, odd):
    partner = [((i - odd) ^ 1) + odd for i in range(size)]
    return [(i, j if 0 <= j < size else i) for i, j in enumerate(partner)]


def swapped(x, axis, odd):
    return lax.ppermute(x, axis, swap_pairs(lax.axis_size(axis), odd))


def diagonal(x, odd_x, odd_y):
    size_x, size_y = lax.axis_size("gx"), lax.axis_size("gy")
    pairs = [
        (i * size_y + j, k * size_y + m)
        for i, k in swap_pairs(size_x, odd_x)
        for j, m in swap_pairs(size_y, odd_y)
    ]
    return lax.ppermute(x, ("gx", "gy"), pairs)


def summed(x):
    for axis in ("gx", "gy"):
        size = lax.axis_size(axis)
        terms = [x]
        for k in range(1, size):
            terms.append(lax.ppermute(x, axis, [(i, (i + k) % size) for i in range(size)]))
        x = sum(terms)
    return x


def call(kernel, outs, scratch=(), cost=10_000_000, specs=None, grid=()):
    def run(*args):
        return pl.pallas_call(
            kernel,
            out_shape=outs,
            grid=grid,
            in_specs=specs or [pl.BlockSpec(memory_space=VMEM)] * len(args),
            out_specs=jax.tree.map(lambda _: pl.BlockSpec(memory_space=VMEM), outs),
            scratch_shapes=list(scratch),
            compiler_params=pltpu.CompilerParams(vmem_limit_bytes=48 * 2**20),
            cost_estimate=pl.CostEstimate(flops=cost, bytes_accessed=1_000_000, transcendentals=0),
        )(*args)

    return run


def struct(shape, dtype):
    return jax.ShapeDtypeStruct(shape, dtype)


class Place:
    def __init__(self):
        self.index = {}
        self.size = {}
        for axis in ("gx", "gy"):
            self.index[axis] = lax.axis_index(axis)
            self.size[axis] = lax.axis_size(axis)

    def plus(self, axis, odd):
        return lax.rem(self.index[axis], 2) == odd

    def has(self, axis, odd):
        i = self.index[axis]
        if not odd:
            return None
        return jnp.logical_and(i > 0, i < self.size[axis] - 1)


def column_rows(y, n):
    start = y * ROWS
    if not isinstance(start, int):
        start = pl.multiple_of(start, ROWS)
    return pl.ds(start, n * ROWS)


def pack_edges(place, load, fields, width_x, width_y, z_out, x_out, c_out):
    for odd in (0, 1):
        y0 = jnp.where(place.plus("gy", odd), width_y - HALO, 0)
        x0 = jnp.where(place.plus("gx", odd), width_x - HALO, 0)
        for f in range(fields):
            for x in range(width_x):
                z_out[odd][f, x] = load(f, x, y0, HALO).astype(BF)
            for j in range(HALO):
                x_out[odd][f, j] = load(f, x0 + j, 0, width_y).astype(BF)
    for odd_x in (0, 1):
        plus_x = place.plus("gx", odd_x)
        for odd_y in (0, 1):
            plus_y = place.plus("gy", odd_y)
            out = c_out[2 * odd_x + odd_y]
            for f in range(fields):
                for k in range(0, len(CORNER), 2):
                    two = []
                    for i, j in CORNER[k : k + 2]:
                        x = jnp.where(plus_x, width_x - i, i - 1)
                        y = jnp.where(plus_y, width_y - j, j - 1)
                        two.append(load(f, x, y, 1))
                    out[f, k * ROWS : (k + 2) * ROWS] = jnp.concatenate(two, axis=0).astype(BF)


def place_edges(place, store, fields, width_x, width_y, z_in, x_in, c_in):
    def masked(value, *conditions):
        value = value.astype(F32)
        for condition in conditions:
            if condition is not None:
                value = jnp.where(condition, value, 0.0)
        return value

    for odd in (0, 1):
        y0 = jnp.where(place.plus("gy", odd), width_y + HALO, 0)
        x0 = jnp.where(place.plus("gx", odd), width_x + HALO, 0)
        for f in range(fields):
            for x in range(width_x):
                store(f, HALO + x, y0, HALO, masked(z_in[odd][f, x], place.has("gy", odd)))
            for j in range(HALO):
                store(f, x0 + j, HALO, width_y, masked(x_in[odd][f, j], place.has("gx", odd)))
    for odd_x in (0, 1):
        plus_x = place.plus("gx", odd_x)
        for odd_y in (0, 1):
            plus_y = place.plus("gy", odd_y)
            got = c_in[2 * odd_x + odd_y]
            for f in range(fields):
                for k in range(0, len(CORNER), 2):
                    two = masked(
                        got[f, k * ROWS : (k + 2) * ROWS],
                        place.has("gx", odd_x),
                        place.has("gy", odd_y),
                    )
                    for n, (i, j) in enumerate(CORNER[k : k + 2]):
                        x = jnp.where(plus_x, HALO + width_x - 1 + i, HALO - i)
                        y = jnp.where(plus_y, HALO + width_y - 1 + j, HALO - j)
                        store(f, x, y, 1, two[n * ROWS : (n + 1) * ROWS])


class Altitude:
    def __init__(self):
        lane = lax.broadcasted_iota(jnp.int32, (ROWS, LANES), 1)
        row = lax.broadcasted_iota(jnp.int32, (ROWS, LANES), 0)
        self.last_lane = lane == LANES - 1
        self.first_lane = lane == 0
        self.last_row = row == ROWS - 1
        self.first_row = row == 0

    def __call__(self, v):
        up = pltpu.roll(v, LANES - 1, 1)
        carried = jnp.where(self.last_row, 0.0, pltpu.roll(up, ROWS - 1, 0))
        up = jnp.where(self.last_lane, carried, up)
        down = pltpu.roll(v, 1, 1)
        carried = jnp.where(self.first_row, 0.0, pltpu.roll(down, 1, 0))
        down = jnp.where(self.first_lane, carried, down)
        return up - down


def over_diamond(radius, width_x, width_y, row):
    if radius >= 0:

        def own(i, carry):
            row(HALO + i, HALO - radius, width_y + 2 * radius)
            return carry

        lax.fori_loop(0, width_x, own, 0)
    for d in range(1, radius + 1):
        rest = radius - d
        row(HALO - d, HALO - rest, width_y + 2 * rest)
        row(HALO + width_x - 1 + d, HALO - rest, width_y + 2 * rest)


def advance(place, altitude, old, new, speed, wind, inject, carry_dz, radius, width_x, width_y):
    east, north, vertical = wind

    def at(ref, x, y):
        return ref[x, column_rows(y, 1), :]

    def clear(fields, reach):
        length = width_y + 2 * reach
        sides = (("gx", 0, 0), ("gx", 1, 1), ("gy", 0, 0), ("gy", 1, 1))
        for axis, high, _ in sides:
            edge = place.index[axis] == (place.size[axis] - 1 if high else 0)

            @pl.when(edge)
            def _():
                for f in fields:
                    if axis == "gx":
                        for d in range(1, reach + 1):
                            x = HALO + width_x - 1 + d if high else HALO - d
                            new[f, x, column_rows(HALO - reach, length), :] = jnp.zeros(
                                (length * ROWS, LANES), F32
                            )
                    else:
                        y = HALO + width_y if high else HALO - reach
                        for x in range(HALO - reach, HALO + width_x + reach):
                            new[f, x, column_rows(y, reach), :] = jnp.zeros(
                                (reach * ROWS, LANES), F32
                            )

    p, ax, ay, az = (old.at[f] for f in range(4))

    def p_row(x, y0, n):
        ps = [at(p, x, y0 + k - 1) for k in range(n + 2)]
        ays = [at(ay, x, y0 + k - 1) for k in range(n + 2)]
        for k in range(n):
            y = y0 + k
            up = altitude(at(az, x, y))
            carry_dz[x, column_rows(y, 1), :] = up
            div = (at(ax, x + 1, y) - at(ax, x - 1, y)) + (ays[k + 2] - ays[k]) + up
            value = (
                at(speed, x, y) * div
                + east * (at(p, x + 1, y) - at(p, x - 1, y))
                + north * (ps[k + 2] - ps[k])
                + vertical * altitude(ps[k + 1])
            )
            new[0, x, column_rows(y, 1), :] = ps[k + 1] + value + inject(x, y)

    over_diamond(radius, width_x, width_y, p_row)
    if radius:
        clear((0,), radius)
    pn = new.at[0]

    def a_row(x, y0, n):
        ps = [at(pn, x, y0 + k - 1) for k in range(n + 2)]
        for f, a in ((1, ax), (2, ay), (3, az)):
            vs = [at(a, x, y0 + k - 1) for k in range(n + 2)]
            for k in range(n):
                y = y0 + k
                if f == 1:
                    grad = at(pn, x + 1, y) - at(pn, x - 1, y)
                elif f == 2:
                    grad = ps[k + 2] - ps[k]
                else:
                    grad = altitude(ps[k + 1])
                up = carry_dz[x, column_rows(y, 1), :] if f == 3 else altitude(vs[k + 1])
                value = (
                    SCALE * grad
                    + east * (at(a, x + 1, y) - at(a, x - 1, y))
                    + north * (vs[k + 2] - vs[k])
                    + vertical * up
                )
                new[f, x, column_rows(y, 1), :] = vs[k + 1] + value

    over_diamond(radius - 1, width_x, width_y, a_row)
    if radius > 1:
        clear((1, 2, 3), radius - 1)


def add_increment(altitude, state, forward, total, width_x, width_y):
    wide = width_y + 2

    def column(f, x, y):
        start = (x * wide + y) * ROWS
        return forward[f, pl.ds(pl.multiple_of(start, ROWS), ROWS), :]

    def row(i, carry):
        for k in range(width_y):
            p, ax, ay, az = (state(f, i, k) for f in range(4))
            dx = [column(f, i + 2, k + 1) - column(f, i, k + 1) for f in range(4)]
            dy = [column(f, i + 1, k + 2) - column(f, i + 1, k) for f in range(4)]
            dz = [altitude(column(f, i + 1, k + 1)) for f in range(4)]
            rows = column_rows(k, 1)
            total[0, i, rows, :] += p * (dx[1] + dy[2] + dz[3])
            for n, d in ((1, dx), (2, dy), (3, dz)):
                total[n, i, rows, :] += p * d[0] + ax * d[1] + ay * d[2] + az * d[3]
        return carry

    lax.fori_loop(0, width_x, row, 0)


def halo_structs(fields, width_x, width_y):
    faces_z = [struct((fields, width_x, HALO * ROWS, LANES), BF)] * 2
    faces_x = [struct((fields, HALO, width_y * ROWS, LANES), BF)] * 2
    corners = [struct((fields, len(CORNER) * ROWS, LANES), BF)] * 4
    return faces_z + faces_x + corners


def exchanged(edges):
    z, x, c = edges[:2], edges[2:4], edges[4:]
    z = [swapped(z[odd], "gy", odd) for odd in (0, 1)]
    c = [diagonal(c[2 * i + j], i, j) for i in (0, 1) for j in (0, 1)]
    x = [swapped(x[odd], "gx", odd) for odd in (0, 1)]
    return z + x + c


def shards(
    sound_speed_sq,
    wind_profile,
    forward_field,
    adjoint_state,
    pair_counts,
    source_cells,
    receiver_cells,
    residuals,
):
    steps_total = forward_field.shape[0]
    width_x, width_y, depth = sound_speed_sq.shape
    slots = residuals.shape[0]
    ext_x, ext_y = width_x + 2 * HALO, width_y + 2 * HALO
    blocks = depth // LANES
    assert blocks == ROWS and steps_total == 2 * PER_ROUND
    tile = (width_x, width_y * ROWS, LANES)
    ext = (ext_x, ext_y * ROWS, LANES)

    def pack_kernel(state, speed, cols, speed_cols, *outs):
        place = Place()
        for x in range(width_x):
            for b in range(blocks):
                at = pl.ds(b, width_y, stride=ROWS)
                here = slice(b * LANES, (b + 1) * LANES)
                for f in range(4):
                    cols[f, x, at, :] = state[0, f, x, :, here]
                speed_cols[x, at, :] = speed[x, :, here] * SCALE

        def load(f, x, y, n):
            ref = cols.at[f] if f < 4 else speed_cols
            return ref[x, column_rows(y, n), :]

        pack_edges(place, load, 5, width_x, width_y, outs[:2], outs[2:4], outs[4:])

    packed = call(
        pack_kernel,
        [struct((4,) + tile, F32), struct(tile, F32)] + halo_structs(5, width_x, width_y),
    )(adjoint_state, sound_speed_sq)
    cols, speed_cols, edges = packed[0], packed[1], packed[2:]
    first_halo = exchanged(edges)

    forward_edges = []
    for axis, dim in (("gy", 3), ("gx", 2)):
        for odd in (0, 1):
            plus = lax.rem(lax.axis_index(axis), 2) == odd
            start = jnp.where(plus, forward_field.shape[dim] - 1, 0)
            edge = lax.dynamic_slice_in_dim(forward_field, start, 1, axis=dim)
            forward_edges.append(swapped(jnp.squeeze(edge, dim), axis, odd))

    def sample_kernel(source, pressure, out):
        local_x = source[:, 0:1] - lax.axis_index("gx") * width_x
        local_y = source[:, 1:2] - lax.axis_index("gy") * width_y
        inside = (local_x >= 0) & (local_x < width_x) & (local_y >= 0) & (local_y < width_y)
        where = jnp.where(inside, local_x * width_y + local_y, -1)
        cells = width_x * width_y
        chosen = lax.broadcasted_iota(jnp.int32, (slots, cells), 1) == where
        chosen = jnp.where(chosen, 1.0, 0.0).astype(BF)
        level = lax.broadcasted_iota(jnp.int32, (slots, depth), 1) == source[:, 2:3]
        lane = lax.broadcasted_iota(jnp.int32, (slots, LANES), 1)
        result = jnp.zeros((slots, LANES), F32)
        for t in range(steps_total):
            columns = jnp.dot(
                chosen, pressure[t, 0].reshape(cells, depth), preferred_element_type=F32
            )
            picked = jnp.sum(jnp.where(level, columns, 0.0), axis=1, keepdims=True)
            result = jnp.where(lane == t, picked, result)
        out[...] = result.T[:ROWS]

    samples = call(
        sample_kernel,
        struct((ROWS, slots), F32),
        specs=[
            pl.BlockSpec(memory_space=VMEM),
            pl.BlockSpec((steps_total, 1, width_x, width_y, depth), lambda i: (0, 0, 0, 0, 0)),
        ],
        grid=(1,),
    )(source_cells, forward_field)
    samples = summed(samples)

    def inject_kernel(counts, receiver, receiver_rows, misfit, sample, out):
        local_x = receiver_rows[0:1] - (lax.axis_index("gx") * width_x - HALO)
        local_y = receiver_rows[1:2] - (lax.axis_index("gy") * width_y - HALO)
        inside = (local_x >= 0) & (local_x < ext_x) & (local_y >= 0) & (local_y < ext_y)
        live = lax.broadcasted_iota(jnp.int32, (1, slots), 1) < counts[0]
        where = jnp.where(inside & live, local_x * ext_y + local_y, -1)
        cells = ext_x * ext_y
        chosen = lax.broadcasted_iota(jnp.int32, (cells, slots), 0) == where
        level = lax.broadcasted_iota(jnp.int32, (slots, depth), 1) == receiver[:, 2:3]
        level = jnp.where(level, 1.0, 0.0).astype(BF)
        for t in range(steps_total):
            amplitude = misfit[t : t + 1] * sample[t : t + 1]
            head = amplitude.astype(BF).astype(F32)
            result = jnp.zeros((cells, depth), F32)
            for part in (head, amplitude - head):
                spread = jnp.where(chosen, part, 0.0).astype(BF)
                result += jnp.dot(spread, level, preferred_element_type=F32)
            for g in range(cells // ROWS):
                for b in range(blocks):
                    out[t, pl.ds(g * ROWS * ROWS + b, ROWS, stride=ROWS), :] = result[
                        g * ROWS : (g + 1) * ROWS, b * LANES : (b + 1) * LANES
                    ]

    injected = call(
        inject_kernel,
        struct((steps_total, ext_x * ext_y * ROWS, LANES), F32),
        specs=[pl.BlockSpec(memory_space=pltpu.SMEM)] + [pl.BlockSpec(memory_space=VMEM)] * 4,
    )(pair_counts, receiver_cells, receiver_cells.T, residuals.T, samples)

    wind = wind_profile.reshape(3, ROWS, LANES) * SCALE

    def run_round(place, number, wind, inject, buffers, speed, carry_dz, after):
        altitude = Altitude()
        winds = tuple(wind[i] for i in range(3))
        for s in range(PER_ROUND):
            step = number * PER_ROUND + s
            snap = steps_total - 1 - step
            old, new = buffers[s % 2], buffers[(s + 1) % 2]

            def injected_at(x, y):
                start = (x * ext_y + y) * ROWS
                if not isinstance(start, int):
                    start = pl.multiple_of(start, ROWS)
                return inject[snap, pl.ds(start, ROWS), :]

            radius = 2 * (PER_ROUND - 1 - s) + 1
            advance(
                place, altitude, old, new, speed, winds, injected_at, carry_dz, radius, width_x, width_y
            )
            after(altitude, s, snap, new)

    def own(ref, f, x, y, n):
        return ref[f, HALO + x, column_rows(HALO + y, n), :]

    def fill(place, buffer, speed, cols, speed_cols, halo):
        def store(f, x, y, n, value):
            ref = buffer.at[f] if f < 4 else speed
            ref[x, column_rows(y, n), :] = value

        for f in range(4):
            for x in range(width_x):
                store(f, HALO + x, HALO, width_y, cols[f, x])
        fields = 4
        if speed_cols is not None:
            fields = 5
            for x in range(width_x):
                store(4, HALO + x, HALO, width_y, speed_cols[x])
        place_edges(place, store, fields, width_x, width_y, halo[:2], halo[2:4], halo[4:])

    halos = 8

    def first_kernel(wind, inject, cols, speed_cols, *refs):
        halo, refs = refs[:halos], refs[halos:]
        early, late, speed, edges = refs[0], refs[1], refs[2], refs[3 : 3 + halos]
        here, there, carry_dz = refs[3 + halos :]
        place = Place()
        fill(place, here, speed, cols, speed_cols, halo)

        def after(altitude, s, snap, state):
            out = (early, late)[s]
            for f in range(4):
                for x in range(width_x):
                    out[f, x] = own(state, f, x, 0, width_y)

        run_round(place, 0, wind, inject, (here, there), speed, carry_dz, after)

        def load(f, x, y, n):
            return own(here, f, x, y, n)

        pack_edges(place, load, 4, width_x, width_y, edges[:2], edges[2:4], edges[4:])

    first = call(
        first_kernel,
        [struct((4,) + tile, F32)] * 2 + [struct(ext, F32)] + halo_structs(4, width_x, width_y),
        scratch=[VMEM((4,) + ext, F32)] * 2 + [VMEM(ext, F32)],
    )(wind, injected, cols, speed_cols, *first_halo)
    early, late, speed_ext, edges = first[0], first[1], first[2], first[3:]
    second_halo = exchanged(edges)

    rim = (width_x + 2) * (width_y + 2) * ROWS
    wide = width_y + 2

    def early_kernel(early, late, forward, *refs):
        edges, (total, kept), (columns,) = refs[:4], refs[4:6], refs[6:]
        place = Place()
        altitude = Altitude()

        def spread(snap, target):
            for f in range(4):
                for x in range(width_x):
                    for b in range(blocks):
                        target[f, pl.ds(((x + 1) * wide + 1) * ROWS + b, width_y, stride=ROWS), :] = (
                            forward[snap, f, x, :, b * LANES : (b + 1) * LANES].astype(F32)
                        )
                for odd in (0, 1):
                    y = jnp.where(place.plus("gy", odd), width_y + 1, 0)
                    x = jnp.where(place.plus("gx", odd), width_x + 1, 0)
                    for b in range(blocks):
                        here = slice(b * LANES, (b + 1) * LANES)
                        value = edges[odd][snap, f, :, here].astype(F32)
                        if odd:
                            value = jnp.where(place.has("gy", odd), value, 0.0)
                        target[f, pl.ds((wide + y) * ROWS + b, width_x, stride=wide * ROWS), :] = value
                        value = edges[2 + odd][snap, f, :, here].astype(F32)
                        if odd:
                            value = jnp.where(place.has("gx", odd), value, 0.0)
                        target[f, pl.ds((x * wide + 1) * ROWS + b, width_y, stride=ROWS), :] = value

        total[...] = jnp.zeros_like(total)
        for s, state in ((0, early), (1, late)):
            spread(steps_total - 1 - s, columns)
            add_increment(
                altitude,
                lambda f, x, y: state[f, x, column_rows(y, 1), :],
                columns,
                total,
                width_x,
                width_y,
            )
        for s in range(PER_ROUND):
            spread(steps_total - 1 - PER_ROUND - s, kept.at[s])

    total, kept = call(
        early_kernel,
        [struct((4,) + tile, F32), struct((PER_ROUND, 4, rim, LANES), F32)],
        scratch=[VMEM((4, rim, LANES), F32)],
    )(early, late, forward_field, *forward_edges)

    half = depth // 2

    def second_kernel(wind, inject, cols, speed, total, kept, *refs):
        halo, refs = refs[:halos], refs[halos:]
        final, mine, other = refs[:3]
        here, there, carry_dz, sums = refs[3:]
        place = Place()
        fill(place, here, None, cols, None, halo)
        sums[...] = total[...]

        def after(altitude, s, snap, state):
            add_increment(
                altitude,
                lambda f, x, y: own(state, f, x, y, 1),
                kept.at[s],
                sums,
                width_x,
                width_y,
            )

        run_round(place, 1, wind, inject, (here, there), speed, carry_dz, after)
        me = lax.axis_index("pair")
        for f in range(4):
            for x in range(width_x):
                for b in range(blocks):
                    final[0, f, x, :, b * LANES : (b + 1) * LANES] = here[
                        f, HALO + x, pl.ds(HALO * ROWS + b, width_y, stride=ROWS), :
                    ]
                for b in range(blocks // 2):
                    for ref, part in ((mine, me), (other, 1 - me)):
                        ref[f, x, :, b * LANES : (b + 1) * LANES] = 0.5 * sums[
                            f, x, pl.ds(part * (blocks // 2) + b, width_y, stride=ROWS), :
                        ]

    kernel_half = struct((4, width_x, width_y, half), F32)
    final, mine, other = call(
        second_kernel,
        [struct(adjoint_state.shape, F32), kernel_half, kernel_half],
        scratch=[VMEM((4,) + ext, F32)] * 2 + [VMEM(ext, F32), VMEM((4,) + tile, F32)],
    )(wind, injected, late, speed_ext, total, kept, *second_halo)
    received = lax.ppermute(other, "pair", [(0, 1), (1, 0)])
    return (mine + received, final)


def solution(mesh):
    assert mesh.shape["pair"] == 2 and mesh.shape["gx"] % 2 == 0 and mesh.shape["gy"] % 2 == 0
    in_specs = (
        P("gx", "gy", None),
        P(),
        P(None, None, "gx", "gy", None),
        P("pair", None, "gx", "gy", None),
        P("pair"),
        P("pair", None),
        P("pair", None),
        P("pair", None),
    )
    out_specs = (P(None, "gx", "gy", "pair"), P("pair", None, "gx", "gy", None))
    return jax.shard_map(shards, mesh=mesh, in_specs=in_specs, out_specs=out_specs, check_vma=False)
```

```python
import jax
import jax.numpy as jnp
from jax import lax
from jax.experimental import pallas as pl
from jax.experimental.pallas import tpu as pltpu
from jax.sharding import PartitionSpec as P

step_length = 0.25
SCALE = 0.5 * step_length
HALO = 4
PER_ROUND = 2
LANES = 128
ROWS = 8
VMEM = pltpu.VMEM
CORNER = [(i, j) for i in range(1, HALO) for j in range(1, HALO) if i + j <= HALO]
BF = jnp.bfloat16
F32 = jnp.float32


def swap_pairs(size, odd):
    partner = [((i - odd) ^ 1) + odd for i in range(size)]
    return [(i, j if 0 <= j < size else i) for i, j in enumerate(partner)]


def swapped(x, axis, odd):
    return lax.ppermute(x, axis, swap_pairs(lax.axis_size(axis), odd))


def summed(x):
    for axis in ("gx", "gy"):
        size = lax.axis_size(axis)
        if size & (size - 1):
            terms = [x]
            for k in range(1, size):
                terms.append(lax.ppermute(x, axis, [(i, (i + k) % size) for i in range(size)]))
            x = sum(terms)
            continue
        k = 1
        while k < size:
            x = x + lax.ppermute(x, axis, [(i, i ^ k) for i in range(size)])
            k *= 2
    return x


def call(kernel, outs, scratch=(), micros=1.0, specs=None, grid=(), limit=16):
    def run(*args):
        return pl.pallas_call(
            kernel,
            out_shape=outs,
            grid=grid,
            in_specs=specs or [pl.BlockSpec(memory_space=VMEM)] * len(args),
            out_specs=jax.tree.map(lambda _: pl.BlockSpec(memory_space=VMEM), outs),
            scratch_shapes=list(scratch),
            compiler_params=pltpu.CompilerParams(vmem_limit_bytes=limit * 2**20),
            cost_estimate=pl.CostEstimate(
                flops=int(1.1e9 * micros), bytes_accessed=100_000, transcendentals=0
            ),
        )(*args)

    return run


def struct(shape, dtype):
    return jax.ShapeDtypeStruct(shape, dtype)


class Place:
    def __init__(self):
        self.index = {}
        self.size = {}
        for axis in ("gx", "gy"):
            self.index[axis] = lax.axis_index(axis)
            self.size[axis] = lax.axis_size(axis)

    def plus(self, axis, odd):
        return lax.rem(self.index[axis], 2) == odd

    def has(self, axis, odd):
        i = self.index[axis]
        if not odd:
            return None
        return jnp.logical_and(i > 0, i < self.size[axis] - 1)


def column_rows(y, n):
    start = y * ROWS
    if not isinstance(start, int):
        start = pl.multiple_of(start, ROWS)
    return pl.ds(start, n * ROWS)


def pack_faces(place, load, fields, width_x, width_y, z_out, x_out):
    for odd in (0, 1):
        y0 = jnp.where(place.plus("gy", odd), width_y - HALO, 0)
        x0 = jnp.where(place.plus("gx", odd), width_x - HALO, 0)
        for f in range(fields):
            for x in range(width_x):
                value = load(f, x, y0, HALO).reshape(HALO, ROWS, LANES)
                z_out[odd][f, x] = value.astype(BF)
            for j in range(HALO):
                x_out[odd][f, j] = load(f, x0 + j, 0, width_y).astype(BF)


def pack_corners(place, fields, width_x, z_in, c_out):
    for odd_x in (0, 1):
        plus_x = place.plus("gx", odd_x)
        for odd_y in (0, 1):
            plus_y = place.plus("gy", odd_y)
            for f in range(fields):
                for k, (i, j) in enumerate(CORNER):
                    x = jnp.where(plus_x, width_x - i, i - 1)
                    y = jnp.where(plus_y, j - 1, HALO - j)
                    c_out[odd_x][f, odd_y, k] = z_in[odd_y][f, x, y]


def place_edges(place, store, fields, width_x, width_y, z_in, x_in, c_in):
    def masked(value, *conditions):
        value = value.astype(F32)
        for condition in conditions:
            if condition is not None:
                value = jnp.where(condition, value, 0.0)
        return value

    for odd in (0, 1):
        y0 = jnp.where(place.plus("gy", odd), width_y + HALO, 0)
        x0 = jnp.where(place.plus("gx", odd), width_x + HALO, 0)
        for f in range(fields):
            for x in range(width_x):
                value = masked(z_in[odd][f, x], place.has("gy", odd))
                store(f, HALO + x, y0, HALO, value.reshape(HALO * ROWS, LANES))
            for j in range(HALO):
                store(f, x0 + j, HALO, width_y, masked(x_in[odd][f, j], place.has("gx", odd)))
    for odd_x in (0, 1):
        plus_x = place.plus("gx", odd_x)
        for odd_y in (0, 1):
            plus_y = place.plus("gy", odd_y)
            for f in range(fields):
                for k, (i, j) in enumerate(CORNER):
                    value = masked(
                        c_in[odd_x][f, odd_y, k], place.has("gx", odd_x), place.has("gy", odd_y)
                    )
                    x = jnp.where(plus_x, HALO + width_x - 1 + i, HALO - i)
                    y = jnp.where(plus_y, HALO + width_y - 1 + j, HALO - j)
                    store(f, x, y, 1, value)


class Altitude:
    def __init__(self):
        lane = lax.broadcasted_iota(jnp.int32, (ROWS, LANES), 1)
        row = lax.broadcasted_iota(jnp.int32, (ROWS, LANES), 0)
        self.last_lane = lane == LANES - 1
        self.first_lane = lane == 0
        self.last_row = row == ROWS - 1
        self.first_row = row == 0

    def __call__(self, v):
        up = pltpu.roll(v, LANES - 1, 1)
        carried = jnp.where(self.last_row, 0.0, pltpu.roll(up, ROWS - 1, 0))
        up = jnp.where(self.last_lane, carried, up)
        down = pltpu.roll(v, 1, 1)
        carried = jnp.where(self.first_row, 0.0, pltpu.roll(down, 1, 0))
        down = jnp.where(self.first_lane, carried, down)
        return up - down


def over_diamond(radius, width_x, width_y, row):
    if radius >= 0:

        def own(i, carry):
            row(HALO + i, HALO - radius, width_y + 2 * radius)
            return carry

        lax.fori_loop(0, width_x, own, 0)
    for d in range(1, radius + 1):
        rest = radius - d
        row(HALO - d, HALO - rest, width_y + 2 * rest)
        row(HALO + width_x - 1 + d, HALO - rest, width_y + 2 * rest)


def advance(place, altitude, old, new, speed, wind, inject, carry_dz, radius, width_x, width_y):
    east, north, vertical = wind

    def at(ref, x, y):
        return ref[x, column_rows(y, 1), :]

    def clear(fields, reach):
        length = width_y + 2 * reach
        sides = (("gx", 0, 0), ("gx", 1, 1), ("gy", 0, 0), ("gy", 1, 1))
        for axis, high, _ in sides:
            edge = place.index[axis] == (place.size[axis] - 1 if high else 0)

            @pl.when(edge)
            def _():
                for f in fields:
                    if axis == "gx":
                        for d in range(1, reach + 1):
                            x = HALO + width_x - 1 + d if high else HALO - d
                            new[f, x, column_rows(HALO - reach, length), :] = jnp.zeros(
                                (length * ROWS, LANES), F32
                            )
                    else:
                        y = HALO + width_y if high else HALO - reach
                        for x in range(HALO - reach, HALO + width_x + reach):
                            new[f, x, column_rows(y, reach), :] = jnp.zeros(
                                (reach * ROWS, LANES), F32
                            )

    p, ax, ay, az = (old.at[f] for f in range(4))

    def p_row(x, y0, n):
        ps = [at(p, x, y0 + k - 1) for k in range(n + 2)]
        ays = [at(ay, x, y0 + k - 1) for k in range(n + 2)]
        for k in range(n):
            y = y0 + k
            up = altitude(at(az, x, y))
            carry_dz[x, column_rows(y, 1), :] = up
            div = (at(ax, x + 1, y) - at(ax, x - 1, y)) + (ays[k + 2] - ays[k]) + up
            value = (
                at(speed, x, y) * div
                + east * (at(p, x + 1, y) - at(p, x - 1, y))
                + north * (ps[k + 2] - ps[k])
                + vertical * altitude(ps[k + 1])
            )
            new[0, x, column_rows(y, 1), :] = ps[k + 1] + value + inject(x, y)

    over_diamond(radius, width_x, width_y, p_row)
    if radius:
        clear((0,), radius)
    pn = new.at[0]

    def a_row(x, y0, n):
        ps = [at(pn, x, y0 + k - 1) for k in range(n + 2)]
        for f, a in ((1, ax), (2, ay), (3, az)):
            vs = [at(a, x, y0 + k - 1) for k in range(n + 2)]
            for k in range(n):
                y = y0 + k
                if f == 1:
                    grad = at(pn, x + 1, y) - at(pn, x - 1, y)
                elif f == 2:
                    grad = ps[k + 2] - ps[k]
                else:
                    grad = altitude(ps[k + 1])
                up = carry_dz[x, column_rows(y, 1), :] if f == 3 else altitude(vs[k + 1])
                value = (
                    SCALE * grad
                    + east * (at(a, x + 1, y) - at(a, x - 1, y))
                    + north * (vs[k + 2] - vs[k])
                    + vertical * up
                )
                new[f, x, column_rows(y, 1), :] = vs[k + 1] + value

    over_diamond(radius - 1, width_x, width_y, a_row)
    if radius > 1:
        clear((1, 2, 3), radius - 1)


def add_increment(altitude, state, forward, total, width_x, width_y):
    def row(i):
        for k in range(width_y):
            p, ax, ay, az = (state(f, i, k) for f in range(4))
            dx = [forward(f, i + 1, k) - forward(f, i - 1, k) for f in range(4)]
            dy = [forward(f, i, k + 1) - forward(f, i, k - 1) for f in range(4)]
            dz = [altitude(forward(f, i, k)) for f in range(4)]
            rows = column_rows(k, 1)
            total[0, i, rows, :] += p * (dx[1] + dy[2] + dz[3])
            for n, d in ((1, dx), (2, dy), (3, dz)):
                total[n, i, rows, :] += p * d[0] + ax * d[1] + ay * d[2] + az * d[3]

    def inner(i, carry):
        row(i)
        return carry

    row(0)
    lax.fori_loop(1, width_x - 1, inner, 0)
    row(width_x - 1)


def face_structs(fields, width_x, width_y):
    faces_z = [struct((fields, width_x, HALO, ROWS, LANES), BF)] * 2
    faces_x = [struct((fields, HALO, width_y * ROWS, LANES), BF)] * 2
    return faces_z + faces_x


def shards(
    sound_speed_sq,
    wind_profile,
    forward_field,
    adjoint_state,
    pair_counts,
    source_cells,
    receiver_cells,
    residuals,
):
    steps_total = forward_field.shape[0]
    width_x, width_y, depth = sound_speed_sq.shape
    slots = residuals.shape[0]
    ext_x, ext_y = width_x + 2 * HALO, width_y + 2 * HALO
    blocks = depth // LANES
    assert blocks == ROWS and steps_total == 2 * PER_ROUND and slots % LANES == 0
    tile = (width_x, width_y * ROWS, LANES)
    ext = (ext_x, ext_y * ROWS, LANES)

    def exchanged(faces, fields):
        z = [swapped(faces[odd], "gy", odd) for odd in (0, 1)]
        x = [swapped(faces[2 + odd], "gx", odd) for odd in (0, 1)]

        def corner_kernel(z_even, z_odd, *outs):
            pack_corners(Place(), fields, width_x, (z_even, z_odd), outs)

        shape = (fields, 2, len(CORNER), ROWS, LANES)
        corners = call(corner_kernel, [struct(shape, BF)] * 2, micros=0.7, limit=8)(*z)
        corners = [swapped(corners[odd], "gx", odd) for odd in (0, 1)]
        return z + x + corners

    def pack_kernel(state, speed, cols, speed_cols, *outs):
        place = Place()
        for x in range(width_x):
            for b in range(blocks):
                at = pl.ds(b, width_y, stride=ROWS)
                here = slice(b * LANES, (b + 1) * LANES)
                for f in range(4):
                    cols[f, x, at, :] = state[0, f, x, :, here]
                speed_cols[x, at, :] = speed[x, :, here] * SCALE

        def load(f, x, y, n):
            ref = cols.at[f] if f < 4 else speed_cols
            return ref[x, column_rows(y, n), :]

        pack_faces(place, load, 5, width_x, width_y, outs[:2], outs[2:])

    packed = call(
        pack_kernel,
        [struct((4,) + tile, F32), struct(tile, F32)] + face_structs(5, width_x, width_y),
        micros=1.2,
    )(adjoint_state, sound_speed_sq)
    cols, speed_cols = packed[:2]
    first_halo = exchanged(packed[2:], 5)

    def sample_kernel(source, pressure, out):
        local_x = source[0:1] - lax.axis_index("gx") * width_x
        local_y = source[1:2] - lax.axis_index("gy") * width_y
        inside = (local_x >= 0) & (local_x < width_x) & (local_y >= 0) & (local_y < width_y)
        where = jnp.where(inside, local_x * width_y + local_y, -1)
        cells = width_x * width_y
        chosen = lax.broadcasted_iota(jnp.int32, (cells, slots), 0) == where
        chosen = jnp.where(chosen, 1.0, 0.0).astype(BF)
        level = lax.broadcasted_iota(jnp.int32, (depth, slots), 0) == source[2:3]
        row = lax.broadcasted_iota(jnp.int32, (ROWS, slots), 0)
        result = jnp.zeros((ROWS, slots), F32)
        for t in range(steps_total):
            columns = lax.dot_general(
                pressure[t, 0].reshape(cells, depth),
                chosen,
                (((0,), (0,)), ((), ())),
                preferred_element_type=F32,
            )
            picked = jnp.sum(jnp.where(level, columns, 0.0), axis=0, keepdims=True)
            result = jnp.where(row == t, picked, result)
        out[...] = result

    samples = call(
        sample_kernel,
        struct((ROWS, slots), F32),
        specs=[
            pl.BlockSpec(memory_space=VMEM),
            pl.BlockSpec((steps_total, 1, width_x, width_y, depth), lambda i: (0, 0, 0, 0, 0)),
        ],
        grid=(1,),
        micros=1.2,
        limit=12,
    )(source_cells.T, forward_field)
    samples = summed(samples)

    def inject_kernel(counts, receiver, misfit, sample, out):
        local_x = receiver[0:1] - (lax.axis_index("gx") * width_x - HALO)
        local_y = receiver[1:2] - (lax.axis_index("gy") * width_y - HALO)
        inside = (local_x >= 0) & (local_x < ext_x) & (local_y >= 0) & (local_y < ext_y)
        live = lax.broadcasted_iota(jnp.int32, (1, slots), 1) < counts[0]
        where = jnp.where(inside & live, local_x * ext_y + local_y, -1)
        cells = ext_x * ext_y
        chosen = lax.broadcasted_iota(jnp.int32, (cells, slots), 0) == where
        level = lax.broadcasted_iota(jnp.int32, (depth, slots), 0) == receiver[2:3]
        level = jnp.where(level, 1.0, 0.0).astype(BF)
        for t in range(steps_total):
            amplitude = misfit[t : t + 1] * sample[t : t + 1]
            head = amplitude.astype(BF).astype(F32)
            result = jnp.zeros((cells, depth), F32)
            for part in (head, amplitude - head):
                spread = jnp.where(chosen, part, 0.0).astype(BF)
                result += lax.dot_general(
                    spread, level, (((1,), (1,)), ((), ())), preferred_element_type=F32
                )
            for g in range(cells // ROWS):
                for b in range(blocks):
                    out[t, pl.ds(g * ROWS * ROWS + b, ROWS, stride=ROWS), :] = result[
                        g * ROWS : (g + 1) * ROWS, b * LANES : (b + 1) * LANES
                    ]

    injected = call(
        inject_kernel,
        struct((steps_total, ext_x * ext_y * ROWS, LANES), F32),
        specs=[pl.BlockSpec(memory_space=pltpu.SMEM)] + [pl.BlockSpec(memory_space=VMEM)] * 3,
        micros=1.8,
    )(pair_counts, receiver_cells.T, residuals.T, samples)

    def forward_kernel(forward, early, late, *edges):
        place = Place()

        def one(n, carry):
            t, f = n // 4, lax.rem(n, 4)
            for ref, snap in ((late, t), (early, t + PER_ROUND)):
                number = snap * 4 + f
                for x in range(width_x):
                    for b in range(blocks):
                        ref[n, x, pl.ds(b, width_y, stride=ROWS), :] = forward[
                            snap, f, x, :, b * LANES : (b + 1) * LANES
                        ].astype(F32)
                for odd in (0, 1):
                    y = jnp.where(place.plus("gy", odd), width_y - 1, 0)
                    x = jnp.where(place.plus("gx", odd), width_x - 1, 0)
                    edges[2 + odd][number] = ref[n, x].astype(BF)
                    edges[odd][number] = ref[n, :, column_rows(y, 1), :].reshape(
                        width_x * ROWS, LANES
                    ).astype(BF)
            return carry

        lax.fori_loop(0, 4 * PER_ROUND, one, 0)

    forward_struct = struct((4 * PER_ROUND,) + tile, F32)
    edge_structs = [struct((4 * steps_total, n * ROWS, LANES), BF) for n in (width_x, width_y)]
    made = call(
        forward_kernel,
        [forward_struct] * 2 + [edge_structs[0]] * 2 + [edge_structs[1]] * 2,
        micros=2.0,
    )(forward_field)
    forward_early, forward_late = made[:2]
    rim = [swapped(made[2 + odd], "gy", odd) for odd in (0, 1)]
    rim += [swapped(made[4 + odd], "gx", odd) for odd in (0, 1)]

    rim_scratch = [
        VMEM((2, 4 * PER_ROUND, width_x * ROWS, LANES), F32),
        VMEM((2, 4 * PER_ROUND, width_y * ROWS, LANES), F32),
    ]

    def forward_of(place, columns, first, rim, rim_y, rim_x):
        for odd in (0, 1):
            for axis, source, target in (("gy", rim[odd], rim_y), ("gx", rim[2 + odd], rim_x)):
                side = jnp.where(place.plus(axis, odd), 1, 0)
                for n in range(4 * PER_ROUND):
                    value = source[4 * first + n].astype(F32)
                    if odd:
                        value = jnp.where(place.has(axis, odd), value, 0.0)
                    target[side, n] = value

        def reader(snap):
            base = 4 * (snap - first)

            def column(f, x, y):
                if isinstance(x, int) and x in (-1, width_x):
                    return rim_x[int(x > 0), base + f, column_rows(y, 1), :]
                if y in (-1, width_y):
                    rows = x * ROWS if isinstance(x, int) else pl.multiple_of(x * ROWS, ROWS)
                    return rim_y[int(y > 0), base + f, pl.ds(rows, ROWS), :]
                return columns[base + f, x, column_rows(y, 1), :]

            return column

        return reader

    def run_round(place, number, wind, inject, buffers, speed, carry_dz, after):
        altitude = Altitude()
        winds = []
        for i in range(3):
            rows = [wind[i : i + 1, b * LANES : (b + 1) * LANES] for b in range(blocks)]
            winds.append(jnp.concatenate(rows, axis=0) * SCALE)
        for s in range(PER_ROUND):
            step = number * PER_ROUND + s
            snap = steps_total - 1 - step
            old, new = buffers[s % 2], buffers[(s + 1) % 2]

            def injected_at(x, y):
                start = (x * ext_y + y) * ROWS
                if not isinstance(start, int):
                    start = pl.multiple_of(start, ROWS)
                return inject[snap, pl.ds(start, ROWS), :]

            radius = 2 * (PER_ROUND - 1 - s) + 1
            advance(
                place, altitude, old, new, speed, winds, injected_at, carry_dz, radius, width_x, width_y
            )
            after(altitude, s, snap, new)

    def own(ref, f, x, y, n):
        return ref[f, HALO + x, column_rows(HALO + y, n), :]

    def fill(place, buffer, speed, cols, speed_cols, halo):
        def store(f, x, y, n, value):
            ref = buffer.at[f] if f < 4 else speed
            ref[x, column_rows(y, n), :] = value

        for f in range(4):
            for x in range(width_x):
                store(f, HALO + x, HALO, width_y, cols[f, x])
        fields = 4
        if speed_cols is not None:
            fields = 5
            for x in range(width_x):
                store(4, HALO + x, HALO, width_y, speed_cols[x])
        place_edges(place, store, fields, width_x, width_y, halo[:2], halo[2:4], halo[4:])

    halos, faces = 6, 4

    def first_kernel(wind, inject, cols, speed_cols, *refs):
        halo, refs = refs[:halos], refs[halos:]
        early, late, speed, edges = refs[0], refs[1], refs[2], refs[3 : 3 + faces]
        here, there, carry_dz = refs[3 + faces :]
        place = Place()
        fill(place, here, speed, cols, speed_cols, halo)

        def after(altitude, s, snap, state):
            out = (early, late)[s]
            for f in range(4):
                for x in range(width_x):
                    out[f, x] = own(state, f, x, 0, width_y)

        run_round(place, 0, wind, inject, (here, there), speed, carry_dz, after)

        def load(f, x, y, n):
            return own(here, f, x, y, n)

        pack_faces(place, load, 4, width_x, width_y, edges[:2], edges[2:])

    first = call(
        first_kernel,
        [struct((4,) + tile, F32)] * 2 + [struct(ext, F32)] + face_structs(4, width_x, width_y),
        scratch=[VMEM((4,) + ext, F32)] * 2 + [VMEM(ext, F32)],
        micros=8.0,
        limit=28,
    )(wind_profile, injected, cols, speed_cols, *first_halo)
    early, late, speed_ext = first[:3]
    second_halo = exchanged(first[3:], 4)

    def early_kernel(early, late, columns, *refs):
        rim, total, rim_y, rim_x = refs[:4], refs[4], refs[5], refs[6]
        altitude = Altitude()
        reader = forward_of(Place(), columns, PER_ROUND, rim, rim_y, rim_x)
        total[...] = jnp.zeros_like(total)
        for s, state in ((0, early), (1, late)):
            add_increment(
                altitude,
                lambda f, x, y: state[f, x, column_rows(y, 1), :],
                reader(steps_total - 1 - s),
                total,
                width_x,
                width_y,
            )

    total = call(
        early_kernel, struct((4,) + tile, F32), scratch=rim_scratch, micros=5.0, limit=16
    )(early, late, forward_early, *rim)

    half = depth // 2

    def second_kernel(wind, inject, cols, speed, total, columns, *refs):
        halo, rim, refs = refs[:halos], refs[halos : halos + 4], refs[halos + 4 :]
        final, mine, other = refs[:3]
        here, there, carry_dz, sums, rim_y, rim_x = refs[3:]
        place = Place()
        fill(place, here, None, cols, None, halo)
        reader = forward_of(place, columns, 0, rim, rim_y, rim_x)
        sums[...] = total[...]

        def after(altitude, s, snap, state):
            add_increment(
                altitude,
                lambda f, x, y: own(state, f, x, y, 1),
                reader(snap),
                sums,
                width_x,
                width_y,
            )

        run_round(place, 1, wind, inject, (here, there), speed, carry_dz, after)
        me = lax.axis_index("pair")
        for f in range(4):
            for x in range(width_x):
                for b in range(blocks):
                    final[0, f, x, :, b * LANES : (b + 1) * LANES] = here[
                        f, HALO + x, pl.ds(HALO * ROWS + b, width_y, stride=ROWS), :
                    ]
                for b in range(blocks // 2):
                    for ref, part in ((mine, me), (other, 1 - me)):
                        ref[f, x, :, b * LANES : (b + 1) * LANES] = 0.5 * sums[
                            f, x, pl.ds(part * (blocks // 2) + b, width_y, stride=ROWS), :
                        ]

    kernel_half = struct((4, width_x, width_y, half), F32)
    final, mine, other = call(
        second_kernel,
        [struct(adjoint_state.shape, F32), kernel_half, kernel_half],
        scratch=[VMEM((4,) + ext, F32)] * 2 + [VMEM(ext, F32), VMEM((4,) + tile, F32)] + rim_scratch,
        micros=11.0,
        limit=30,
    )(wind_profile, injected, late, speed_ext, total, forward_late, *second_halo, *rim)
    received = lax.ppermute(other, "pair", [(0, 1), (1, 0)])
    return (mine + received, final)


def solution(mesh):
    assert mesh.shape["pair"] == 2 and mesh.shape["gx"] % 2 == 0 and mesh.shape["gy"] % 2 == 0
    in_specs = (
        P("gx", "gy", None),
        P(),
        P(None, None, "gx", "gy", None),
        P("pair", None, "gx", "gy", None),
        P("pair"),
        P("pair", None),
        P("pair", None),
        P("pair", None),
    )
    out_specs = (P(None, "gx", "gy", "pair"), P("pair", None, "gx", "gy", None))
    return jax.shard_map(shards, mesh=mesh, in_specs=in_specs, out_specs=out_specs, check_vma=False)
```

```python
import jax
import jax.numpy as jnp
from jax import lax
from jax.experimental import pallas as pl
from jax.experimental.pallas import tpu as pltpu
from jax.sharding import PartitionSpec as P

step_length = 0.25
SCALE = 0.5 * step_length
HALO = 4
PER_ROUND = 2
LANES = 128
ROWS = 8
VMEM = pltpu.VMEM
CORNER = [(i, j) for i in range(1, HALO) for j in range(1, HALO) if i + j <= HALO]
BF = jnp.bfloat16
F32 = jnp.float32


def swap_pairs(size, odd):
    partner = [((i - odd) ^ 1) + odd for i in range(size)]
    return [(i, j if 0 <= j < size else i) for i, j in enumerate(partner)]


def swapped(x, axis, odd):
    return lax.ppermute(x, axis, swap_pairs(lax.axis_size(axis), odd))


def summed(x):
    for axis in ("gx", "gy"):
        size = lax.axis_size(axis)
        if size & (size - 1):
            terms = [x]
            for k in range(1, size):
                terms.append(lax.ppermute(x, axis, [(i, (i + k) % size) for i in range(size)]))
            x = sum(terms)
            continue
        k = 1
        while k < size:
            x = x + lax.ppermute(x, axis, [(i, i ^ k) for i in range(size)])
            k *= 2
    return x


def call(kernel, outs, scratch=(), micros=1.0, specs=None, grid=(), limit=16):
    def run(*args):
        return pl.pallas_call(
            kernel,
            out_shape=outs,
            grid=grid,
            in_specs=specs or [pl.BlockSpec(memory_space=VMEM)] * len(args),
            out_specs=jax.tree.map(lambda _: pl.BlockSpec(memory_space=VMEM), outs),
            scratch_shapes=list(scratch),
            compiler_params=pltpu.CompilerParams(vmem_limit_bytes=limit * 2**20),
            cost_estimate=pl.CostEstimate(
                flops=int(1.1e9 * micros), bytes_accessed=100_000, transcendentals=0
            ),
        )(*args)

    return run


def struct(shape, dtype):
    return jax.ShapeDtypeStruct(shape, dtype)


class Place:
    def __init__(self):
        self.index = {}
        self.size = {}
        for axis in ("gx", "gy"):
            self.index[axis] = lax.axis_index(axis)
            self.size[axis] = lax.axis_size(axis)

    def plus(self, axis, odd):
        return lax.rem(self.index[axis], 2) == odd

    def has(self, axis, odd):
        i = self.index[axis]
        if not odd:
            return None
        return jnp.logical_and(i > 0, i < self.size[axis] - 1)


def column_rows(y, n):
    start = y * ROWS
    if not isinstance(start, int):
        start = pl.multiple_of(start, ROWS)
    return pl.ds(start, n * ROWS)


def pack_faces(place, load, fields, width_x, width_y, z_out, x_out):
    for odd in (0, 1):
        y0 = jnp.where(place.plus("gy", odd), width_y - HALO, 0)
        x0 = jnp.where(place.plus("gx", odd), width_x - HALO, 0)
        for f in range(fields):
            for x in range(width_x):
                value = load(f, x, y0, HALO).reshape(HALO, ROWS, LANES)
                z_out[odd][f, x] = value.astype(BF)
            for j in range(HALO):
                x_out[odd][HALO * f + j] = load(f, x0 + j, 0, width_y).astype(BF)


def corner_blocks(fields, width_y):
    return -(-2 * fields * len(CORNER) // width_y)


def corner_place(fields, odd_y, f, k, width_y):
    n = (odd_y * fields + f) * len(CORNER) + k
    return n // width_y, pl.ds(n % width_y * ROWS, 2 * ROWS)


def pack_corners(place, fields, width_x, width_y, z_in, outs, firsts):
    for odd_x in (0, 1):
        plus_x = place.plus("gx", odd_x)
        for odd_y in (0, 1):
            plus_y = place.plus("gy", odd_y)
            for f in range(fields):
                for k in range(0, len(CORNER), 2):
                    two = []
                    for i, j in CORNER[k : k + 2]:
                        x = jnp.where(plus_x, width_x - i, i - 1)
                        y = jnp.where(plus_y, j - 1, HALO - j)
                        two.append(z_in[odd_y][f, x, y].astype(F32))
                    block, rows = corner_place(fields, odd_y, f, k, width_y)
                    outs[odd_x][firsts[odd_x] + block, rows, :] = jnp.concatenate(
                        two, axis=0
                    ).astype(BF)


def place_edges(place, store, fields, width_x, width_y, z_in, x_in, c_in, firsts):
    def masked(value, *conditions):
        value = value.astype(F32)
        for condition in conditions:
            if condition is not None:
                value = jnp.where(condition, value, 0.0)
        return value

    for odd in (0, 1):
        y0 = jnp.where(place.plus("gy", odd), width_y + HALO, 0)
        x0 = jnp.where(place.plus("gx", odd), width_x + HALO, 0)
        for f in range(fields):
            for x in range(width_x):
                value = masked(z_in[odd][f, x], place.has("gy", odd))
                store(f, HALO + x, y0, HALO, value.reshape(HALO * ROWS, LANES))
            for j in range(HALO):
                value = masked(x_in[odd][HALO * f + j], place.has("gx", odd))
                store(f, x0 + j, HALO, width_y, value)
    for odd_x in (0, 1):
        plus_x = place.plus("gx", odd_x)
        for odd_y in (0, 1):
            plus_y = place.plus("gy", odd_y)
            for f in range(fields):
                for k in range(0, len(CORNER), 2):
                    block, rows = corner_place(fields, odd_y, f, k, width_y)
                    two = masked(
                        c_in[odd_x][firsts[odd_x] + block, rows, :],
                        place.has("gx", odd_x),
                        place.has("gy", odd_y),
                    )
                    for n, (i, j) in enumerate(CORNER[k : k + 2]):
                        x = jnp.where(plus_x, HALO + width_x - 1 + i, HALO - i)
                        y = jnp.where(plus_y, HALO + width_y - 1 + j, HALO - j)
                        store(f, x, y, 1, two[n * ROWS : (n + 1) * ROWS])


class Altitude:
    def __init__(self):
        lane = lax.broadcasted_iota(jnp.int32, (ROWS, LANES), 1)
        row = lax.broadcasted_iota(jnp.int32, (ROWS, LANES), 0)
        self.last_lane = lane == LANES - 1
        self.first_lane = lane == 0
        self.last_row = row == ROWS - 1
        self.first_row = row == 0

    def __call__(self, v):
        up = pltpu.roll(v, LANES - 1, 1)
        carried = jnp.where(self.last_row, 0.0, pltpu.roll(up, ROWS - 1, 0))
        up = jnp.where(self.last_lane, carried, up)
        down = pltpu.roll(v, 1, 1)
        carried = jnp.where(self.first_row, 0.0, pltpu.roll(down, 1, 0))
        down = jnp.where(self.first_lane, carried, down)
        return up - down


def over_diamond(radius, width_x, width_y, row):
    if radius >= 0:

        def own(i, carry):
            row(HALO + i, HALO - radius, width_y + 2 * radius)
            return carry

        lax.fori_loop(0, width_x, own, 0)
    for d in range(1, radius + 1):
        rest = radius - d
        row(HALO - d, HALO - rest, width_y + 2 * rest)
        row(HALO + width_x - 1 + d, HALO - rest, width_y + 2 * rest)


def advance(place, altitude, old, new, speed, wind, inject, carry_dz, radius, width_x, width_y):
    east, north, vertical = wind

    def at(ref, x, y):
        return ref[x, column_rows(y, 1), :]

    def clear(fields, reach):
        length = width_y + 2 * reach
        sides = (("gx", 0, 0), ("gx", 1, 1), ("gy", 0, 0), ("gy", 1, 1))
        for axis, high, _ in sides:
            edge = place.index[axis] == (place.size[axis] - 1 if high else 0)

            @pl.when(edge)
            def _():
                for f in fields:
                    if axis == "gx":
                        for d in range(1, reach + 1):
                            x = HALO + width_x - 1 + d if high else HALO - d
                            new[f, x, column_rows(HALO - reach, length), :] = jnp.zeros(
                                (length * ROWS, LANES), F32
                            )
                    else:
                        y = HALO + width_y if high else HALO - reach
                        for x in range(HALO - reach, HALO + width_x + reach):
                            new[f, x, column_rows(y, reach), :] = jnp.zeros(
                                (reach * ROWS, LANES), F32
                            )

    p, ax, ay, az = (old.at[f] for f in range(4))

    def p_row(x, y0, n):
        ps = [at(p, x, y0 + k - 1) for k in range(n + 2)]
        ays = [at(ay, x, y0 + k - 1) for k in range(n + 2)]
        for k in range(n):
            y = y0 + k
            up = altitude(at(az, x, y))
            carry_dz[x, column_rows(y, 1), :] = up
            div = (at(ax, x + 1, y) - at(ax, x - 1, y)) + (ays[k + 2] - ays[k]) + up
            value = (
                at(speed, x, y) * div
                + east * (at(p, x + 1, y) - at(p, x - 1, y))
                + north * (ps[k + 2] - ps[k])
                + vertical * altitude(ps[k + 1])
            )
            new[0, x, column_rows(y, 1), :] = ps[k + 1] + value + inject(x, y)

    over_diamond(radius, width_x, width_y, p_row)
    if radius:
        clear((0,), radius)
    pn = new.at[0]

    def a_row(x, y0, n):
        ps = [at(pn, x, y0 + k - 1) for k in range(n + 2)]
        for f, a in ((1, ax), (2, ay), (3, az)):
            vs = [at(a, x, y0 + k - 1) for k in range(n + 2)]
            for k in range(n):
                y = y0 + k
                if f == 1:
                    grad = at(pn, x + 1, y) - at(pn, x - 1, y)
                elif f == 2:
                    grad = ps[k + 2] - ps[k]
                else:
                    grad = altitude(ps[k + 1])
                up = carry_dz[x, column_rows(y, 1), :] if f == 3 else altitude(vs[k + 1])
                value = (
                    SCALE * grad
                    + east * (at(a, x + 1, y) - at(a, x - 1, y))
                    + north * (vs[k + 2] - vs[k])
                    + vertical * up
                )
                new[f, x, column_rows(y, 1), :] = vs[k + 1] + value

    over_diamond(radius - 1, width_x, width_y, a_row)
    if radius > 1:
        clear((1, 2, 3), radius - 1)


def add_increment(altitude, state, forward, total, width_x, width_y):
    def row(i):
        for k in range(width_y):
            p, ax, ay, az = (state(f, i, k) for f in range(4))
            dx = [forward(f, i + 1, k) - forward(f, i - 1, k) for f in range(4)]
            dy = [forward(f, i, k + 1) - forward(f, i, k - 1) for f in range(4)]
            dz = [altitude(forward(f, i, k)) for f in range(4)]
            rows = column_rows(k, 1)
            total[0, i, rows, :] += p * (dx[1] + dy[2] + dz[3])
            for n, d in ((1, dx), (2, dy), (3, dz)):
                total[n, i, rows, :] += p * d[0] + ax * d[1] + ay * d[2] + az * d[3]

    def inner(i, carry):
        row(i)
        return carry

    row(0)
    lax.fori_loop(1, width_x - 1, inner, 0)
    row(width_x - 1)


def shards(
    sound_speed_sq,
    wind_profile,
    forward_field,
    adjoint_state,
    pair_counts,
    source_cells,
    receiver_cells,
    residuals,
):
    steps_total = forward_field.shape[0]
    width_x, width_y, depth = sound_speed_sq.shape
    slots = residuals.shape[0]
    ext_x, ext_y = width_x + 2 * HALO, width_y + 2 * HALO
    blocks = depth // LANES
    assert blocks == ROWS and steps_total == 2 * PER_ROUND and slots % LANES == 0
    assert width_x == width_y and width_x % 2 == 0
    tile = (width_x, width_y * ROWS, LANES)
    ext = (ext_x, ext_y * ROWS, LANES)
    block = (width_y * ROWS, LANES)
    forward_fields = 4 * steps_total

    def face_structs(fields, more=0):
        z = struct((fields, width_x, HALO, ROWS, LANES), BF)
        return [z, z, struct((HALO * fields,) + block, BF), struct((HALO * fields + more,) + block, BF)]

    def second_hop(fields, z, faces, *more):
        extra = sum(m.shape[0] for m in more)
        corners = corner_blocks(fields, width_y)

        def corner_kernel(z_even, z_odd, faces, *refs):
            even, odd = refs[-2:]
            even[: HALO * fields] = faces[...]
            at = HALO * fields
            for ref in refs[:-2]:
                even[at : at + ref.shape[0]] = ref[...]
                at += ref.shape[0]
            pack_corners(Place(), fields, width_x, width_y, (z_even, z_odd), (even, odd), (at, 0))

        even, odd = call(
            corner_kernel,
            [
                struct((HALO * fields + extra + corners,) + block, BF),
                struct((corners,) + block, BF),
            ],
            micros=0.3,
            limit=8,
        )(*z, faces, *more)
        return swapped(even, "gx", 0), swapped(odd, "gx", 1)

    def pack_kernel(state, speed, source, pressure, cols, speed_cols, sample, *outs):
        place = Place()
        for x in range(width_x):
            for b in range(blocks):
                at = pl.ds(b, width_y, stride=ROWS)
                here = slice(b * LANES, (b + 1) * LANES)
                for f in range(4):
                    cols[f, x, at, :] = state[0, f, x, :, here]
                speed_cols[x, at, :] = speed[x, :, here] * SCALE

        def load(f, x, y, n):
            ref = cols.at[f] if f < 4 else speed_cols
            return ref[x, column_rows(y, n), :]

        pack_faces(place, load, 5, width_x, width_y, outs[:2], outs[2:])

        local_x = source[0:1] - place.index["gx"] * width_x
        local_y = source[1:2] - place.index["gy"] * width_y
        inside = (local_x >= 0) & (local_x < width_x) & (local_y >= 0) & (local_y < width_y)
        where = jnp.where(inside, local_x * width_y + local_y, -1)
        cells = width_x * width_y
        chosen = lax.broadcasted_iota(jnp.int32, (cells, slots), 0) == where
        chosen = jnp.where(chosen, 1.0, 0.0).astype(BF)
        level = lax.broadcasted_iota(jnp.int32, (depth, slots), 0) == source[2:3]
        row = lax.broadcasted_iota(jnp.int32, (ROWS, slots), 0)
        result = jnp.zeros((ROWS, slots), F32)
        for t in range(steps_total):
            columns = lax.dot_general(
                pressure[t, 0].reshape(cells, depth),
                chosen,
                (((0,), (0,)), ((), ())),
                preferred_element_type=F32,
            )
            picked = jnp.sum(jnp.where(level, columns, 0.0), axis=0, keepdims=True)
            result = jnp.where(row == t, picked, result)
        sample[...] = result

    whole = pl.BlockSpec(memory_space=VMEM)
    packed = call(
        pack_kernel,
        [struct((4,) + tile, F32), struct(tile, F32), struct((ROWS, slots), F32)] + face_structs(5),
        specs=[whole] * 3
        + [pl.BlockSpec((steps_total, 1, width_x, width_y, depth), lambda i: (0, 0, 0, 0, 0))],
        grid=(1,),
        micros=1.5,
    )(adjoint_state, sound_speed_sq, source_cells.T, forward_field)
    cols, speed_cols, samples = packed[:3]
    z_even, z_odd, x_even, x_odd = packed[3:]
    z_first = [swapped(z_even, "gy", 0), swapped(z_odd, "gy", 1)]
    x_first = swapped(x_odd, "gx", 1)
    samples = summed(samples)

    def forward_kernel(forward, early, late, *edges):
        place = Place()

        def one(n, carry):
            t, f = n // 4, lax.rem(n, 4)
            for ref, snap in ((late, t), (early, t + PER_ROUND)):
                number = snap * 4 + f
                for x in range(width_x):
                    for b in range(blocks):
                        ref[n, x, pl.ds(b, width_y, stride=ROWS), :] = forward[
                            snap, f, x, :, b * LANES : (b + 1) * LANES
                        ].astype(F32)
                for odd in (0, 1):
                    y = jnp.where(place.plus("gy", odd), width_y - 1, 0)
                    x = jnp.where(place.plus("gx", odd), width_x - 1, 0)
                    edges[2 + odd][number] = ref[n, x].astype(BF)
                    edges[odd][number] = ref[n, :, column_rows(y, 1), :].reshape(block).astype(BF)
            return carry

        lax.fori_loop(0, 4 * PER_ROUND, one, 0)

    made = call(
        forward_kernel,
        [struct((4 * PER_ROUND,) + tile, F32)] * 2 + [struct((forward_fields,) + block, BF)] * 4,
        micros=0.9,
    )(forward_field)
    forward_early, forward_late, edge_z_even, edge_z_odd, edge_x_even, edge_x_odd = made
    rim_z = [swapped(edge_z_even, "gy", 0), swapped(edge_z_odd, "gy", 1)]
    hop_even, hop_odd = second_hop(5, z_first, x_even, edge_x_even)
    rim_at = HALO * 5
    corners_at = (rim_at + forward_fields, 0)

    def inject_kernel(counts, receiver, misfit, sample, out):
        local_x = receiver[0:1] - (lax.axis_index("gx") * width_x - HALO)
        local_y = receiver[1:2] - (lax.axis_index("gy") * width_y - HALO)
        inside = (local_x >= 0) & (local_x < ext_x) & (local_y >= 0) & (local_y < ext_y)
        live = lax.broadcasted_iota(jnp.int32, (1, slots), 1) < counts[0]
        where = jnp.where(inside & live, local_x * ext_y + local_y, -1)
        cells = ext_x * ext_y
        chosen = lax.broadcasted_iota(jnp.int32, (cells, slots), 0) == where
        level = lax.broadcasted_iota(jnp.int32, (depth, slots), 0) == receiver[2:3]
        level = jnp.where(level, 1.0, 0.0).astype(BF)
        for t in range(steps_total):
            amplitude = misfit[t : t + 1] * sample[t : t + 1]
            head = amplitude.astype(BF).astype(F32)
            result = jnp.zeros((cells, depth), F32)
            for part in (head, amplitude - head):
                spread = jnp.where(chosen, part, 0.0).astype(BF)
                result += lax.dot_general(
                    spread, level, (((1,), (1,)), ((), ())), preferred_element_type=F32
                )
            for g in range(cells // ROWS):
                for b in range(blocks):
                    out[t, pl.ds(g * ROWS * ROWS + b, ROWS, stride=ROWS), :] = result[
                        g * ROWS : (g + 1) * ROWS, b * LANES : (b + 1) * LANES
                    ]

    injected = call(
        inject_kernel,
        struct((steps_total, ext_x * ext_y * ROWS, LANES), F32),
        specs=[pl.BlockSpec(memory_space=pltpu.SMEM)] + [pl.BlockSpec(memory_space=VMEM)] * 3,
        micros=1.8,
    )(pair_counts, receiver_cells.T, residuals.T, samples)

    rim_scratch = [
        VMEM((2, 4 * PER_ROUND) + block, F32),
        VMEM((2, 4 * PER_ROUND) + block, F32),
    ]

    def forward_of(place, columns, first, rims, rim_y, rim_x):
        for axis, odd, source, at in rims:
            target = rim_y if axis == "gy" else rim_x
            side = jnp.where(place.plus(axis, odd), 1, 0)
            for n in range(4 * PER_ROUND):
                value = source[at + 4 * first + n].astype(F32)
                if odd:
                    value = jnp.where(place.has(axis, odd), value, 0.0)
                target[side, n] = value

        def reader(snap):
            base = 4 * (snap - first)

            def column(f, x, y):
                if isinstance(x, int) and x in (-1, width_x):
                    return rim_x[int(x > 0), base + f, column_rows(y, 1), :]
                if y in (-1, width_y):
                    rows = x * ROWS if isinstance(x, int) else pl.multiple_of(x * ROWS, ROWS)
                    return rim_y[int(y > 0), base + f, pl.ds(rows, ROWS), :]
                return columns[base + f, x, column_rows(y, 1), :]

            return column

        return reader

    def run_round(place, number, wind, inject, buffers, speed, carry_dz, after):
        altitude = Altitude()
        winds = []
        for i in range(3):
            rows = [wind[i : i + 1, b * LANES : (b + 1) * LANES] for b in range(blocks)]
            winds.append(jnp.concatenate(rows, axis=0) * SCALE)
        for s in range(PER_ROUND):
            step = number * PER_ROUND + s
            snap = steps_total - 1 - step
            old, new = buffers[s % 2], buffers[(s + 1) % 2]

            def injected_at(x, y):
                start = (x * ext_y + y) * ROWS
                if not isinstance(start, int):
                    start = pl.multiple_of(start, ROWS)
                return inject[snap, pl.ds(start, ROWS), :]

            radius = 2 * (PER_ROUND - 1 - s) + 1
            advance(
                place, altitude, old, new, speed, winds, injected_at, carry_dz, radius, width_x, width_y
            )
            after(altitude, s, snap, new)

    def own(ref, f, x, y, n):
        return ref[f, HALO + x, column_rows(HALO + y, n), :]

    def fill(place, buffer, speed, cols, speed_cols, z_in, x_in, c_in, firsts):
        def store(f, x, y, n, value):
            ref = buffer.at[f] if f < 4 else speed
            ref[x, column_rows(y, n), :] = value

        for f in range(4):
            for x in range(width_x):
                store(f, HALO + x, HALO, width_y, cols[f, x])
        fields = 4
        if speed_cols is not None:
            fields = 5
            for x in range(width_x):
                store(4, HALO + x, HALO, width_y, speed_cols[x])
        place_edges(place, store, fields, width_x, width_y, z_in, x_in, c_in, firsts)

    def first_kernel(wind, inject, cols, speed_cols, edge_x, z0, z1, x1, c0, c1, *refs):
        early, late, speed, *faces, here, there, carry_dz = refs
        place = Place()
        fill(place, here, speed, cols, speed_cols, (z0, z1), (c0, x1), (c0, c1), corners_at)

        def after(altitude, s, snap, state):
            out = (early, late)[s]
            for f in range(4):
                for x in range(width_x):
                    out[f, x] = own(state, f, x, 0, width_y)

        run_round(place, 0, wind, inject, (here, there), speed, carry_dz, after)

        def load(f, x, y, n):
            return own(here, f, x, y, n)

        pack_faces(place, load, 4, width_x, width_y, faces[:2], faces[2:])
        faces[3][HALO * 4 :] = edge_x[...]

    injected, *rim_z = lax.optimization_barrier((injected, *rim_z))
    first = call(
        first_kernel,
        [struct((4,) + tile, F32)] * 2 + [struct(ext, F32)] + face_structs(4, forward_fields),
        scratch=[VMEM((4,) + ext, F32)] * 2 + [VMEM(ext, F32)],
        micros=6.0,
        limit=28,
    )(
        wind_profile, injected, cols, speed_cols, edge_x_odd, *z_first, x_first, hop_even, hop_odd
    )
    early, late, speed_ext, z_even, z_odd, x_even, x_odd = first
    z_second = [swapped(z_even, "gy", 0), swapped(z_odd, "gy", 1)]
    x_second = swapped(x_odd, "gx", 1)
    again_even, again_odd = second_hop(4, z_second, x_even)

    def rims(z_even, z_odd, x_even, x_odd):
        return (
            ("gy", 0, z_even, 0),
            ("gy", 1, z_odd, 0),
            ("gx", 0, x_even, rim_at),
            ("gx", 1, x_odd, HALO * 4),
        )

    def early_kernel(early, late, columns, z0, z1, c0, x1, total, rim_y, rim_x):
        altitude = Altitude()
        reader = forward_of(Place(), columns, PER_ROUND, rims(z0, z1, c0, x1), rim_y, rim_x)
        total[...] = jnp.zeros_like(total)
        for s, state in ((0, early), (1, late)):
            add_increment(
                altitude,
                lambda f, x, y: state[f, x, column_rows(y, 1), :],
                reader(steps_total - 1 - s),
                total,
                width_x,
                width_y,
            )

    total = call(early_kernel, struct((4,) + tile, F32), scratch=rim_scratch, micros=2.3, limit=16)(
        early, late, forward_early, *rim_z, hop_even, x_second
    )

    half = depth // 2
    half_blocks = blocks // 2

    def second_kernel(
        wind, inject, cols, speed, total, columns, rz0, rz1, rx0, z0, z1, x1, c0, c1, *refs
    ):
        final, mine, other, scales, here, there, carry_dz, sums, rim_y, rim_x = refs
        place = Place()
        fill(place, here, None, cols, None, (z0, z1), (c0, x1), (c0, c1), (HALO * 4, 0))
        reader = forward_of(place, columns, 0, rims(rz0, rz1, rx0, x1), rim_y, rim_x)
        sums[...] = total[...]

        def after(altitude, s, snap, state):
            add_increment(
                altitude,
                lambda f, x, y: own(state, f, x, y, 1),
                reader(snap),
                sums,
                width_x,
                width_y,
            )

        run_round(place, 1, wind, inject, (here, there), speed, carry_dz, after)
        me = lax.axis_index("pair")

        def sums_at(f, x, part, b):
            return sums[f, x, pl.ds(part * half_blocks + b, width_y, stride=ROWS), :]

        for f in range(4):
            for b in range(half_blocks):
                here_lanes = slice(b * LANES, (b + 1) * LANES)
                largest = jnp.abs(sums_at(f, 0, 1 - me, b))
                for x in range(1, width_x):
                    largest = jnp.maximum(largest, jnp.abs(sums_at(f, x, 1 - me, b)))
                largest = jnp.maximum(jnp.max(largest, axis=0, keepdims=True), 1e-30)
                scales[f : f + 1, here_lanes] = largest * (0.5 / 32767.0)
                inverse = 32767.0 / largest
                for x in range(0, width_x, 2):
                    two = [sums_at(f, x + i, 1 - me, b) * inverse for i in (0, 1)]
                    two = jnp.round(jnp.concatenate(two, axis=0))
                    other[f, x // 2, :, here_lanes] = two.astype(jnp.int32).astype(jnp.int16)
        for f in range(4):
            for x in range(width_x):
                for b in range(blocks):
                    final[0, f, x, :, b * LANES : (b + 1) * LANES] = here[
                        f, HALO + x, pl.ds(HALO * ROWS + b, width_y, stride=ROWS), :
                    ]
                for b in range(half_blocks):
                    mine[f, x, :, b * LANES : (b + 1) * LANES] = 0.5 * sums_at(f, x, me, b)

    kernel_half = struct((4, width_x, width_y, half), F32)
    final, mine, other, scales = call(
        second_kernel,
        [
            struct(adjoint_state.shape, F32),
            kernel_half,
            struct((4, width_x // 2, 2 * width_y, half), jnp.int16),
            struct((4, half), F32),
        ],
        scratch=[VMEM((4,) + ext, F32)] * 2 + [VMEM(ext, F32), VMEM((4,) + tile, F32)] + rim_scratch,
        micros=9.0,
        limit=30,
    )(
        wind_profile,
        injected,
        late,
        speed_ext,
        total,
        forward_late,
        *rim_z,
        hop_even,
        *z_second,
        x_second,
        again_even,
        again_odd,
    )
    across = [(0, 1), (1, 0)]
    other, scales = lax.ppermute(other, "pair", across), lax.ppermute(scales, "pair", across)

    def sum_kernel(mine, other, scales, out):
        for f in range(4):
            for x in range(0, width_x, 2):
                two = other[f, x // 2].astype(jnp.int32).astype(F32) * scales[f : f + 1]
                for i in (0, 1):
                    out[f, x + i] = mine[f, x + i] + two[i * width_y : (i + 1) * width_y]

    kernels = call(sum_kernel, kernel_half, micros=0.8, limit=8)(mine, other, scales)
    return (kernels, final)


def solution(mesh):
    assert mesh.shape["pair"] == 2 and mesh.shape["gx"] % 2 == 0 and mesh.shape["gy"] % 2 == 0
    in_specs = (
        P("gx", "gy", None),
        P(),
        P(None, None, "gx", "gy", None),
        P("pair", None, "gx", "gy", None),
        P("pair"),
        P("pair", None),
        P("pair", None),
        P("pair", None),
    )
    out_specs = (P(None, "gx", "gy", "pair"), P("pair", None, "gx", "gy", None))
    return jax.shard_map(shards, mesh=mesh, in_specs=in_specs, out_specs=out_specs, check_vma=False)
```

```python
import jax
import jax.numpy as jnp
from jax import lax
from jax.experimental import pallas as pl
from jax.experimental.pallas import tpu as pltpu
from jax.sharding import PartitionSpec as P

step_length = 0.25
SCALE = 0.5 * step_length
HALO = 4
PER_ROUND = 2
LANES = 128
ROWS = 8
VMEM = pltpu.VMEM
CORNER = [(i, j) for i in range(1, HALO) for j in range(1, HALO) if i + j <= HALO]
BF = jnp.bfloat16
F32 = jnp.float32


def swap_pairs(size, odd):
    partner = [((i - odd) ^ 1) + odd for i in range(size)]
    return [(i, j if 0 <= j < size else i) for i, j in enumerate(partner)]


def swapped(x, axis, odd):
    return lax.ppermute(x, axis, swap_pairs(lax.axis_size(axis), odd))


def diagonal(x, odd_x, odd_y):
    size_x, size_y = lax.axis_size("gx"), lax.axis_size("gy")
    pairs = [
        (i * size_y + j, k * size_y + m)
        for i, k in swap_pairs(size_x, odd_x)
        for j, m in swap_pairs(size_y, odd_y)
    ]
    return lax.ppermute(x, ("gx", "gy"), pairs)


def total_of(x, axis):
    size = lax.axis_size(axis)
    parts = [lax.ppermute(x, axis, [(i, (i + k) % size) for i in range(size)]) for k in range(1, size)]
    return sum(parts, x)


def summed(x, axis, k):
    size = lax.axis_size(axis)
    assert size & (size - 1) == 0
    while k < size:
        x = x + lax.ppermute(x, axis, [(i, i ^ k) for i in range(size)])
        k *= 2
    return x


def call(kernel, outs, scratch=(), micros=1.0, specs=None, out_specs=None, limit=16):
    def run(*args):
        return pl.pallas_call(
            kernel,
            out_shape=outs,
            in_specs=specs or [pl.BlockSpec(memory_space=VMEM)] * len(args),
            out_specs=out_specs
            or jax.tree.map(lambda _: pl.BlockSpec(memory_space=VMEM), outs),
            scratch_shapes=list(scratch),
            compiler_params=pltpu.CompilerParams(vmem_limit_bytes=limit * 2**20),
            cost_estimate=pl.CostEstimate(
                flops=int(1.1e9 * micros), bytes_accessed=100_000, transcendentals=0
            ),
        )(*args)

    return run


def struct(shape, dtype):
    return jax.ShapeDtypeStruct(shape, dtype)


class Place:
    def __init__(self):
        self.index = {}
        self.size = {}
        for axis in ("gx", "gy"):
            self.index[axis] = lax.axis_index(axis)
            self.size[axis] = lax.axis_size(axis)

    def plus(self, axis, odd):
        return lax.rem(self.index[axis], 2) == odd

    def has(self, axis, odd):
        i = self.index[axis]
        if not odd:
            return None
        return jnp.logical_and(i > 0, i < self.size[axis] - 1)


def column_rows(y, n):
    start = y * ROWS
    if not isinstance(start, int):
        start = pl.multiple_of(start, ROWS)
    return pl.ds(start, n * ROWS)


def pack_faces(place, load, fields, width_x, width_y, z_out, x_out, d_out):
    for odd in (0, 1):
        plus_y = place.plus("gy", odd)
        y0 = jnp.where(plus_y, width_y - HALO, 0)
        x0 = jnp.where(place.plus("gx", odd), width_x - HALO, 0)
        plus_x = place.plus("gx", 1)
        for f in range(fields):
            for x in range(width_x):
                value = load(f, x, y0, HALO).reshape(HALO, ROWS, LANES)
                z_out[odd][pl.ds((f * width_x + x) * HALO, HALO)] = value.astype(BF)
            for j in range(HALO):
                x_out[odd][HALO * f + j] = load(f, x0 + j, 0, width_y).astype(BF)
            for k, (i, j) in enumerate(CORNER):
                x = jnp.where(plus_x, width_x - i, i - 1)
                y = jnp.where(plus_y, width_y - j, j - 1)
                d_out[odd][f * len(CORNER) + k] = load(f, x, y, 1).astype(BF)


def corner_blocks(fields, width_y):
    return -(-2 * fields * len(CORNER) // width_y)


def corner_place(fields, odd_y, f, k, width_y):
    n = (odd_y * fields + f) * len(CORNER) + k
    return n // width_y, pl.ds(n % width_y * ROWS, 2 * ROWS)


def pack_corners(place, fields, width_x, width_y, z_in, out, first):
    plus_x = place.plus("gx", 0)
    for odd_y in (0, 1):
        plus_y = place.plus("gy", odd_y)
        for f in range(fields):
            for k in range(0, len(CORNER), 2):
                two = []
                for i, j in CORNER[k : k + 2]:
                    x = jnp.where(plus_x, width_x - i, i - 1)
                    y = jnp.where(plus_y, j - 1, HALO - j)
                    two.append(z_in[odd_y][(f * width_x + x) * HALO + y].astype(F32))
                block, rows = corner_place(fields, odd_y, f, k, width_y)
                out[first + block, rows, :] = jnp.concatenate(two, axis=0).astype(BF)


def place_edges(place, store, fields, width_x, width_y, z_in, x_in, c_in, first, d_in):
    def masked(value, *conditions):
        value = value.astype(F32)
        for condition in conditions:
            if condition is not None:
                value = jnp.where(condition, value, 0.0)
        return value

    for odd in (0, 1):
        y0 = jnp.where(place.plus("gy", odd), width_y + HALO, 0)
        x0 = jnp.where(place.plus("gx", odd), width_x + HALO, 0)
        for f in range(fields):
            for x in range(width_x):
                value = z_in[odd][pl.ds((f * width_x + x) * HALO, HALO)]
                value = masked(value, place.has("gy", odd))
                store(f, HALO + x, y0, HALO, value.reshape(HALO * ROWS, LANES))
            for j in range(HALO):
                value = masked(x_in[odd][HALO * f + j], place.has("gx", odd))
                store(f, x0 + j, HALO, width_y, value)
    for odd_x in (0, 1):
        plus_x = place.plus("gx", odd_x)
        for odd_y in (0, 1):
            plus_y = place.plus("gy", odd_y)
            for f in range(fields):
                for k in range(0, len(CORNER), 2):
                    if odd_x:
                        n = f * len(CORNER) + k
                        two = [d_in[odd_y][n], d_in[odd_y][n + 1]]
                    else:
                        block, rows = corner_place(fields, odd_y, f, k, width_y)
                        two = c_in[first + block, rows, :].astype(F32)
                        two = [two[:ROWS], two[ROWS:]]
                    for value, (i, j) in zip(two, CORNER[k : k + 2]):
                        x = jnp.where(plus_x, HALO + width_x - 1 + i, HALO - i)
                        y = jnp.where(plus_y, HALO + width_y - 1 + j, HALO - j)
                        value = masked(value, place.has("gx", odd_x), place.has("gy", odd_y))
                        store(f, x, y, 1, value)


class Altitude:
    def __init__(self):
        lane = lax.broadcasted_iota(jnp.int32, (ROWS, LANES), 1)
        row = lax.broadcasted_iota(jnp.int32, (ROWS, LANES), 0)
        self.last_lane = lane == LANES - 1
        self.first_lane = lane == 0
        self.last_row = row == ROWS - 1
        self.first_row = row == 0

    def __call__(self, v):
        up = pltpu.roll(v, LANES - 1, 1)
        carried = jnp.where(self.last_row, 0.0, pltpu.roll(up, ROWS - 1, 0))
        up = jnp.where(self.last_lane, carried, up)
        down = pltpu.roll(v, 1, 1)
        carried = jnp.where(self.first_row, 0.0, pltpu.roll(down, 1, 0))
        down = jnp.where(self.first_lane, carried, down)
        return up - down


def over_diamond(radius, width_x, width_y, row, sides):
    def own(i, carry):
        row(HALO + i, HALO - radius, width_y + 2 * radius, None)
        return carry

    lax.fori_loop(0, width_x, own, 0)
    for d in range(1, radius + 1):
        rest = radius - d
        row(HALO - d, HALO - rest, width_y + 2 * rest, sides[0])
        row(HALO + width_x - 1 + d, HALO - rest, width_y + 2 * rest, sides[1])


def advance(place, altitude, old, new, state_dz, wind, inject, radius, first, width_x, width_y):
    east, north, vertical = wind
    speed, dz_az, dz_p = state_dz
    sides = {
        axis: [
            jnp.where(place.index[axis] == edge, 0.0, 1.0) for edge in (0, place.size[axis] - 1)
        ]
        for axis in ("gx", "gy")
    }

    def at(ref, x, y):
        return ref[x, column_rows(y, 1), :]

    def inside(value, kept, y):
        if y < HALO or y >= HALO + width_y:
            side = sides["gy"][int(y > HALO)]
            kept = side if kept is None else kept * side
        return value if kept is None else value * kept

    p, ax, ay, az = (old.at[f] for f in range(4))

    def p_row(x, y0, n, kept):
        ps = [at(p, x, y0 + k - 1) for k in range(n + 2)]
        ays = [at(ay, x, y0 + k - 1) for k in range(n + 2)]
        for k in range(n):
            y = y0 + k
            up = altitude(at(az, x, y))
            dz_az[x, column_rows(y, 1), :] = up
            up_p = altitude(ps[k + 1]) if first else at(dz_p, x, y)
            div = (at(ax, x + 1, y) - at(ax, x - 1, y)) + (ays[k + 2] - ays[k]) + up
            value = (
                at(speed, x, y) * div
                + east * (at(p, x + 1, y) - at(p, x - 1, y))
                + north * (ps[k + 2] - ps[k])
                + vertical * up_p
            )
            value = ps[k + 1] + value + inject(x, y)
            new[0, x, column_rows(y, 1), :] = inside(value, kept, y)

    over_diamond(radius, width_x, width_y, p_row, sides["gx"])
    pn = new.at[0]

    def a_row(x, y0, n, kept):
        ps = [at(pn, x, y0 + k - 1) for k in range(n + 2)]
        for f, a in ((1, ax), (2, ay), (3, az)):
            vs = [at(a, x, y0 + k - 1) for k in range(n + 2)]
            for k in range(n):
                y = y0 + k
                if f == 1:
                    grad = at(pn, x + 1, y) - at(pn, x - 1, y)
                elif f == 2:
                    grad = ps[k + 2] - ps[k]
                else:
                    grad = altitude(ps[k + 1])
                    if radius > 1:
                        dz_p[x, column_rows(y, 1), :] = grad
                up = at(dz_az, x, y) if f == 3 else altitude(vs[k + 1])
                value = (
                    SCALE * grad
                    + east * (at(a, x + 1, y) - at(a, x - 1, y))
                    + north * (vs[k + 2] - vs[k])
                    + vertical * up
                )
                new[f, x, column_rows(y, 1), :] = inside(vs[k + 1] + value, kept, y)

    over_diamond(radius - 1, width_x, width_y, a_row, sides["gx"])


def add_increment(state, forward, forward_dz, total, width_x, width_y):
    def row(i):
        for k in range(width_y):
            p, ax, ay, az = (state(f, i, k) for f in range(4))
            dx = [forward(f, i + 1, k) - forward(f, i - 1, k) for f in range(4)]
            dy = [forward(f, i, k + 1) - forward(f, i, k - 1) for f in range(4)]
            dz = [forward_dz(f, i, k) for f in range(4)]
            rows = column_rows(k, 1)
            total[0, i, rows, :] += p * (dx[1] + dy[2] + dz[3])
            for n, d in ((1, dx), (2, dy), (3, dz)):
                total[n, i, rows, :] += p * d[0] + ax * d[1] + ay * d[2] + az * d[3]

    def inner(i, carry):
        row(i)
        return carry

    row(0)
    lax.fori_loop(1, width_x - 1, inner, 0)
    row(width_x - 1)


def shards(
    sound_speed_sq,
    wind_profile,
    forward_field,
    adjoint_state,
    pair_counts,
    source_cells,
    receiver_cells,
    residuals,
):
    steps_total = forward_field.shape[0]
    width_x, width_y, depth = sound_speed_sq.shape
    slots = residuals.shape[0]
    ext_x, ext_y = width_x + 2 * HALO, width_y + 2 * HALO
    blocks = depth // LANES
    assert blocks == ROWS and steps_total == 2 * PER_ROUND and slots % (2 * LANES) == 0 and slots <= 8 * LANES
    assert width_x == width_y and width_x % 2 == 0
    tile = (width_x, width_y * ROWS, LANES)
    ext = (ext_x, ext_y * ROWS, LANES)
    block = (width_y * ROWS, LANES)
    forward_fields = 4 * steps_total

    def face_structs(fields, more=0):
        z = struct((HALO * width_x * fields + more // 2 * width_x, ROWS, LANES), BF)
        x = [struct((HALO * fields + more,) + block, BF)] * 2
        d = struct((len(CORNER) * fields, ROWS, LANES), BF)
        return [z, z, *x, d, d]

    def first_hop(faces):
        z_even, z_odd, _, x_odd, d_even, d_odd = faces
        z = [swapped(z_even, "gy", 0), swapped(z_odd, "gy", 1)]
        return z, swapped(x_odd, "gx", 1), [diagonal(d_even, 1, 0), diagonal(d_odd, 1, 1)]

    def second_hop(fields, z, faces, *sample):
        at = faces.shape[0]
        ahead = at + len(sample)

        def corner_kernel(z_even, z_odd, faces, *refs):
            even = refs[len(sample)]
            even[:at] = faces[...]
            if sample:
                for n, lanes in enumerate(range(0, slots, 2 * LANES)):
                    two = [refs[0][:, lanes + i : lanes + i + LANES] for i in (0, LANES)]
                    rows = pl.ds(2 * ROWS * n, 2 * ROWS)
                    even[at, rows, :] = jnp.concatenate(two, axis=0).astype(BF)
                for odd, ref in ((0, z_even), (1, z_odd)):
                    for n in range(4 * PER_ROUND):
                        value = ref[pl.ds(rim_z_at + n * width_x, width_x)].reshape(block)
                        refs[2][4 * PER_ROUND * odd + n] = value
            pack_corners(Place(), fields, width_x, width_y, (z_even, z_odd), even, ahead)

        outs = [struct((ahead + corner_blocks(fields, width_y),) + block, BF)]
        if sample:
            outs.append(struct((8 * PER_ROUND,) + block, BF))
        made = call(corner_kernel, outs, micros=0.3, limit=8)(*z, faces, *sample)
        return [swapped(made[0], "gx", 0), *made[1:]]

    whole = pl.BlockSpec(memory_space=VMEM)
    remain = pl.BlockSpec(memory_space=pltpu.HBM)

    def sample_kernel(source, forward, sample, pressure, done):
        copy = pltpu.make_async_copy(forward.at[:, 0], pressure, done)
        copy.start()
        local_x = source[0:1] - lax.axis_index("gx") * width_x
        local_y = source[1:2] - lax.axis_index("gy") * width_y
        inside = (local_x >= 0) & (local_x < width_x) & (local_y >= 0) & (local_y < width_y)
        where = jnp.where(inside, local_x * width_y + local_y, -1)
        cells = width_x * width_y
        chosen = lax.broadcasted_iota(jnp.int32, (cells, slots), 0) == where
        chosen = jnp.where(chosen, 1.0, 0.0).astype(BF)
        level = lax.broadcasted_iota(jnp.int32, (depth, slots), 0) == source[2:3]
        row = lax.broadcasted_iota(jnp.int32, (ROWS, slots), 0)
        result = jnp.zeros((ROWS, slots), F32)
        copy.wait()
        for t in range(steps_total):
            columns = lax.dot_general(
                pressure[t].reshape(cells, depth),
                chosen,
                (((0,), (0,)), ((), ())),
                preferred_element_type=F32,
            )
            picked = jnp.sum(jnp.where(level, columns, 0.0), axis=0, keepdims=True)
            result = jnp.where(row == t, picked, result)
        sample[...] = result

    samples = call(
        sample_kernel,
        struct((ROWS, slots), F32),
        scratch=[VMEM((steps_total, width_x, width_y, depth), BF), pltpu.SemaphoreType.DMA],
        specs=[whole, remain],
        micros=1.5,
        limit=8,
    )(source_cells.T, forward_field)
    samples = total_of(samples, "gy")
    state, samples = lax.optimization_barrier((adjoint_state, samples))
    samples = summed(samples, "gx", 2)

    def pack_kernel(state, speed, forward, cols, speed_cols, early, late, *outs):
        place = Place()
        for x in range(width_x):
            for b in range(blocks):
                at = pl.ds(b, width_y, stride=ROWS)
                here = slice(b * LANES, (b + 1) * LANES)
                for f in range(4):
                    cols[f, x, at, :] = state[0, f, x, :, here]
                speed_cols[x, at, :] = speed[x, :, here] * SCALE

        def load(f, x, y, n):
            ref = cols.at[f] if f < 4 else speed_cols
            return ref[x, column_rows(y, n), :]

        pack_faces(place, load, 5, width_x, width_y, outs[:2], outs[2:4], outs[4:])

        mine_is_late = lax.axis_index("pair") == 0

        def one(n, carry):
            t, f = n // 4, lax.rem(n, 4)
            for is_late, ref, snap in ((True, late, t), (False, early, t + PER_ROUND)):
                number = snap * 4 + f
                for x in range(width_x):
                    for b in range(blocks):
                        ref[n, x, pl.ds(b, width_y, stride=ROWS), :] = forward[
                            snap, f, x, :, b * LANES : (b + 1) * LANES
                        ].astype(F32)
                for odd in (0, 1):
                    y = jnp.where(place.plus("gy", odd), width_y - 1, 0)
                    x = jnp.where(place.plus("gx", odd), width_x - 1, 0)
                    outs[2 + odd][rim_at + number] = ref[n, x].astype(BF)
                    value = ref[n, :, column_rows(y, 1), :].astype(BF)
                    to = rim_z_at + n * width_x

                    @pl.when(mine_is_late if is_late else jnp.logical_not(mine_is_late))
                    def _():
                        outs[odd][pl.ds(to, width_x)] = value

            return carry

        lax.fori_loop(0, 4 * PER_ROUND, one, 0)

    rim_z_at, rim_at = HALO * width_x * 5, HALO * 5
    packed = call(
        pack_kernel,
        [struct((4,) + tile, F32), struct(tile, F32)]
        + [struct((4 * PER_ROUND,) + tile, F32)] * 2
        + face_structs(5, forward_fields),
        micros=1.3,
        limit=12,
    )(state, sound_speed_sq, forward_field)
    cols, speed_cols, forward_early, forward_late = packed[:4]
    faces = packed[4:]
    z_first, x_first, d_first = first_hop(faces)
    z_first, x_first, d_first, samples = lax.optimization_barrier(
        (z_first, x_first, d_first, samples)
    )
    hop, rim_z = second_hop(5, z_first, faces[2], samples)
    rim_z = lax.ppermute(rim_z, "pair", [(0, 1), (1, 0)])

    def slope_kernel(early, late, *outs):
        altitude = Altitude()

        def one(n, carry):
            for ref, out in zip((early, late), outs):
                for x in range(width_x):
                    for y in range(width_y):
                        rows = column_rows(y, 1)
                        out[n, x, rows, :] = altitude(ref[n, x, rows, :])
            return carry

        lax.fori_loop(0, 4 * PER_ROUND, one, 0)

    slopes_early, slopes_late = call(
        slope_kernel, [struct((4 * PER_ROUND,) + tile, F32)] * 2, micros=3.3, limit=8
    )(forward_early, forward_late)

    def inject_kernel(counts, receiver, misfit, sample, message, out):
        parts = []
        for n in range(slots // (2 * LANES)):
            two = message[rim_at + forward_fields, pl.ds(2 * ROWS * n, 2 * ROWS), :].astype(F32)
            parts += [two[:ROWS], two[ROWS:]]
        samples = sample[...] + jnp.concatenate(parts, axis=1)
        local_x = receiver[0:1] - (lax.axis_index("gx") * width_x - HALO)
        local_y = receiver[1:2] - (lax.axis_index("gy") * width_y - HALO)
        inside = (local_x >= 0) & (local_x < ext_x) & (local_y >= 0) & (local_y < ext_y)
        live = lax.broadcasted_iota(jnp.int32, (1, slots), 1) < counts[0]
        where = jnp.where(inside & live, local_x * ext_y + local_y, -1)
        cells = ext_x * ext_y
        chosen = lax.broadcasted_iota(jnp.int32, (cells, slots), 0) == where
        level = lax.broadcasted_iota(jnp.int32, (depth, slots), 0) == receiver[2:3]
        level = jnp.where(level, 1.0, 0.0).astype(BF)
        for t in range(steps_total):
            amplitude = misfit[t : t + 1] * samples[t : t + 1]
            head = amplitude.astype(BF).astype(F32)
            result = jnp.zeros((cells, depth), F32)
            for part in (head, amplitude - head):
                spread = jnp.where(chosen, part, 0.0).astype(BF)
                result += lax.dot_general(
                    spread, level, (((1,), (1,)), ((), ())), preferred_element_type=F32
                )
            for g in range(cells // ROWS):
                for b in range(blocks):
                    out[t, pl.ds(g * ROWS * ROWS + b, ROWS, stride=ROWS), :] = result[
                        g * ROWS : (g + 1) * ROWS, b * LANES : (b + 1) * LANES
                    ]

    injected = call(
        inject_kernel,
        struct((steps_total, ext_x * ext_y * ROWS, LANES), F32),
        specs=[pl.BlockSpec(memory_space=pltpu.SMEM)] + [whole] * 4,
        micros=1.6,
    )(pair_counts, receiver_cells.T, residuals.T, samples, hop)

    rim_scratch = [
        VMEM((2, 4 * PER_ROUND) + block, F32),
        VMEM((2, 4 * PER_ROUND) + block, F32),
    ]

    def forward_of(place, columns, first, z_even, z_odd, z_other, x_even, x_odd, rim_y, rim_x):
        from_pair = (lax.axis_index("pair") == 0) == (first == 0)
        for odd, z, x in ((0, z_even, x_even), (1, z_odd, x_odd)):
            side_x = jnp.where(place.plus("gx", odd), 1, 0)
            side_y = jnp.where(place.plus("gy", odd), 1, 0)
            for n in range(4 * PER_ROUND):
                value = x[rim_at + 4 * first + n].astype(F32)
                if odd:
                    value = jnp.where(place.has("gx", odd), value, 0.0)
                rim_x[side_x, n] = value
                own_z = z[pl.ds(rim_z_at + n * width_x, width_x)].astype(F32).reshape(block)
                other = z_other[4 * PER_ROUND * odd + n].astype(F32)
                value = jnp.where(from_pair, own_z, other)
                if odd:
                    value = jnp.where(place.has("gy", odd), value, 0.0)
                rim_y[side_y, n] = value

        def reader(snap):
            base = 4 * (snap - first)

            def column(f, x, y):
                if isinstance(x, int) and x in (-1, width_x):
                    return rim_x[int(x > 0), base + f, column_rows(y, 1), :]
                if y in (-1, width_y):
                    rows = x * ROWS if isinstance(x, int) else pl.multiple_of(x * ROWS, ROWS)
                    return rim_y[int(y > 0), base + f, pl.ds(rows, ROWS), :]
                return columns[base + f, x, column_rows(y, 1), :]

            return column

        return reader

    def run_round(place, number, wind, inject, buffers, state_dz, after):
        altitude = Altitude()
        winds = []
        for i in range(3):
            rows = [wind[i : i + 1, b * LANES : (b + 1) * LANES] for b in range(blocks)]
            winds.append(jnp.concatenate(rows, axis=0) * SCALE)
        for s in range(PER_ROUND):
            step = number * PER_ROUND + s
            snap = steps_total - 1 - step
            old, new = buffers[s % 2], buffers[(s + 1) % 2]

            def injected_at(x, y):
                start = (x * ext_y + y) * ROWS
                if not isinstance(start, int):
                    start = pl.multiple_of(start, ROWS)
                return inject[snap, pl.ds(start, ROWS), :]

            radius = 2 * (PER_ROUND - 1 - s) + 1
            advance(
                place, altitude, old, new, state_dz, winds, injected_at, radius, s == 0, width_x, width_y
            )
            after(altitude, s, snap, new)

    def own(ref, f, x, y, n):
        return ref[f, HALO + x, column_rows(HALO + y, n), :]

    def fill(place, buffer, speed, cols, speed_cols, z_in, x_in, c_in, first, d_in):
        def store(f, x, y, n, value):
            ref = buffer.at[f] if f < 4 else speed
            ref[x, column_rows(y, n), :] = value

        for f in range(4):
            for x in range(width_x):
                store(f, HALO + x, HALO, width_y, cols[f, x])
        fields = 4
        if speed_cols is not None:
            fields = 5
            for x in range(width_x):
                store(4, HALO + x, HALO, width_y, speed_cols[x])
        place_edges(place, store, fields, width_x, width_y, z_in, x_in, c_in, first, d_in)

    def first_kernel(wind, inject, cols, speed_cols, z0, z1, x1, d0, d1, c0, *refs):
        early, late, speed, *faces, here, there, dz_az, dz_p = refs
        place = Place()
        fill(
            place, here, speed, cols, speed_cols, (z0, z1), (c0, x1), c0, rim_at + forward_fields + 1, (d0, d1)
        )

        def after(altitude, s, snap, state):
            out = (early, late)[s]
            for f in range(4):
                for x in range(width_x):
                    out[f, x] = own(state, f, x, 0, width_y)

        run_round(place, 0, wind, inject, (here, there), (speed, dz_az, dz_p), after)

        def load(f, x, y, n):
            return own(here, f, x, y, n)

        pack_faces(place, load, 4, width_x, width_y, faces[:2], faces[2:4], faces[4:])

    first = call(
        first_kernel,
        [struct((4,) + tile, F32)] * 2 + [struct(ext, F32)] + face_structs(4),
        scratch=[VMEM((4,) + ext, F32)] * 2 + [VMEM(ext, F32)] * 2,
        micros=6.0,
        limit=28,
    )(
        wind_profile, injected, cols, speed_cols, *z_first, x_first, *d_first, hop
    )
    early, late, speed_ext = first[:3]
    z_second, x_second, d_second = first_hop(first[3:])

    rim = (*z_first, rim_z, hop, x_first)

    def early_kernel(early, late, columns, slopes, z0, z1, zp, c0, x1, total, rim_y, rim_x):
        place = Place()
        reader = forward_of(place, columns, PER_ROUND, z0, z1, zp, c0, x1, rim_y, rim_x)
        total[...] = jnp.zeros_like(total)
        for s, state in ((0, early), (1, late)):
            add_increment(
                lambda f, x, y: state[f, x, column_rows(y, 1), :],
                reader(steps_total - 1 - s),
                lambda f, x, y: slopes[
                    4 * (steps_total - 1 - s - PER_ROUND) + f, x, column_rows(y, 1), :
                ],
                total,
                width_x,
                width_y,
            )

    total = call(early_kernel, struct((4,) + tile, F32), scratch=rim_scratch, micros=2.3, limit=16)(
        early, late, forward_early, slopes_early, *rim
    )
    z_second, x_second, d_second, total = lax.optimization_barrier(
        (z_second, x_second, d_second, total)
    )
    (again,) = second_hop(4, z_second, first[5])

    half = depth // 2
    half_blocks = blocks // 2

    def second_kernel(
        wind, inject, cols, speed, total, columns, slopes, *refs
    ):
        rims, (z0, z1, x1, d0, d1, c0), refs = refs[:5], refs[5:11], refs[11:]
        last, mine, other, scales, here, there, dz_az, dz_p, sums, rim_y, rim_x = refs
        place = Place()
        fill(place, here, None, cols, None, (z0, z1), (c0, x1), c0, HALO * 4, (d0, d1))
        reader = forward_of(place, columns, 0, *rims, rim_y, rim_x)
        sums[...] = total[...]

        def after(altitude, s, snap, state):
            add_increment(
                lambda f, x, y: own(state, f, x, y, 1),
                reader(snap),
                lambda f, x, y: slopes[4 * snap + f, x, column_rows(y, 1), :],
                sums,
                width_x,
                width_y,
            )

        run_round(place, 1, wind, inject, (here, there), (speed, dz_az, dz_p), after)
        me = lax.axis_index("pair")
        for f in range(4):
            for x in range(width_x):
                last[f, x] = own(here, f, x, 0, width_y)

        def sums_at(f, x, part, b):
            return sums[f, x, pl.ds(part * half_blocks + b, width_y, stride=ROWS), :]

        for f in range(4):
            for b in range(half_blocks):
                here_lanes = slice(b * LANES, (b + 1) * LANES)
                largest = jnp.abs(sums_at(f, 0, 1 - me, b))
                for x in range(1, width_x):
                    largest = jnp.maximum(largest, jnp.abs(sums_at(f, x, 1 - me, b)))
                largest = jnp.maximum(jnp.max(largest, axis=0, keepdims=True), 1e-30)
                scales[f : f + 1, here_lanes] = largest * (0.5 / 32767.0)
                inverse = 32767.0 / largest
                for x in range(0, width_x, 2):
                    two = [sums_at(f, x + i, 1 - me, b) * inverse for i in (0, 1)]
                    two = jnp.round(jnp.concatenate(two, axis=0))
                    other[f, x // 2, :, here_lanes] = two.astype(jnp.int32).astype(jnp.int16)
        for f in range(4):
            for x in range(width_x):
                mine[f, x] = sums[f, x]

    kernel_half = struct((4, width_x, width_y, half), F32)
    last, mine, other, scales = call(
        second_kernel,
        [
            struct((4,) + tile, F32),
            struct((4,) + tile, F32),
            struct((4, width_x // 2, 2 * width_y, half), jnp.int16),
            struct((4, half), F32),
        ],
        scratch=[VMEM((4,) + ext, F32)] * 2
        + [VMEM(ext, F32)] * 2
        + [VMEM((4,) + tile, F32)]
        + rim_scratch,
        micros=9.0,
        limit=30,
    )(
        wind_profile,
        injected,
        late,
        speed_ext,
        total,
        forward_late,
        slopes_late,
        *rim,
        *z_second,
        x_second,
        *d_second,
        again,
    )
    across = [(0, 1), (1, 0)]
    other, scales = lax.ppermute(other, "pair", across), lax.ppermute(scales, "pair", across)

    def final_kernel(last, sums, final, mine):
        me = lax.axis_index("pair")
        for f in range(4):
            for x in range(width_x):
                for b in range(blocks):
                    final[0, f, x, :, b * LANES : (b + 1) * LANES] = last[
                        f, x, pl.ds(b, width_y, stride=ROWS), :
                    ]
                for b in range(half_blocks):
                    mine[f, x, :, b * LANES : (b + 1) * LANES] = (
                        0.5 * sums[f, x, pl.ds(me * half_blocks + b, width_y, stride=ROWS), :]
                    )

    final, mine = call(
        final_kernel, [struct(adjoint_state.shape, F32), kernel_half], micros=1.0, limit=8
    )(last, mine)

    def sum_kernel(mine, other, scales, out):
        for f in range(4):
            for x in range(0, width_x, 2):
                two = other[f, x // 2].astype(jnp.int32).astype(F32) * scales[f : f + 1]
                for i in (0, 1):
                    out[f, x + i] = mine[f, x + i] + two[i * width_y : (i + 1) * width_y]

    kernels = call(sum_kernel, kernel_half, micros=0.8, limit=8)(mine, other, scales)
    return (kernels, final)


def solution(mesh):
    assert mesh.shape["pair"] == 2 and mesh.shape["gx"] % 2 == 0 and mesh.shape["gy"] % 2 == 0
    in_specs = (
        P("gx", "gy", None),
        P(),
        P(None, None, "gx", "gy", None),
        P("pair", None, "gx", "gy", None),
        P("pair"),
        P("pair", None),
        P("pair", None),
        P("pair", None),
    )
    out_specs = (P(None, "gx", "gy", "pair"), P("pair", None, "gx", "gy", None))
    return jax.shard_map(shards, mesh=mesh, in_specs=in_specs, out_specs=out_specs, check_vma=False)
```

```python
import jax
import jax.numpy as jnp
from jax import lax
from jax.experimental import pallas as pl
from jax.experimental.pallas import tpu as pltpu
from jax.sharding import PartitionSpec as P

step_length = 0.25
SCALE = 0.5 * step_length
HALO = 4
PER_ROUND = 2
LANES = 128
ROWS = 8
VMEM = pltpu.VMEM
CORNER = [(i, j) for i in range(1, HALO) for j in range(1, HALO) if i + j <= HALO]
BF = jnp.bfloat16
F32 = jnp.float32


def swap_pairs(size, odd):
    partner = [((i - odd) ^ 1) + odd for i in range(size)]
    return [(i, j if 0 <= j < size else i) for i, j in enumerate(partner)]


def swapped(x, axis, odd):
    return lax.ppermute(x, axis, swap_pairs(lax.axis_size(axis), odd))


def total_of(x, axis):
    size = lax.axis_size(axis)
    parts = [lax.ppermute(x, axis, [(i, (i + k) % size) for i in range(size)]) for k in range(1, size)]
    return sum(parts, x)


def summed(x, axis, k):
    size = lax.axis_size(axis)
    assert size & (size - 1) == 0
    while k < size:
        x = x + lax.ppermute(x, axis, [(i, i ^ k) for i in range(size)])
        k *= 2
    return x


def call(kernel, outs, scratch=(), micros=1.0, specs=None, out_specs=None, limit=16):
    def run(*args):
        return pl.pallas_call(
            kernel,
            out_shape=outs,
            in_specs=specs or [pl.BlockSpec(memory_space=VMEM)] * len(args),
            out_specs=out_specs
            or jax.tree.map(lambda _: pl.BlockSpec(memory_space=VMEM), outs),
            scratch_shapes=list(scratch),
            compiler_params=pltpu.CompilerParams(vmem_limit_bytes=limit * 2**20),
            cost_estimate=pl.CostEstimate(
                flops=int(1.1e9 * micros), bytes_accessed=100_000, transcendentals=0
            ),
        )(*args)

    return run


def struct(shape, dtype):
    return jax.ShapeDtypeStruct(shape, dtype)


class Place:
    def __init__(self):
        self.index = {}
        self.size = {}
        for axis in ("gx", "gy"):
            self.index[axis] = lax.axis_index(axis)
            self.size[axis] = lax.axis_size(axis)

    def plus(self, axis, odd):
        return lax.rem(self.index[axis], 2) == odd

    def has(self, axis, odd):
        i = self.index[axis]
        if not odd:
            return None
        return jnp.logical_and(i > 0, i < self.size[axis] - 1)


def column_rows(y, n):
    start = y * ROWS
    if not isinstance(start, int):
        start = pl.multiple_of(start, ROWS)
    return pl.ds(start, n * ROWS)


def face_depth(f, axis):
    return HALO if f in (0, {"gx": 1, "gy": 2}[axis]) else HALO - 1


def face_start(f, axis):
    return sum(face_depth(g, axis) for g in range(f))


def pack_faces(place, load, fields, width_x, width_y, z_out, x_out):
    for odd in (0, 1):
        for f in range(fields):
            deep = face_depth(f, "gy")
            y0 = jnp.where(place.plus("gy", odd), width_y - deep, 0)
            for x in range(width_x):
                value = load(f, x, y0, deep).reshape(deep, ROWS, LANES)
                at = face_start(f, "gy") * width_x + x * deep
                z_out[odd][pl.ds(at, deep)] = value.astype(BF)
            deep = face_depth(f, "gx")
            x0 = jnp.where(place.plus("gx", odd), width_x - deep, 0)
            for j in range(deep):
                value = load(f, x0 + j, 0, width_y)
                x_out[odd][face_start(f, "gx") + j] = value.astype(BF)


def corner_blocks(fields, width_y):
    return -(-2 * fields * len(CORNER) // width_y)


def corner_place(fields, odd_y, f, k, width_y):
    n = (odd_y * fields + f) * len(CORNER) + k
    return n // width_y, pl.ds(n % width_y * ROWS, 2 * ROWS)


def pack_corners(place, fields, width_x, width_y, z_in, out, first, odd_x):
    plus_x = place.plus("gx", odd_x)
    for odd_y in (0, 1):
        plus_y = place.plus("gy", odd_y)
        for f in range(fields):
            for k in range(0, len(CORNER), 2):
                two = []
                for i, j in CORNER[k : k + 2]:
                    x = jnp.where(plus_x, width_x - i, i - 1)
                    deep = face_depth(f, "gy")
                    y = jnp.where(plus_y, j - 1, deep - j)
                    at = face_start(f, "gy") * width_x + x * deep + y
                    two.append(z_in[odd_y][at].astype(F32))
                block, rows = corner_place(fields, odd_y, f, k, width_y)
                out[first + block, rows, :] = jnp.concatenate(two, axis=0).astype(BF)


def place_edges(place, store, fields, width_x, width_y, z_in, x_in, c_in, firsts):
    def masked(value, *conditions):
        value = value.astype(F32)
        for condition in conditions:
            if condition is not None:
                value = jnp.where(condition, value, 0.0)
        return value

    for odd in (0, 1):
        for f in range(fields):
            deep = face_depth(f, "gy")
            y0 = jnp.where(place.plus("gy", odd), width_y + HALO, HALO - deep)
            for x in range(width_x):
                at = face_start(f, "gy") * width_x + x * deep
                value = masked(z_in[odd][pl.ds(at, deep)], place.has("gy", odd))
                store(f, HALO + x, y0, deep, value.reshape(deep * ROWS, LANES))
            deep = face_depth(f, "gx")
            x0 = jnp.where(place.plus("gx", odd), width_x + HALO, HALO - deep)
            for j in range(deep):
                value = masked(x_in[odd][face_start(f, "gx") + j], place.has("gx", odd))
                store(f, x0 + j, HALO, width_y, value)
    for odd_x in (0, 1):
        plus_x = place.plus("gx", odd_x)
        for odd_y in (0, 1):
            plus_y = place.plus("gy", odd_y)
            for f in range(fields):
                for k in range(0, len(CORNER), 2):
                    block, rows = corner_place(fields, odd_y, f, k, width_y)
                    two = c_in[odd_x][firsts[odd_x] + block, rows, :].astype(F32)
                    two = [two[:ROWS], two[ROWS:]]
                    for value, (i, j) in zip(two, CORNER[k : k + 2]):
                        x = jnp.where(plus_x, HALO + width_x - 1 + i, HALO - i)
                        y = jnp.where(plus_y, HALO + width_y - 1 + j, HALO - j)
                        value = masked(value, place.has("gx", odd_x), place.has("gy", odd_y))
                        store(f, x, y, 1, value)


class Altitude:
    def __init__(self):
        lane = lax.broadcasted_iota(jnp.int32, (ROWS, LANES), 1)
        row = lax.broadcasted_iota(jnp.int32, (ROWS, LANES), 0)
        self.last_lane = lane == LANES - 1
        self.first_lane = lane == 0
        self.last_row = row == ROWS - 1
        self.first_row = row == 0

    def __call__(self, v):
        up = pltpu.roll(v, LANES - 1, 1)
        carried = jnp.where(self.last_row, 0.0, pltpu.roll(up, ROWS - 1, 0))
        up = jnp.where(self.last_lane, carried, up)
        down = pltpu.roll(v, 1, 1)
        carried = jnp.where(self.first_row, 0.0, pltpu.roll(down, 1, 0))
        down = jnp.where(self.first_lane, carried, down)
        return up - down


def over_diamond(radius, width_x, width_y, row, sides):
    def own(i, carry):
        row(HALO + i, HALO - radius, width_y + 2 * radius, None)
        return carry

    lax.fori_loop(0, width_x, own, 0)
    for d in range(1, radius + 1):
        rest = radius - d
        row(HALO - d, HALO - rest, width_y + 2 * rest, sides[0])
        row(HALO + width_x - 1 + d, HALO - rest, width_y + 2 * rest, sides[1])


def advance(
    place, altitude, old, new, state_dz, wind, inject, radius, own_dz, width_x, width_y
):
    east, north, vertical = wind
    speed, dz_az, dz_p = state_dz
    sides = {
        axis: [
            jnp.where(place.index[axis] == edge, 0.0, 1.0) for edge in (0, place.size[axis] - 1)
        ]
        for axis in ("gx", "gy")
    }

    def at(ref, x, y):
        return ref[x, column_rows(y, 1), :]

    def inside(value, kept, y):
        if y < HALO or y >= HALO + width_y:
            side = sides["gy"][int(y > HALO)]
            kept = side if kept is None else kept * side
        return value if kept is None else value * kept

    p, ax, ay, az = (old.at[f] for f in range(4))

    def slope(f, value, x, y, kept):
        if own_dz is None or kept is not None or not HALO <= y < HALO + width_y:
            return altitude(value)
        return own_dz[f, x - HALO, column_rows(y - HALO, 1), :]

    def p_row(x, y0, n, kept):
        ps = [at(p, x, y0 + k - 1) for k in range(n + 2)]
        ays = [at(ay, x, y0 + k - 1) for k in range(n + 2)]
        for k in range(n):
            y = y0 + k
            up = slope(3, at(az, x, y), x, y, kept)
            dz_az[x, column_rows(y, 1), :] = up
            up_p = at(dz_p, x, y) if own_dz is None else slope(0, ps[k + 1], x, y, kept)
            div = (at(ax, x + 1, y) - at(ax, x - 1, y)) + (ays[k + 2] - ays[k]) + up
            value = (
                at(speed, x, y) * div
                + east * (at(p, x + 1, y) - at(p, x - 1, y))
                + north * (ps[k + 2] - ps[k])
                + vertical * up_p
            )
            value = ps[k + 1] + value + inject(x, y)
            new[0, x, column_rows(y, 1), :] = inside(value, kept, y)

    over_diamond(radius, width_x, width_y, p_row, sides["gx"])
    pn = new.at[0]

    def a_row(x, y0, n, kept):
        ps = [at(pn, x, y0 + k - 1) for k in range(n + 2)]
        for f, a in ((1, ax), (2, ay), (3, az)):
            vs = [at(a, x, y0 + k - 1) for k in range(n + 2)]
            for k in range(n):
                y = y0 + k
                if f == 1:
                    grad = at(pn, x + 1, y) - at(pn, x - 1, y)
                elif f == 2:
                    grad = ps[k + 2] - ps[k]
                else:
                    grad = altitude(ps[k + 1])
                    if radius > 1:
                        dz_p[x, column_rows(y, 1), :] = grad
                up = at(dz_az, x, y) if f == 3 else slope(f, vs[k + 1], x, y, kept)
                value = (
                    SCALE * grad
                    + east * (at(a, x + 1, y) - at(a, x - 1, y))
                    + north * (vs[k + 2] - vs[k])
                    + vertical * up
                )
                new[f, x, column_rows(y, 1), :] = inside(vs[k + 1] + value, kept, y)

    over_diamond(radius - 1, width_x, width_y, a_row, sides["gx"])


def add_increment(state, forward, forward_dz, total, width_x, width_y):
    def row(i):
        for k in range(width_y):
            p, ax, ay, az = (state(f, i, k) for f in range(4))
            dx = [forward(f, i + 1, k) - forward(f, i - 1, k) for f in range(4)]
            dy = [forward(f, i, k + 1) - forward(f, i, k - 1) for f in range(4)]
            dz = [forward_dz(f, i, k) for f in range(4)]
            rows = column_rows(k, 1)
            total[0, i, rows, :] += p * (dx[1] + dy[2] + dz[3])
            for n, d in ((1, dx), (2, dy), (3, dz)):
                total[n, i, rows, :] += p * d[0] + ax * d[1] + ay * d[2] + az * d[3]

    def inner(i, carry):
        row(i)
        return carry

    row(0)
    lax.fori_loop(1, width_x - 1, inner, 0)
    row(width_x - 1)


def shards(
    sound_speed_sq,
    wind_profile,
    forward_field,
    adjoint_state,
    pair_counts,
    source_cells,
    receiver_cells,
    residuals,
):
    steps_total = forward_field.shape[0]
    width_x, width_y, depth = sound_speed_sq.shape
    slots = residuals.shape[0]
    ext_x, ext_y = width_x + 2 * HALO, width_y + 2 * HALO
    blocks = depth // LANES
    assert blocks == ROWS and steps_total == 2 * PER_ROUND and slots % (2 * LANES) == 0 and slots <= 8 * LANES
    assert width_x == width_y and width_x % 2 == 0
    tile = (width_x, width_y * ROWS, LANES)
    ext = (ext_x, ext_y * ROWS, LANES)
    block = (width_y * ROWS, LANES)
    forward_fields = 4 * steps_total

    def face_structs(fields, more=0):
        columns = face_start(fields, "gy") + more // 2
        z = struct((columns * width_x, ROWS, LANES), BF)
        x = [struct((face_start(fields, "gx") + more,) + block, BF)] * 2
        return [z, z, *x]

    def first_hop(faces):
        z_even, z_odd, _, x_odd = faces
        z = [swapped(z_even, "gy", 0), swapped(z_odd, "gy", 1)]
        return z, swapped(x_odd, "gx", 1)

    def second_hop(fields, z, faces, first):
        ahead = faces.shape[0]
        corners = corner_blocks(fields, width_y)

        def corner_kernel(z_even, z_odd, faces, even, odd, *rim):
            place = Place()
            even[:ahead] = faces[...]
            z = (z_even, z_odd)
            pack_corners(place, fields, width_x, width_y, z, even, ahead, 0)
            pack_corners(place, fields, width_x, width_y, z, odd, 0, 1)
            for out in rim:
                for odd_y, ref in enumerate(z):
                    for n in range(4 * PER_ROUND):
                        value = ref[pl.ds(rim_z_at + n * width_x, width_x)].reshape(block)
                        out[4 * PER_ROUND * odd_y + n] = value

        outs = [struct((n + corners,) + block, BF) for n in (ahead, 0)]
        if first:
            outs.append(struct((8 * PER_ROUND,) + block, BF))
        even, odd, *rim = call(corner_kernel, outs, micros=0.3, limit=8)(*z, faces)
        rim = [lax.ppermute(r, "pair", [(0, 1), (1, 0)]) for r in rim]
        return [swapped(even, "gx", 0), swapped(odd, "gx", 1), *rim]

    whole = pl.BlockSpec(memory_space=VMEM)
    remain = pl.BlockSpec(memory_space=pltpu.HBM)

    def sample_kernel(source, forward, sample, pressure, done):
        copy = pltpu.make_async_copy(forward.at[:, 0], pressure, done)
        copy.start()
        local_x = source[0:1] - lax.axis_index("gx") * width_x
        local_y = source[1:2] - lax.axis_index("gy") * width_y
        inside = (local_x >= 0) & (local_x < width_x) & (local_y >= 0) & (local_y < width_y)
        where = jnp.where(inside, local_x * width_y + local_y, -1)
        cells = width_x * width_y
        chosen = lax.broadcasted_iota(jnp.int32, (cells, slots), 0) == where
        chosen = jnp.where(chosen, 1.0, 0.0).astype(BF)
        level = lax.broadcasted_iota(jnp.int32, (depth, slots), 0) == source[2:3]
        row = lax.broadcasted_iota(jnp.int32, (ROWS, slots), 0)
        result = jnp.zeros((ROWS, slots), F32)
        copy.wait()
        for t in range(steps_total):
            columns = lax.dot_general(
                pressure[t].reshape(cells, depth),
                chosen,
                (((0,), (0,)), ((), ())),
                preferred_element_type=F32,
            )
            picked = jnp.sum(jnp.where(level, columns, 0.0), axis=0, keepdims=True)
            result = jnp.where(row == t, picked, result)
        sample[...] = result

    samples = call(
        sample_kernel,
        struct((ROWS, slots), F32),
        scratch=[VMEM((steps_total, width_x, width_y, depth), BF), pltpu.SemaphoreType.DMA],
        specs=[whole, remain],
        micros=1.5,
        limit=8,
    )(source_cells.T, forward_field)
    state, samples = lax.optimization_barrier((adjoint_state, samples))
    samples = total_of(samples, "gx")

    def pack_kernel(state, speed, forward, cols, speed_cols, early, late, *outs):
        place = Place()
        for x in range(width_x):
            for b in range(blocks):
                at = pl.ds(b, width_y, stride=ROWS)
                here = slice(b * LANES, (b + 1) * LANES)
                for f in range(4):
                    cols[f, x, at, :] = state[0, f, x, :, here]
                speed_cols[x, at, :] = speed[x, :, here] * SCALE

        def load(f, x, y, n):
            ref = cols.at[f] if f < 4 else speed_cols
            return ref[x, column_rows(y, n), :]

        pack_faces(place, load, 5, width_x, width_y, outs[:2], outs[2:])

        mine_is_late = lax.axis_index("pair") == 0

        def one(n, carry):
            t, f = n // 4, lax.rem(n, 4)
            for is_late, ref, snap in ((True, late, t), (False, early, t + PER_ROUND)):
                number = snap * 4 + f
                for x in range(width_x):
                    for b in range(blocks):
                        ref[n, x, pl.ds(b, width_y, stride=ROWS), :] = forward[
                            snap, f, x, :, b * LANES : (b + 1) * LANES
                        ].astype(F32)
                for odd in (0, 1):
                    y = jnp.where(place.plus("gy", odd), width_y - 1, 0)
                    x = jnp.where(place.plus("gx", odd), width_x - 1, 0)
                    outs[2 + odd][rim_at + number] = ref[n, x].astype(BF)
                    value = ref[n, :, column_rows(y, 1), :].astype(BF)
                    to = rim_z_at + n * width_x

                    @pl.when(mine_is_late if is_late else jnp.logical_not(mine_is_late))
                    def _():
                        outs[odd][pl.ds(to, width_x)] = value

            return carry

        lax.fori_loop(0, 4 * PER_ROUND, one, 0)

    rim_z_at, rim_at = face_start(5, "gy") * width_x, face_start(5, "gx")
    packed = call(
        pack_kernel,
        [struct((4,) + tile, F32), struct(tile, F32)]
        + [struct((4 * PER_ROUND,) + tile, F32)] * 2
        + face_structs(5, forward_fields),
        micros=1.3,
        limit=12,
    )(state, sound_speed_sq, forward_field)
    cols, speed_cols, forward_early, forward_late = packed[:4]
    faces = packed[4:]
    z_first, x_first = first_hop(faces)

    def own_slopes(cols):
        def kernel(cols, out):
            altitude = Altitude()

            def one(f, carry):
                for x in range(width_x):
                    for y in range(width_y):
                        rows = column_rows(y, 1)
                        out[f, x, rows, :] = altitude(cols[f, x, rows, :])
                return carry

            lax.fori_loop(0, 4, one, 0)

        return call(kernel, struct((4,) + tile, F32), micros=0.8, limit=8)(cols)

    own_dz = own_slopes(cols)

    def slope_kernel(early, late, sample, *outs):
        *outs, held = outs
        held[...] = sample[...]
        altitude = Altitude()

        def one(n, carry):
            for ref, out in zip((early, late), outs):
                for x in range(width_x):
                    for y in range(width_y):
                        rows = column_rows(y, 1)
                        out[n, x, rows, :] = altitude(ref[n, x, rows, :])
            return carry

        lax.fori_loop(0, 4 * PER_ROUND, one, 0)

    slopes_early, slopes_late, samples = call(
        slope_kernel,
        [struct((4 * PER_ROUND,) + tile, F32)] * 2 + [struct(samples.shape, F32)],
        micros=2.7,
        limit=8,
    )(forward_early, forward_late, samples)
    samples = total_of(samples, "gy")

    z_first, x_first, samples, slopes_early, slopes_late, own_dz = lax.optimization_barrier(
        (z_first, x_first, samples, slopes_early, slopes_late, own_dz)
    )
    hop, hop_odd, rim_z = second_hop(5, z_first, faces[2], True)

    def inject_kernel(counts, receiver, misfit, samples, out):
        local_x = receiver[0:1] - (lax.axis_index("gx") * width_x - HALO)
        local_y = receiver[1:2] - (lax.axis_index("gy") * width_y - HALO)
        inside = (local_x >= 0) & (local_x < ext_x) & (local_y >= 0) & (local_y < ext_y)
        live = lax.broadcasted_iota(jnp.int32, (1, slots), 1) < counts[0]
        where = jnp.where(inside & live, local_x * ext_y + local_y, -1)
        cells = ext_x * ext_y
        chosen = lax.broadcasted_iota(jnp.int32, (cells, slots), 0) == where
        level = lax.broadcasted_iota(jnp.int32, (depth, slots), 0) == receiver[2:3]
        level = jnp.where(level, 1.0, 0.0).astype(BF)
        for t in range(steps_total):
            amplitude = misfit[t : t + 1] * samples[t : t + 1]
            head = amplitude.astype(BF).astype(F32)
            result = jnp.zeros((cells, depth), F32)
            for part in (head, amplitude - head):
                spread = jnp.where(chosen, part, 0.0).astype(BF)
                result += lax.dot_general(
                    spread, level, (((1,), (1,)), ((), ())), preferred_element_type=F32
                )
            for g in range(cells // ROWS):
                for b in range(blocks):
                    out[t, pl.ds(g * ROWS * ROWS + b, ROWS, stride=ROWS), :] = result[
                        g * ROWS : (g + 1) * ROWS, b * LANES : (b + 1) * LANES
                    ]

    injected = call(
        inject_kernel,
        struct((steps_total, ext_x * ext_y * ROWS, LANES), F32),
        specs=[pl.BlockSpec(memory_space=pltpu.SMEM)] + [whole] * 3,
        micros=1.6,
    )(pair_counts, receiver_cells.T, residuals.T, samples)

    rim_scratch = [
        VMEM((2, 4 * PER_ROUND) + block, F32),
        VMEM((2, 4 * PER_ROUND) + block, F32),
    ]

    def forward_of(place, columns, first, z_even, z_odd, z_other, x_even, x_odd, rim_y, rim_x):
        from_pair = (lax.axis_index("pair") == 0) == (first == 0)
        for odd, z, x in ((0, z_even, x_even), (1, z_odd, x_odd)):
            side_x = jnp.where(place.plus("gx", odd), 1, 0)
            side_y = jnp.where(place.plus("gy", odd), 1, 0)
            for n in range(4 * PER_ROUND):
                value = x[rim_at + 4 * first + n].astype(F32)
                if odd:
                    value = jnp.where(place.has("gx", odd), value, 0.0)
                rim_x[side_x, n] = value
                own_z = z[pl.ds(rim_z_at + n * width_x, width_x)].astype(F32).reshape(block)
                other = z_other[4 * PER_ROUND * odd + n].astype(F32)
                value = jnp.where(from_pair, own_z, other)
                if odd:
                    value = jnp.where(place.has("gy", odd), value, 0.0)
                rim_y[side_y, n] = value

        def reader(snap):
            base = 4 * (snap - first)

            def column(f, x, y):
                if isinstance(x, int) and x in (-1, width_x):
                    return rim_x[int(x > 0), base + f, column_rows(y, 1), :]
                if y in (-1, width_y):
                    rows = x * ROWS if isinstance(x, int) else pl.multiple_of(x * ROWS, ROWS)
                    return rim_y[int(y > 0), base + f, pl.ds(rows, ROWS), :]
                return columns[base + f, x, column_rows(y, 1), :]

            return column

        return reader

    def run_round(place, number, wind, inject, buffers, state_dz, own_dz, after):
        altitude = Altitude()
        winds = []
        for i in range(3):
            rows = [wind[i : i + 1, b * LANES : (b + 1) * LANES] for b in range(blocks)]
            winds.append(jnp.concatenate(rows, axis=0) * SCALE)
        for s in range(PER_ROUND):
            step = number * PER_ROUND + s
            snap = steps_total - 1 - step
            old, new = buffers[s % 2], buffers[(s + 1) % 2]

            def injected_at(x, y):
                start = (x * ext_y + y) * ROWS
                if not isinstance(start, int):
                    start = pl.multiple_of(start, ROWS)
                return inject[snap, pl.ds(start, ROWS), :]

            radius = 2 * (PER_ROUND - 1 - s) + 1
            advance(
                place,
                altitude,
                old,
                new,
                state_dz,
                winds,
                injected_at,
                radius,
                None if s else own_dz,
                width_x,
                width_y,
            )
            after(altitude, s, snap, new)

    def own(ref, f, x, y, n):
        return ref[f, HALO + x, column_rows(HALO + y, n), :]

    def fill(place, buffer, speed, cols, speed_cols, z_in, x_in, c_in, firsts):
        def store(f, x, y, n, value):
            ref = buffer.at[f] if f < 4 else speed
            ref[x, column_rows(y, n), :] = value

        for f in range(4):
            for x in range(width_x):
                store(f, HALO + x, HALO, width_y, cols[f, x])
        fields = 4
        if speed_cols is not None:
            fields = 5
            for x in range(width_x):
                store(4, HALO + x, HALO, width_y, speed_cols[x])
        place_edges(place, store, fields, width_x, width_y, z_in, x_in, c_in, firsts)

    def first_kernel(wind, inject, cols, own_dz, speed_cols, z0, z1, x1, c0, c1, *refs):
        early, late, speed, *faces, here, there, dz_az, dz_p = refs
        place = Place()
        corners_at = (rim_at + forward_fields, 0)
        fill(place, here, speed, cols, speed_cols, (z0, z1), (c0, x1), (c0, c1), corners_at)

        def after(altitude, s, snap, state):
            out = (early, late)[s]
            for f in range(4):
                for x in range(width_x):
                    out[f, x] = own(state, f, x, 0, width_y)

        run_round(place, 0, wind, inject, (here, there), (speed, dz_az, dz_p), own_dz, after)

        def load(f, x, y, n):
            return own(here, f, x, y, n)

        pack_faces(place, load, 4, width_x, width_y, faces[:2], faces[2:])

    first = call(
        first_kernel,
        [struct((4,) + tile, F32)] * 2 + [struct(ext, F32)] + face_structs(4),
        scratch=[VMEM((4,) + ext, F32)] * 2 + [VMEM(ext, F32)] * 2,
        micros=6.0,
        limit=28,
    )(
        wind_profile, injected, cols, own_dz, speed_cols, *z_first, x_first, hop, hop_odd
    )
    early, late, speed_ext = first[:3]
    z_second, x_second = first_hop(first[3:])

    rim = (*z_first, rim_z, hop, x_first)

    def early_kernel(early, late, columns, slopes, z0, z1, zp, c0, x1, total, rim_y, rim_x):
        place = Place()
        reader = forward_of(place, columns, PER_ROUND, z0, z1, zp, c0, x1, rim_y, rim_x)
        total[...] = jnp.zeros_like(total)
        for s, state in ((0, early), (1, late)):
            add_increment(
                lambda f, x, y: state[f, x, column_rows(y, 1), :],
                reader(steps_total - 1 - s),
                lambda f, x, y: slopes[
                    4 * (steps_total - 1 - s - PER_ROUND) + f, x, column_rows(y, 1), :
                ],
                total,
                width_x,
                width_y,
            )

    total = call(early_kernel, struct((4,) + tile, F32), scratch=rim_scratch, micros=2.3, limit=16)(
        early, late, forward_early, slopes_early, *rim
    )
    late_dz = own_slopes(late)
    z_second, x_second, total, late_dz = lax.optimization_barrier(
        (z_second, x_second, total, late_dz)
    )
    again, again_odd = second_hop(4, z_second, first[5], False)

    half = depth // 2
    half_blocks = blocks // 2

    def second_kernel(
        wind, inject, cols, own_dz, speed, total, columns, slopes, *refs
    ):
        rims, (z0, z1, x1, c0, c1), refs = refs[:5], refs[5:10], refs[10:]
        last, mine, other, scales, here, there, dz_az, dz_p, sums, rim_y, rim_x = refs
        place = Place()
        fill(place, here, None, cols, None, (z0, z1), (c0, x1), (c0, c1), (face_start(4, "gx"), 0))
        reader = forward_of(place, columns, 0, *rims, rim_y, rim_x)
        sums[...] = total[...]

        def after(altitude, s, snap, state):
            add_increment(
                lambda f, x, y: own(state, f, x, y, 1),
                reader(snap),
                lambda f, x, y: slopes[4 * snap + f, x, column_rows(y, 1), :],
                sums,
                width_x,
                width_y,
            )

        run_round(place, 1, wind, inject, (here, there), (speed, dz_az, dz_p), own_dz, after)
        me = lax.axis_index("pair")
        for f in range(4):
            for x in range(width_x):
                last[f, x] = own(here, f, x, 0, width_y)

        def sums_at(f, x, part, b):
            return sums[f, x, pl.ds(part * half_blocks + b, width_y, stride=ROWS), :]

        for f in range(4):
            for b in range(half_blocks):
                here_lanes = slice(b * LANES, (b + 1) * LANES)
                largest = jnp.abs(sums_at(f, 0, 1 - me, b))
                for x in range(1, width_x):
                    largest = jnp.maximum(largest, jnp.abs(sums_at(f, x, 1 - me, b)))
                largest = jnp.maximum(jnp.max(largest, axis=0, keepdims=True), 1e-30)
                scales[f : f + 1, here_lanes] = largest * (0.5 / 32767.0)
                inverse = 32767.0 / largest
                for x in range(0, width_x, 2):
                    two = [sums_at(f, x + i, 1 - me, b) * inverse for i in (0, 1)]
                    two = jnp.round(jnp.concatenate(two, axis=0))
                    other[f, x // 2, :, here_lanes] = two.astype(jnp.int32).astype(jnp.int16)
        for f in range(4):
            for x in range(width_x):
                mine[f, x] = sums[f, x]

    kernel_half = struct((4, width_x, width_y, half), F32)
    last, mine, other, scales = call(
        second_kernel,
        [
            struct((4,) + tile, F32),
            struct((4,) + tile, F32),
            struct((4, width_x // 2, 2 * width_y, half), jnp.int16),
            struct((4, half), F32),
        ],
        scratch=[VMEM((4,) + ext, F32)] * 2
        + [VMEM(ext, F32)] * 2
        + [VMEM((4,) + tile, F32)]
        + rim_scratch,
        micros=9.0,
        limit=30,
    )(
        wind_profile,
        injected,
        late,
        late_dz,
        speed_ext,
        total,
        forward_late,
        slopes_late,
        *rim,
        *z_second,
        x_second,
        again,
        again_odd,
    )
    across = [(0, 1), (1, 0)]
    other, scales = lax.ppermute(other, "pair", across), lax.ppermute(scales, "pair", across)

    def final_kernel(last, sums, final, mine):
        me = lax.axis_index("pair")
        for f in range(4):
            for x in range(width_x):
                for b in range(blocks):
                    final[0, f, x, :, b * LANES : (b + 1) * LANES] = last[
                        f, x, pl.ds(b, width_y, stride=ROWS), :
                    ]
                for b in range(half_blocks):
                    mine[f, x, :, b * LANES : (b + 1) * LANES] = (
                        0.5 * sums[f, x, pl.ds(me * half_blocks + b, width_y, stride=ROWS), :]
                    )

    final, mine = call(
        final_kernel, [struct(adjoint_state.shape, F32), kernel_half], micros=1.0, limit=8
    )(last, mine)

    def sum_kernel(mine, other, scales, out):
        for f in range(4):
            for x in range(0, width_x, 2):
                two = other[f, x // 2].astype(jnp.int32).astype(F32) * scales[f : f + 1]
                for i in (0, 1):
                    out[f, x + i] = mine[f, x + i] + two[i * width_y : (i + 1) * width_y]

    kernels = call(sum_kernel, kernel_half, micros=0.8, limit=8)(mine, other, scales)
    return (kernels, final)


def solution(mesh):
    assert mesh.shape["pair"] == 2 and mesh.shape["gx"] % 2 == 0 and mesh.shape["gy"] % 2 == 0
    in_specs = (
        P("gx", "gy", None),
        P(),
        P(None, None, "gx", "gy", None),
        P("pair", None, "gx", "gy", None),
        P("pair"),
        P("pair", None),
        P("pair", None),
        P("pair", None),
    )
    out_specs = (P(None, "gx", "gy", "pair"), P("pair", None, "gx", "gy", None))
    return jax.shard_map(shards, mesh=mesh, in_specs=in_specs, out_specs=out_specs, check_vma=False)
```

```python
import jax
import jax.numpy as jnp
from jax import lax
from jax.experimental import pallas as pl
from jax.experimental.pallas import tpu as pltpu
from jax.sharding import PartitionSpec as P

step_length = 0.25
SCALE = 0.5 * step_length
HALO = 4
PER_ROUND = 2
LANES = 128
ROWS = 8
VMEM = pltpu.VMEM
CORNER = [(i, j) for i in range(1, HALO) for j in range(1, HALO) if i + j <= HALO]
BF = jnp.bfloat16
F32 = jnp.float32


def swap_pairs(size, odd):
    partner = [((i - odd) ^ 1) + odd for i in range(size)]
    return [(i, j if 0 <= j < size else i) for i, j in enumerate(partner)]


def swapped(x, axis, odd):
    return lax.ppermute(x, axis, swap_pairs(lax.axis_size(axis), odd))


def total_of(x, axis):
    size = lax.axis_size(axis)
    parts = [lax.ppermute(x, axis, [(i, (i + k) % size) for i in range(size)]) for k in range(1, size)]
    return sum(parts, x)


def summed(x, axis, k):
    size = lax.axis_size(axis)
    assert size & (size - 1) == 0
    while k < size:
        x = x + lax.ppermute(x, axis, [(i, i ^ k) for i in range(size)])
        k *= 2
    return x


def call(kernel, outs, scratch=(), micros=1.0, specs=None, out_specs=None, limit=16):
    def run(*args):
        return pl.pallas_call(
            kernel,
            out_shape=outs,
            in_specs=specs or [pl.BlockSpec(memory_space=VMEM)] * len(args),
            out_specs=out_specs
            or jax.tree.map(lambda _: pl.BlockSpec(memory_space=VMEM), outs),
            scratch_shapes=list(scratch),
            compiler_params=pltpu.CompilerParams(vmem_limit_bytes=limit * 2**20),
            cost_estimate=pl.CostEstimate(
                flops=int(1.1e9 * micros), bytes_accessed=100_000, transcendentals=0
            ),
        )(*args)

    return run


def struct(shape, dtype):
    return jax.ShapeDtypeStruct(shape, dtype)


class Place:
    def __init__(self):
        self.index = {}
        self.size = {}
        for axis in ("gx", "gy"):
            self.index[axis] = lax.axis_index(axis)
            self.size[axis] = lax.axis_size(axis)

    def plus(self, axis, odd):
        return lax.rem(self.index[axis], 2) == odd

    def has(self, axis, odd):
        i = self.index[axis]
        if not odd:
            return None
        return jnp.logical_and(i > 0, i < self.size[axis] - 1)


def column_rows(y, n):
    start = y * ROWS
    if not isinstance(start, int):
        start = pl.multiple_of(start, ROWS)
    return pl.ds(start, n * ROWS)


def face_depth(f, axis):
    return HALO if f in (0, {"gx": 1, "gy": 2}[axis]) else HALO - 1


def face_start(f, axis):
    return sum(face_depth(g, axis) for g in range(f))


def pack_faces(place, load, fields, width_x, width_y, z_out, x_out):
    for odd in (0, 1):
        for f in range(fields):
            deep = face_depth(f, "gy")
            y0 = jnp.where(place.plus("gy", odd), width_y - deep, 0)
            for x in range(width_x):
                value = load(f, x, y0, deep).reshape(deep, ROWS, LANES)
                at = face_start(f, "gy") * width_x + x * deep
                z_out[odd][pl.ds(at, deep)] = value.astype(BF)
            deep = face_depth(f, "gx")
            x0 = jnp.where(place.plus("gx", odd), width_x - deep, 0)
            for j in range(deep):
                value = load(f, x0 + j, 0, width_y)
                x_out[odd][face_start(f, "gx") + j] = value.astype(BF)


def corner_blocks(fields, width_y):
    return -(-2 * fields * len(CORNER) // width_y)


def corner_place(fields, odd_y, f, k, width_y):
    n = (odd_y * fields + f) * len(CORNER) + k
    return n // width_y, pl.ds(n % width_y * ROWS, 2 * ROWS)


def pack_corners(place, fields, width_x, width_y, z_in, out, first, odd_x):
    plus_x = place.plus("gx", odd_x)
    for odd_y in (0, 1):
        plus_y = place.plus("gy", odd_y)
        for f in range(fields):
            for k in range(0, len(CORNER), 2):
                two = []
                for i, j in CORNER[k : k + 2]:
                    x = jnp.where(plus_x, width_x - i, i - 1)
                    deep = face_depth(f, "gy")
                    y = jnp.where(plus_y, j - 1, deep - j)
                    at = face_start(f, "gy") * width_x + x * deep + y
                    two.append(z_in[odd_y][at].astype(F32))
                block, rows = corner_place(fields, odd_y, f, k, width_y)
                out[first + block, rows, :] = jnp.concatenate(two, axis=0).astype(BF)


def place_edges(place, store, fields, width_x, width_y, z_in, x_in, c_in, firsts):
    def masked(value, *conditions):
        value = value.astype(F32)
        for condition in conditions:
            if condition is not None:
                value = jnp.where(condition, value, 0.0)
        return value

    for odd in (0, 1):
        for f in range(fields):
            deep = face_depth(f, "gy")
            y0 = jnp.where(place.plus("gy", odd), width_y + HALO, HALO - deep)
            for x in range(width_x):
                at = face_start(f, "gy") * width_x + x * deep
                value = masked(z_in[odd][pl.ds(at, deep)], place.has("gy", odd))
                store(f, HALO + x, y0, deep, value.reshape(deep * ROWS, LANES))
            deep = face_depth(f, "gx")
            x0 = jnp.where(place.plus("gx", odd), width_x + HALO, HALO - deep)
            for j in range(deep):
                value = masked(x_in[odd][face_start(f, "gx") + j], place.has("gx", odd))
                store(f, x0 + j, HALO, width_y, value)
    for odd_x in (0, 1):
        plus_x = place.plus("gx", odd_x)
        for odd_y in (0, 1):
            plus_y = place.plus("gy", odd_y)
            for f in range(fields):
                for k in range(0, len(CORNER), 2):
                    block, rows = corner_place(fields, odd_y, f, k, width_y)
                    two = c_in[odd_x][firsts[odd_x] + block, rows, :].astype(F32)
                    two = [two[:ROWS], two[ROWS:]]
                    for value, (i, j) in zip(two, CORNER[k : k + 2]):
                        x = jnp.where(plus_x, HALO + width_x - 1 + i, HALO - i)
                        y = jnp.where(plus_y, HALO + width_y - 1 + j, HALO - j)
                        value = masked(value, place.has("gx", odd_x), place.has("gy", odd_y))
                        store(f, x, y, 1, value)


class Altitude:
    def __init__(self):
        lane = lax.broadcasted_iota(jnp.int32, (ROWS, LANES), 1)
        row = lax.broadcasted_iota(jnp.int32, (ROWS, LANES), 0)
        self.last_lane = lane == LANES - 1
        self.first_lane = lane == 0
        self.last_row = row == ROWS - 1
        self.first_row = row == 0

    def __call__(self, v):
        up = pltpu.roll(v, LANES - 1, 1)
        carried = jnp.where(self.last_row, 0.0, pltpu.roll(up, ROWS - 1, 0))
        up = jnp.where(self.last_lane, carried, up)
        down = pltpu.roll(v, 1, 1)
        carried = jnp.where(self.first_row, 0.0, pltpu.roll(down, 1, 0))
        down = jnp.where(self.first_lane, carried, down)
        return up - down


def over_diamond(radius, width_x, width_y, row, sides):
    def own(i, carry):
        row(HALO + i, HALO - radius, width_y + 2 * radius, None)
        return carry

    lax.fori_loop(0, width_x, own, 0)
    for d in range(1, radius + 1):
        rest = radius - d
        row(HALO - d, HALO - rest, width_y + 2 * rest, sides[0])
        row(HALO + width_x - 1 + d, HALO - rest, width_y + 2 * rest, sides[1])


def advance(
    place, altitude, old, new, state_dz, wind, inject, radius, own_dz, width_x, width_y
):
    east, north, vertical = wind
    speed, dz_az, dz_p = state_dz
    sides = {
        axis: [
            jnp.where(place.index[axis] == edge, 0.0, 1.0) for edge in (0, place.size[axis] - 1)
        ]
        for axis in ("gx", "gy")
    }

    def at(ref, x, y):
        return ref[x, column_rows(y, 1), :]

    def inside(value, kept, y):
        if y < HALO or y >= HALO + width_y:
            side = sides["gy"][int(y > HALO)]
            kept = side if kept is None else kept * side
        return value if kept is None else value * kept

    p, ax, ay, az = (old.at[f] for f in range(4))

    def slope(f, value, x, y, kept):
        if own_dz is None or kept is not None:
            return altitude(value)
        if HALO <= y < HALO + width_y:
            return own_dz[0][f, x - HALO, column_rows(y - HALO, 1), :]
        lower = jnp.where(place.plus("gy", 0), 1, 0)
        if y < HALO:
            return own_dz[1][lower, f, x - HALO, HALO - 1 - y]
        return own_dz[1][1 - lower, f, x - HALO, y - HALO - width_y]

    def p_row(x, y0, n, kept):
        ps = [at(p, x, y0 + k - 1) for k in range(n + 2)]
        ays = [at(ay, x, y0 + k - 1) for k in range(n + 2)]
        for k in range(n):
            y = y0 + k
            up = slope(3, at(az, x, y), x, y, kept)
            dz_az[x, column_rows(y, 1), :] = up
            up_p = at(dz_p, x, y) if own_dz is None else slope(0, ps[k + 1], x, y, kept)
            div = (at(ax, x + 1, y) - at(ax, x - 1, y)) + (ays[k + 2] - ays[k]) + up
            value = (
                at(speed, x, y) * div
                + east * (at(p, x + 1, y) - at(p, x - 1, y))
                + north * (ps[k + 2] - ps[k])
                + vertical * up_p
            )
            value = ps[k + 1] + value + inject(x, y)
            new[0, x, column_rows(y, 1), :] = inside(value, kept, y)

    over_diamond(radius, width_x, width_y, p_row, sides["gx"])
    pn = new.at[0]

    def a_row(x, y0, n, kept):
        ps = [at(pn, x, y0 + k - 1) for k in range(n + 2)]
        away = radius - 1 - (HALO - y0)
        for f, a in ((1, ax), (2, ay), (3, az)):
            if radius == 1:
                deep = 0
            elif f == 1:
                deep = radius - 2 if not away else radius - 1 - away
            elif f == 2:
                deep = radius - 1 - away if away < radius - 1 else -1
            else:
                deep = radius - 2 - away
            if deep < 0:
                continue
            start = HALO - deep - y0
            vs = [at(a, x, y0 + k - 1) for k in range(n + 2)]
            for k in range(start, n - start):
                y = y0 + k
                if f == 1:
                    grad = at(pn, x + 1, y) - at(pn, x - 1, y)
                elif f == 2:
                    grad = ps[k + 2] - ps[k]
                else:
                    grad = altitude(ps[k + 1])
                    if radius > 1:
                        dz_p[x, column_rows(y, 1), :] = grad
                up = at(dz_az, x, y) if f == 3 else slope(f, vs[k + 1], x, y, kept)
                value = (
                    SCALE * grad
                    + east * (at(a, x + 1, y) - at(a, x - 1, y))
                    + north * (vs[k + 2] - vs[k])
                    + vertical * up
                )
                new[f, x, column_rows(y, 1), :] = inside(vs[k + 1] + value, kept, y)

    over_diamond(radius - 1, width_x, width_y, a_row, sides["gx"])


def add_increment(state, forward, forward_dz, total, width_x, width_y):
    def row(i):
        for k in range(width_y):
            p, ax, ay, az = (state(f, i, k) for f in range(4))
            dx = [forward(f, i + 1, k) - forward(f, i - 1, k) for f in range(4)]
            dy = [forward(f, i, k + 1) - forward(f, i, k - 1) for f in range(4)]
            dz = [forward_dz(f, i, k) for f in range(4)]
            rows = column_rows(k, 1)
            total[0, i, rows, :] += p * (dx[1] + dy[2] + dz[3])
            for n, d in ((1, dx), (2, dy), (3, dz)):
                total[n, i, rows, :] += p * d[0] + ax * d[1] + ay * d[2] + az * d[3]

    def inner(i, carry):
        row(i)
        return carry

    row(0)
    lax.fori_loop(1, width_x - 1, inner, 0)
    row(width_x - 1)


def shards(
    sound_speed_sq,
    wind_profile,
    forward_field,
    adjoint_state,
    pair_counts,
    source_cells,
    receiver_cells,
    residuals,
):
    steps_total = forward_field.shape[0]
    width_x, width_y, depth = sound_speed_sq.shape
    slots = residuals.shape[0]
    ext_x, ext_y = width_x + 2 * HALO, width_y + 2 * HALO
    blocks = depth // LANES
    assert blocks == ROWS and steps_total == 2 * PER_ROUND and slots % (2 * LANES) == 0 and slots <= 8 * LANES
    assert width_x == width_y and width_x % 2 == 0
    tile = (width_x, width_y * ROWS, LANES)
    ext = (ext_x, ext_y * ROWS, LANES)
    block = (width_y * ROWS, LANES)
    forward_fields = 4 * steps_total

    def face_structs(fields, more=0):
        columns = face_start(fields, "gy") + more // 2
        z = struct((columns * width_x, ROWS, LANES), BF)
        x = [struct((face_start(fields, "gx") + more,) + block, BF)] * 2
        return [z, z, *x]

    def first_hop(faces):
        z_even, z_odd, _, x_odd = faces
        z = [swapped(z_even, "gy", 0), swapped(z_odd, "gy", 1)]
        return z, swapped(x_odd, "gx", 1)

    def second_hop(fields, z, faces, first):
        ahead = faces.shape[0]
        corners = corner_blocks(fields, width_y)

        def corner_kernel(z_even, z_odd, faces, even, odd, *rim):
            place = Place()
            even[:ahead] = faces[...]
            z = (z_even, z_odd)
            pack_corners(place, fields, width_x, width_y, z, even, ahead, 0)
            pack_corners(place, fields, width_x, width_y, z, odd, 0, 1)
            for out in rim:
                for odd_y, ref in enumerate(z):
                    for n in range(4 * PER_ROUND):
                        value = ref[pl.ds(rim_z_at + n * width_x, width_x)].reshape(block)
                        out[4 * PER_ROUND * odd_y + n] = value

        outs = [struct((n + corners,) + block, BF) for n in (ahead, 0)]
        if first:
            outs.append(struct((8 * PER_ROUND,) + block, BF))
        even, odd, *rim = call(corner_kernel, outs, micros=0.3, limit=8)(*z, faces)
        rim = [lax.ppermute(r, "pair", [(0, 1), (1, 0)]) for r in rim]
        return [swapped(even, "gx", 0), swapped(odd, "gx", 1), *rim]

    whole = pl.BlockSpec(memory_space=VMEM)
    remain = pl.BlockSpec(memory_space=pltpu.HBM)

    def sample_kernel(source, forward, sample, pressure, done):
        copy = pltpu.make_async_copy(forward.at[:, 0], pressure, done)
        copy.start()
        local_x = source[0:1] - lax.axis_index("gx") * width_x
        local_y = source[1:2] - lax.axis_index("gy") * width_y
        inside = (local_x >= 0) & (local_x < width_x) & (local_y >= 0) & (local_y < width_y)
        where = jnp.where(inside, local_x * width_y + local_y, -1)
        cells = width_x * width_y
        chosen = lax.broadcasted_iota(jnp.int32, (cells, slots), 0) == where
        chosen = jnp.where(chosen, 1.0, 0.0).astype(BF)
        level = lax.broadcasted_iota(jnp.int32, (depth, slots), 0) == source[2:3]
        row = lax.broadcasted_iota(jnp.int32, (ROWS, slots), 0)
        result = jnp.zeros((ROWS, slots), F32)
        copy.wait()
        for t in range(steps_total):
            columns = lax.dot_general(
                pressure[t].reshape(cells, depth),
                chosen,
                (((0,), (0,)), ((), ())),
                preferred_element_type=F32,
            )
            picked = jnp.sum(jnp.where(level, columns, 0.0), axis=0, keepdims=True)
            result = jnp.where(row == t, picked, result)
        sample[...] = result

    samples = call(
        sample_kernel,
        struct((ROWS, slots), F32),
        scratch=[VMEM((steps_total, width_x, width_y, depth), BF), pltpu.SemaphoreType.DMA],
        specs=[whole, remain],
        micros=1.5,
        limit=8,
    )(source_cells.T, forward_field)
    state, samples = lax.optimization_barrier((adjoint_state, samples))
    samples = total_of(samples, "gx")

    def pack_kernel(state, speed, forward, cols, speed_cols, early, late, *outs):
        place = Place()
        for x in range(width_x):
            for b in range(blocks):
                at = pl.ds(b, width_y, stride=ROWS)
                here = slice(b * LANES, (b + 1) * LANES)
                for f in range(4):
                    cols[f, x, at, :] = state[0, f, x, :, here]
                speed_cols[x, at, :] = speed[x, :, here] * SCALE

        def load(f, x, y, n):
            ref = cols.at[f] if f < 4 else speed_cols
            return ref[x, column_rows(y, n), :]

        pack_faces(place, load, 5, width_x, width_y, outs[:2], outs[2:])

        mine_is_late = lax.axis_index("pair") == 0

        def one(n, carry):
            t, f = n // 4, lax.rem(n, 4)
            for is_late, ref, snap in ((True, late, t), (False, early, t + PER_ROUND)):
                number = snap * 4 + f
                for x in range(width_x):
                    for b in range(blocks):
                        ref[n, x, pl.ds(b, width_y, stride=ROWS), :] = forward[
                            snap, f, x, :, b * LANES : (b + 1) * LANES
                        ].astype(F32)
                for odd in (0, 1):
                    y = jnp.where(place.plus("gy", odd), width_y - 1, 0)
                    x = jnp.where(place.plus("gx", odd), width_x - 1, 0)
                    outs[2 + odd][rim_at + number] = ref[n, x].astype(BF)
                    value = ref[n, :, column_rows(y, 1), :].astype(BF)
                    to = rim_z_at + n * width_x

                    @pl.when(mine_is_late if is_late else jnp.logical_not(mine_is_late))
                    def _():
                        outs[odd][pl.ds(to, width_x)] = value

            return carry

        lax.fori_loop(0, 4 * PER_ROUND, one, 0)

    rim_z_at, rim_at = face_start(5, "gy") * width_x, face_start(5, "gx")
    packed = call(
        pack_kernel,
        [struct((4,) + tile, F32), struct(tile, F32)]
        + [struct((4 * PER_ROUND,) + tile, F32)] * 2
        + face_structs(5, forward_fields),
        micros=1.3,
        limit=12,
    )(state, sound_speed_sq, forward_field)
    cols, speed_cols, forward_early, forward_late = packed[:4]
    faces = packed[4:]
    z_first, x_first = first_hop(faces)

    def own_slopes(cols):
        def kernel(cols, out):
            altitude = Altitude()

            def one(f, carry):
                for x in range(width_x):
                    for y in range(width_y):
                        rows = column_rows(y, 1)
                        out[f, x, rows, :] = altitude(cols[f, x, rows, :])
                return carry

            lax.fori_loop(0, 4, one, 0)

        return call(kernel, struct((4,) + tile, F32), micros=0.8, limit=8)(cols)

    own_dz = own_slopes(cols)

    def face_slopes(z):
        def kernel(z_even, z_odd, out):
            place, altitude = Place(), Altitude()

            def one(x, carry):
                for odd, ref in enumerate((z_even, z_odd)):
                    plus = place.plus("gy", odd)
                    for f, reach in enumerate((HALO - 1, 1, HALO - 2, HALO - 1)):
                        deep = face_depth(f, "gy")
                        for d in range(reach):
                            at = face_start(f, "gy") * width_x + x * deep
                            at += jnp.where(plus, d, deep - 1 - d)
                            out[odd, f, x, d] = altitude(ref[at].astype(F32))
                return carry

            lax.fori_loop(0, width_x, one, 0)

        out = struct((2, 4, width_x, HALO - 1, ROWS, LANES), F32)
        return call(kernel, out, micros=0.6, limit=8)(*z)

    def slope_kernel(early, late, sample, *outs):
        *outs, held = outs
        held[...] = sample[...]
        altitude = Altitude()

        def one(n, carry):
            for ref, out in zip((early, late), outs):
                for x in range(width_x):
                    for y in range(width_y):
                        rows = column_rows(y, 1)
                        out[n, x, rows, :] = altitude(ref[n, x, rows, :])
            return carry

        lax.fori_loop(0, 4 * PER_ROUND, one, 0)

    slopes_early, slopes_late, samples = call(
        slope_kernel,
        [struct((4 * PER_ROUND,) + tile, F32)] * 2 + [struct(samples.shape, F32)],
        micros=2.7,
        limit=8,
    )(forward_early, forward_late, samples)
    samples = total_of(samples, "gy")

    z_first, x_first, samples, slopes_early, slopes_late, own_dz = lax.optimization_barrier(
        (z_first, x_first, samples, slopes_early, slopes_late, own_dz)
    )
    hop, hop_odd, rim_z = second_hop(5, z_first, faces[2], True)

    def inject_kernel(counts, receiver, misfit, samples, out):
        local_x = receiver[0:1] - (lax.axis_index("gx") * width_x - HALO)
        local_y = receiver[1:2] - (lax.axis_index("gy") * width_y - HALO)
        inside = (local_x >= 0) & (local_x < ext_x) & (local_y >= 0) & (local_y < ext_y)
        live = lax.broadcasted_iota(jnp.int32, (1, slots), 1) < counts[0]
        where = jnp.where(inside & live, local_x * ext_y + local_y, -1)
        cells = ext_x * ext_y
        chosen = lax.broadcasted_iota(jnp.int32, (cells, slots), 0) == where
        level = lax.broadcasted_iota(jnp.int32, (depth, slots), 0) == receiver[2:3]
        level = jnp.where(level, 1.0, 0.0).astype(BF)
        for t in range(steps_total):
            amplitude = misfit[t : t + 1] * samples[t : t + 1]
            head = amplitude.astype(BF).astype(F32)
            result = jnp.zeros((cells, depth), F32)
            for part in (head, amplitude - head):
                spread = jnp.where(chosen, part, 0.0).astype(BF)
                result += lax.dot_general(
                    spread, level, (((1,), (1,)), ((), ())), preferred_element_type=F32
                )
            for g in range(cells // ROWS):
                for b in range(blocks):
                    out[t, pl.ds(g * ROWS * ROWS + b, ROWS, stride=ROWS), :] = result[
                        g * ROWS : (g + 1) * ROWS, b * LANES : (b + 1) * LANES
                    ]

    injected = call(
        inject_kernel,
        struct((steps_total, ext_x * ext_y * ROWS, LANES), F32),
        specs=[pl.BlockSpec(memory_space=pltpu.SMEM)] + [whole] * 3,
        micros=1.6,
    )(pair_counts, receiver_cells.T, residuals.T, samples)

    rim_scratch = [
        VMEM((2, 4 * PER_ROUND) + block, F32),
        VMEM((2, 4 * PER_ROUND) + block, F32),
    ]

    def forward_of(place, columns, first, z_even, z_odd, z_other, x_even, x_odd, rim_y, rim_x):
        from_pair = (lax.axis_index("pair") == 0) == (first == 0)
        for odd, z, x in ((0, z_even, x_even), (1, z_odd, x_odd)):
            side_x = jnp.where(place.plus("gx", odd), 1, 0)
            side_y = jnp.where(place.plus("gy", odd), 1, 0)
            for n in range(4 * PER_ROUND):
                value = x[rim_at + 4 * first + n].astype(F32)
                if odd:
                    value = jnp.where(place.has("gx", odd), value, 0.0)
                rim_x[side_x, n] = value
                own_z = z[pl.ds(rim_z_at + n * width_x, width_x)].astype(F32).reshape(block)
                other = z_other[4 * PER_ROUND * odd + n].astype(F32)
                value = jnp.where(from_pair, own_z, other)
                if odd:
                    value = jnp.where(place.has("gy", odd), value, 0.0)
                rim_y[side_y, n] = value

        def reader(snap):
            base = 4 * (snap - first)

            def column(f, x, y):
                if isinstance(x, int) and x in (-1, width_x):
                    return rim_x[int(x > 0), base + f, column_rows(y, 1), :]
                if y in (-1, width_y):
                    rows = x * ROWS if isinstance(x, int) else pl.multiple_of(x * ROWS, ROWS)
                    return rim_y[int(y > 0), base + f, pl.ds(rows, ROWS), :]
                return columns[base + f, x, column_rows(y, 1), :]

            return column

        return reader

    def run_round(place, number, wind, inject, buffers, state_dz, own_dz, after):
        altitude = Altitude()
        winds = []
        for i in range(3):
            rows = [wind[i : i + 1, b * LANES : (b + 1) * LANES] for b in range(blocks)]
            winds.append(jnp.concatenate(rows, axis=0) * SCALE)
        for s in range(PER_ROUND):
            step = number * PER_ROUND + s
            snap = steps_total - 1 - step
            old, new = buffers[s % 2], buffers[(s + 1) % 2]

            def injected_at(x, y):
                start = (x * ext_y + y) * ROWS
                if not isinstance(start, int):
                    start = pl.multiple_of(start, ROWS)
                return inject[snap, pl.ds(start, ROWS), :]

            radius = 2 * (PER_ROUND - 1 - s) + 1
            advance(
                place,
                altitude,
                old,
                new,
                state_dz,
                winds,
                injected_at,
                radius,
                None if s else own_dz,
                width_x,
                width_y,
            )
            after(altitude, s, snap, new)

    def own(ref, f, x, y, n):
        return ref[f, HALO + x, column_rows(HALO + y, n), :]

    def fill(place, buffer, speed, cols, speed_cols, z_in, x_in, c_in, firsts):
        def store(f, x, y, n, value):
            ref = buffer.at[f] if f < 4 else speed
            ref[x, column_rows(y, n), :] = value

        for f in range(4):
            for x in range(width_x):
                store(f, HALO + x, HALO, width_y, cols[f, x])
        fields = 4
        if speed_cols is not None:
            fields = 5
            for x in range(width_x):
                store(4, HALO + x, HALO, width_y, speed_cols[x])
        place_edges(place, store, fields, width_x, width_y, z_in, x_in, c_in, firsts)

    def first_kernel(wind, inject, cols, own_dz, face_dz, speed_cols, z0, z1, x1, c0, c1, *refs):
        early, late, speed, *faces, here, there, dz_az, dz_p = refs
        place = Place()
        corners_at = (rim_at + forward_fields, 0)
        fill(place, here, speed, cols, speed_cols, (z0, z1), (c0, x1), (c0, c1), corners_at)

        def after(altitude, s, snap, state):
            out = (early, late)[s]
            for f in range(4):
                for x in range(width_x):
                    out[f, x] = own(state, f, x, 0, width_y)

        run_round(place, 0, wind, inject, (here, there), (speed, dz_az, dz_p), (own_dz, face_dz), after)

        def load(f, x, y, n):
            return own(here, f, x, y, n)

        pack_faces(place, load, 4, width_x, width_y, faces[:2], faces[2:])

    first = call(
        first_kernel,
        [struct((4,) + tile, F32)] * 2 + [struct(ext, F32)] + face_structs(4),
        scratch=[VMEM((4,) + ext, F32)] * 2 + [VMEM(ext, F32)] * 2,
        micros=6.0,
        limit=28,
    )(
        wind_profile, injected, cols, own_dz, face_slopes(z_first), speed_cols, *z_first, x_first, hop, hop_odd
    )
    early, late, speed_ext = first[:3]
    z_second, x_second = first_hop(first[3:])

    rim = (*z_first, rim_z, hop, x_first)

    def early_kernel(early, late, columns, slopes, z0, z1, zp, c0, x1, total, rim_y, rim_x):
        place = Place()
        reader = forward_of(place, columns, PER_ROUND, z0, z1, zp, c0, x1, rim_y, rim_x)
        total[...] = jnp.zeros_like(total)
        for s, state in ((0, early), (1, late)):
            add_increment(
                lambda f, x, y: state[f, x, column_rows(y, 1), :],
                reader(steps_total - 1 - s),
                lambda f, x, y: slopes[
                    4 * (steps_total - 1 - s - PER_ROUND) + f, x, column_rows(y, 1), :
                ],
                total,
                width_x,
                width_y,
            )

    total = call(early_kernel, struct((4,) + tile, F32), scratch=rim_scratch, micros=2.3, limit=16)(
        early, late, forward_early, slopes_early, *rim
    )
    late_dz = own_slopes(late)
    z_second, x_second, total, late_dz = lax.optimization_barrier(
        (z_second, x_second, total, late_dz)
    )
    again, again_odd = second_hop(4, z_second, first[5], False)

    half = depth // 2
    half_blocks = blocks // 2

    def second_kernel(
        wind, inject, cols, own_dz, face_dz, speed, total, columns, slopes, *refs
    ):
        rims, (z0, z1, x1, c0, c1), refs = refs[:5], refs[5:10], refs[10:]
        last, mine, other, scales, here, there, dz_az, dz_p, sums, rim_y, rim_x = refs
        place = Place()
        fill(place, here, None, cols, None, (z0, z1), (c0, x1), (c0, c1), (face_start(4, "gx"), 0))
        reader = forward_of(place, columns, 0, *rims, rim_y, rim_x)
        sums[...] = total[...]

        def after(altitude, s, snap, state):
            add_increment(
                lambda f, x, y: own(state, f, x, y, 1),
                reader(snap),
                lambda f, x, y: slopes[4 * snap + f, x, column_rows(y, 1), :],
                sums,
                width_x,
                width_y,
            )

        run_round(place, 1, wind, inject, (here, there), (speed, dz_az, dz_p), (own_dz, face_dz), after)
        me = lax.axis_index("pair")
        for f in range(4):
            for x in range(width_x):
                last[f, x] = own(here, f, x, 0, width_y)

        def sums_at(f, x, part, b):
            return sums[f, x, pl.ds(part * half_blocks + b, width_y, stride=ROWS), :]

        for f in range(4):
            for b in range(half_blocks):
                here_lanes = slice(b * LANES, (b + 1) * LANES)
                largest = jnp.abs(sums_at(f, 0, 1 - me, b))
                for x in range(1, width_x):
                    largest = jnp.maximum(largest, jnp.abs(sums_at(f, x, 1 - me, b)))
                largest = jnp.maximum(jnp.max(largest, axis=0, keepdims=True), 1e-30)
                scales[f : f + 1, here_lanes] = largest * (0.5 / 32767.0)
                inverse = 32767.0 / largest
                for x in range(0, width_x, 2):
                    two = [sums_at(f, x + i, 1 - me, b) * inverse for i in (0, 1)]
                    two = jnp.round(jnp.concatenate(two, axis=0))
                    other[f, x // 2, :, here_lanes] = two.astype(jnp.int32).astype(jnp.int16)
        for f in range(4):
            for x in range(width_x):
                mine[f, x] = sums[f, x]

    kernel_half = struct((4, width_x, width_y, half), F32)
    last, mine, other, scales = call(
        second_kernel,
        [
            struct((4,) + tile, F32),
            struct((4,) + tile, F32),
            struct((4, width_x // 2, 2 * width_y, half), jnp.int16),
            struct((4, half), F32),
        ],
        scratch=[VMEM((4,) + ext, F32)] * 2
        + [VMEM(ext, F32)] * 2
        + [VMEM((4,) + tile, F32)]
        + rim_scratch,
        micros=9.0,
        limit=30,
    )(
        wind_profile,
        injected,
        late,
        late_dz,
        face_slopes(z_second),
        speed_ext,
        total,
        forward_late,
        slopes_late,
        *rim,
        *z_second,
        x_second,
        again,
        again_odd,
    )
    across = [(0, 1), (1, 0)]
    other, scales = lax.ppermute(other, "pair", across), lax.ppermute(scales, "pair", across)

    def final_kernel(last, sums, final, mine):
        me = lax.axis_index("pair")
        for f in range(4):
            for x in range(width_x):
                for b in range(blocks):
                    final[0, f, x, :, b * LANES : (b + 1) * LANES] = last[
                        f, x, pl.ds(b, width_y, stride=ROWS), :
                    ]
                for b in range(half_blocks):
                    mine[f, x, :, b * LANES : (b + 1) * LANES] = (
                        0.5 * sums[f, x, pl.ds(me * half_blocks + b, width_y, stride=ROWS), :]
                    )

    final, mine = call(
        final_kernel, [struct(adjoint_state.shape, F32), kernel_half], micros=1.0, limit=8
    )(last, mine)

    def sum_kernel(mine, other, scales, out):
        for f in range(4):
            for x in range(0, width_x, 2):
                two = other[f, x // 2].astype(jnp.int32).astype(F32) * scales[f : f + 1]
                for i in (0, 1):
                    out[f, x + i] = mine[f, x + i] + two[i * width_y : (i + 1) * width_y]

    kernels = call(sum_kernel, kernel_half, micros=0.8, limit=8)(mine, other, scales)
    return (kernels, final)


def solution(mesh):
    assert mesh.shape["pair"] == 2 and mesh.shape["gx"] % 2 == 0 and mesh.shape["gy"] % 2 == 0
    in_specs = (
        P("gx", "gy", None),
        P(),
        P(None, None, "gx", "gy", None),
        P("pair", None, "gx", "gy", None),
        P("pair"),
        P("pair", None),
        P("pair", None),
        P("pair", None),
    )
    out_specs = (P(None, "gx", "gy", "pair"), P("pair", None, "gx", "gy", None))
    return jax.shard_map(shards, mesh=mesh, in_specs=in_specs, out_specs=out_specs, check_vma=False)
```

```python
import jax
import jax.numpy as jnp
from jax import lax
from jax.experimental import pallas as pl
from jax.experimental.pallas import tpu as pltpu
from jax.sharding import PartitionSpec as P

step_length = 0.25
SCALE = 0.5 * step_length
HALO = 4
PER_ROUND = 2
LANES = 128
ROWS = 8
VMEM = pltpu.VMEM
CORNER = [(i, j) for i in range(1, HALO) for j in range(1, HALO) if i + j <= HALO]
BF = jnp.bfloat16
F32 = jnp.float32


def swap_pairs(size, odd):
    partner = [((i - odd) ^ 1) + odd for i in range(size)]
    return [(i, j if 0 <= j < size else i) for i, j in enumerate(partner)]


def swapped(x, axis, odd):
    return lax.ppermute(x, axis, swap_pairs(lax.axis_size(axis), odd))


def total_of(x, axis):
    size = lax.axis_size(axis)
    parts = [lax.ppermute(x, axis, [(i, (i + k) % size) for i in range(size)]) for k in range(1, size)]
    return sum(parts, x)


def summed(x, axis, k):
    size = lax.axis_size(axis)
    assert size & (size - 1) == 0
    while k < size:
        x = x + lax.ppermute(x, axis, [(i, i ^ k) for i in range(size)])
        k *= 2
    return x


def call(kernel, outs, scratch=(), micros=1.0, specs=None, out_specs=None, limit=16):
    def run(*args):
        return pl.pallas_call(
            kernel,
            out_shape=outs,
            in_specs=specs or [pl.BlockSpec(memory_space=VMEM)] * len(args),
            out_specs=out_specs
            or jax.tree.map(lambda _: pl.BlockSpec(memory_space=VMEM), outs),
            scratch_shapes=list(scratch),
            compiler_params=pltpu.CompilerParams(vmem_limit_bytes=limit * 2**20),
            cost_estimate=pl.CostEstimate(
                flops=int(1.1e9 * micros), bytes_accessed=100_000, transcendentals=0
            ),
        )(*args)

    return run


def struct(shape, dtype):
    return jax.ShapeDtypeStruct(shape, dtype)


class Place:
    def __init__(self):
        self.index = {}
        self.size = {}
        for axis in ("gx", "gy"):
            self.index[axis] = lax.axis_index(axis)
            self.size[axis] = lax.axis_size(axis)

    def plus(self, axis, odd):
        return lax.rem(self.index[axis], 2) == odd

    def has(self, axis, odd):
        i = self.index[axis]
        if not odd:
            return None
        return jnp.logical_and(i > 0, i < self.size[axis] - 1)


def column_rows(y, n):
    start = y * ROWS
    if not isinstance(start, int):
        start = pl.multiple_of(start, ROWS)
    return pl.ds(start, n * ROWS)


def face_depth(f, axis):
    return HALO if f in (0, {"gx": 1, "gy": 2}[axis]) else HALO - 1


def face_start(f, axis):
    return sum(face_depth(g, axis) for g in range(f))


def pack_faces(place, load, fields, width_x, width_y, z_out, x_out):
    for odd in (0, 1):
        for f in range(fields):
            deep = face_depth(f, "gy")
            y0 = jnp.where(place.plus("gy", odd), width_y - deep, 0)
            for x in range(width_x):
                value = load(f, x, y0, deep).reshape(deep, ROWS, LANES)
                at = face_start(f, "gy") * width_x + x * deep
                z_out[odd][pl.ds(at, deep)] = value.astype(BF)
            deep = face_depth(f, "gx")
            x0 = jnp.where(place.plus("gx", odd), width_x - deep, 0)
            for j in range(deep):
                value = load(f, x0 + j, 0, width_y)
                x_out[odd][face_start(f, "gx") + j] = value.astype(BF)


def corner_blocks(fields, width_y):
    return -(-2 * fields * len(CORNER) // width_y)


def corner_place(fields, odd_y, f, k, width_y):
    n = (odd_y * fields + f) * len(CORNER) + k
    return n // width_y, pl.ds(n % width_y * ROWS, 2 * ROWS)


def pack_corners(place, fields, width_x, width_y, z_in, out, first, odd_x):
    plus_x = place.plus("gx", odd_x)
    for odd_y in (0, 1):
        plus_y = place.plus("gy", odd_y)
        for f in range(fields):
            for k in range(0, len(CORNER), 2):
                two = []
                for i, j in CORNER[k : k + 2]:
                    x = jnp.where(plus_x, width_x - i, i - 1)
                    deep = face_depth(f, "gy")
                    y = jnp.where(plus_y, j - 1, deep - j)
                    at = face_start(f, "gy") * width_x + x * deep + y
                    two.append(z_in[odd_y][at].astype(F32))
                block, rows = corner_place(fields, odd_y, f, k, width_y)
                out[first + block, rows, :] = jnp.concatenate(two, axis=0).astype(BF)


def place_edges(place, store, fields, width_x, width_y, z_in, x_in, c_in, firsts):
    def masked(value, *conditions):
        value = value.astype(F32)
        for condition in conditions:
            if condition is not None:
                value = jnp.where(condition, value, 0.0)
        return value

    for odd in (0, 1):
        for f in range(fields):
            deep = face_depth(f, "gy")
            y0 = jnp.where(place.plus("gy", odd), width_y + HALO, HALO - deep)
            for x in range(width_x):
                at = face_start(f, "gy") * width_x + x * deep
                value = masked(z_in[odd][pl.ds(at, deep)], place.has("gy", odd))
                store(f, HALO + x, y0, deep, value.reshape(deep * ROWS, LANES))
            deep = face_depth(f, "gx")
            x0 = jnp.where(place.plus("gx", odd), width_x + HALO, HALO - deep)
            for j in range(deep):
                value = masked(x_in[odd][face_start(f, "gx") + j], place.has("gx", odd))
                store(f, x0 + j, HALO, width_y, value)
    for odd_x in (0, 1):
        plus_x = place.plus("gx", odd_x)
        for odd_y in (0, 1):
            plus_y = place.plus("gy", odd_y)
            for f in range(fields):
                for k in range(0, len(CORNER), 2):
                    block, rows = corner_place(fields, odd_y, f, k, width_y)
                    two = c_in[odd_x][firsts[odd_x] + block, rows, :].astype(F32)
                    two = [two[:ROWS], two[ROWS:]]
                    for value, (i, j) in zip(two, CORNER[k : k + 2]):
                        x = jnp.where(plus_x, HALO + width_x - 1 + i, HALO - i)
                        y = jnp.where(plus_y, HALO + width_y - 1 + j, HALO - j)
                        value = masked(value, place.has("gx", odd_x), place.has("gy", odd_y))
                        store(f, x, y, 1, value)


class Altitude:
    def __init__(self):
        lane = lax.broadcasted_iota(jnp.int32, (ROWS, LANES), 1)
        row = lax.broadcasted_iota(jnp.int32, (ROWS, LANES), 0)
        self.last_lane = lane == LANES - 1
        self.first_lane = lane == 0
        self.last_row = row == ROWS - 1
        self.first_row = row == 0

    def __call__(self, v):
        up = pltpu.roll(v, LANES - 1, 1)
        carried = jnp.where(self.last_row, 0.0, pltpu.roll(up, ROWS - 1, 0))
        up = jnp.where(self.last_lane, carried, up)
        down = pltpu.roll(v, 1, 1)
        carried = jnp.where(self.first_row, 0.0, pltpu.roll(down, 1, 0))
        down = jnp.where(self.first_lane, carried, down)
        return up - down


def over_diamond(radius, width_x, width_y, row, sides):
    def own(i, carry):
        row(HALO + i, HALO - radius, width_y + 2 * radius, None)
        return carry

    lax.fori_loop(0, width_x, own, 0)
    for d in range(1, radius + 1):
        rest = radius - d
        row(HALO - d, HALO - rest, width_y + 2 * rest, sides[0])
        row(HALO + width_x - 1 + d, HALO - rest, width_y + 2 * rest, sides[1])


def advance(
    place, altitude, old, new, state_dz, wind, inject, radius, own_dz, width_x, width_y
):
    east, north, vertical = wind
    speed, dz_az, dz_p = state_dz
    sides = {
        axis: [
            jnp.where(place.index[axis] == edge, 0.0, 1.0) for edge in (0, place.size[axis] - 1)
        ]
        for axis in ("gx", "gy")
    }

    def at(ref, x, y):
        return ref[x, column_rows(y, 1), :]

    def inside(value, kept, y):
        if y < HALO or y >= HALO + width_y:
            side = sides["gy"][int(y > HALO)]
            kept = side if kept is None else kept * side
        return value if kept is None else value * kept

    p, ax, ay, az = (old.at[f] for f in range(4))

    def slope(f, value, x, y, kept):
        if own_dz is None or kept is not None:
            return altitude(value)
        if HALO <= y < HALO + width_y:
            return own_dz[0][f, x - HALO, column_rows(y - HALO, 1), :]
        lower = jnp.where(place.plus("gy", 0), 1, 0)
        if y < HALO:
            return own_dz[1][lower, f, x - HALO, HALO - 1 - y]
        return own_dz[1][1 - lower, f, x - HALO, y - HALO - width_y]

    def p_row(x, y0, n, kept):
        ps = [at(p, x, y0 + k - 1) for k in range(n + 2)]
        ays = [at(ay, x, y0 + k - 1) for k in range(n + 2)]
        for k in range(n):
            y = y0 + k
            up = slope(3, at(az, x, y), x, y, kept)
            dz_az[x, column_rows(y, 1), :] = up
            up_p = at(dz_p, x, y) if own_dz is None else slope(0, ps[k + 1], x, y, kept)
            div = (at(ax, x + 1, y) - at(ax, x - 1, y)) + (ays[k + 2] - ays[k]) + up
            value = (
                at(speed, x, y) * div
                + east * (at(p, x + 1, y) - at(p, x - 1, y))
                + north * (ps[k + 2] - ps[k])
                + vertical * up_p
            )
            value = ps[k + 1] + value + inject(x, y)
            new[0, x, column_rows(y, 1), :] = inside(value, kept, y)

    over_diamond(radius, width_x, width_y, p_row, sides["gx"])
    pn = new.at[0]

    def a_row(x, y0, n, kept):
        ps = [at(pn, x, y0 + k - 1) for k in range(n + 2)]
        away = radius - 1 - (HALO - y0)
        for f, a in ((1, ax), (2, ay), (3, az)):
            if radius == 1:
                deep = 0
            elif f == 1:
                deep = radius - 2 if not away else radius - 1 - away
            elif f == 2:
                deep = radius - 1 - away if away < radius - 1 else -1
            else:
                deep = radius - 2 - away
            if deep < 0:
                continue
            start = HALO - deep - y0
            vs = [at(a, x, y0 + k - 1) for k in range(n + 2)]
            for k in range(start, n - start):
                y = y0 + k
                if f == 1:
                    grad = at(pn, x + 1, y) - at(pn, x - 1, y)
                elif f == 2:
                    grad = ps[k + 2] - ps[k]
                else:
                    grad = altitude(ps[k + 1])
                    if radius > 1:
                        dz_p[x, column_rows(y, 1), :] = grad
                up = at(dz_az, x, y) if f == 3 else slope(f, vs[k + 1], x, y, kept)
                value = (
                    SCALE * grad
                    + east * (at(a, x + 1, y) - at(a, x - 1, y))
                    + north * (vs[k + 2] - vs[k])
                    + vertical * up
                )
                new[f, x, column_rows(y, 1), :] = inside(vs[k + 1] + value, kept, y)

    over_diamond(radius - 1, width_x, width_y, a_row, sides["gx"])


def add_increment(state, forward, forward_dz, total, width_x, width_y):
    def row(i):
        for k in range(width_y):
            p, ax, ay, az = (state(f, i, k) for f in range(4))
            dx = [forward(f, i + 1, k) - forward(f, i - 1, k) for f in range(4)]
            dy = [forward(f, i, k + 1) - forward(f, i, k - 1) for f in range(4)]
            dz = [forward_dz(f, i, k) for f in range(4)]
            rows = column_rows(k, 1)
            total[0, i, rows, :] += p * (dx[1] + dy[2] + dz[3])
            for n, d in ((1, dx), (2, dy), (3, dz)):
                total[n, i, rows, :] += p * d[0] + ax * d[1] + ay * d[2] + az * d[3]

    def inner(i, carry):
        row(i)
        return carry

    row(0)
    lax.fori_loop(1, width_x - 1, inner, 0)
    row(width_x - 1)


def shards(
    sound_speed_sq,
    wind_profile,
    forward_field,
    adjoint_state,
    pair_counts,
    source_cells,
    receiver_cells,
    residuals,
):
    steps_total = forward_field.shape[0]
    width_x, width_y, depth = sound_speed_sq.shape
    slots = residuals.shape[0]
    ext_x, ext_y = width_x + 2 * HALO, width_y + 2 * HALO
    blocks = depth // LANES
    assert blocks == ROWS and steps_total == 2 * PER_ROUND and slots % (2 * LANES) == 0 and slots <= 8 * LANES
    assert width_x == width_y and width_x % 2 == 0
    tile = (width_x, width_y * ROWS, LANES)
    ext = (ext_x, ext_y * ROWS, LANES)
    block = (width_y * ROWS, LANES)
    forward_fields = 4 * steps_total

    def face_structs(fields, more=0):
        columns = face_start(fields, "gy") + more // 2
        z = struct((columns * width_x, ROWS, LANES), BF)
        x = [struct((face_start(fields, "gx") + more,) + block, BF)] * 2
        return [z, z, *x]

    def first_hop(faces):
        z_even, z_odd, _, x_odd = faces
        z = [swapped(z_even, "gy", 0), swapped(z_odd, "gy", 1)]
        return z, swapped(x_odd, "gx", 1)

    def second_hop(fields, z, faces, first):
        ahead = faces.shape[0]
        corners = corner_blocks(fields, width_y)

        def corner_kernel(z_even, z_odd, faces, even, odd, *rim):
            place = Place()
            even[:ahead] = faces[...]
            z = (z_even, z_odd)
            pack_corners(place, fields, width_x, width_y, z, even, ahead, 0)
            pack_corners(place, fields, width_x, width_y, z, odd, 0, 1)
            for out in rim:
                for odd_y, ref in enumerate(z):
                    for n in range(4 * PER_ROUND):
                        value = ref[pl.ds(rim_z_at + n * width_x, width_x)].reshape(block)
                        out[4 * PER_ROUND * odd_y + n] = value

        outs = [struct((n + corners,) + block, BF) for n in (ahead, 0)]
        if first:
            outs.append(struct((8 * PER_ROUND,) + block, BF))
        even, odd, *rim = call(corner_kernel, outs, micros=0.3, limit=8)(*z, faces)
        return [swapped(even, "gx", 0), swapped(odd, "gx", 1), *rim]

    whole = pl.BlockSpec(memory_space=VMEM)
    remain = pl.BlockSpec(memory_space=pltpu.HBM)

    def sample_kernel(source, forward, sample, pressure, done):
        copy = pltpu.make_async_copy(forward.at[:, 0], pressure, done)
        copy.start()
        local_x = source[0:1] - lax.axis_index("gx") * width_x
        local_y = source[1:2] - lax.axis_index("gy") * width_y
        inside = (local_x >= 0) & (local_x < width_x) & (local_y >= 0) & (local_y < width_y)
        where = jnp.where(inside, local_x * width_y + local_y, -1)
        cells = width_x * width_y
        chosen = lax.broadcasted_iota(jnp.int32, (cells, slots), 0) == where
        chosen = jnp.where(chosen, 1.0, 0.0).astype(BF)
        level = lax.broadcasted_iota(jnp.int32, (depth, slots), 0) == source[2:3]
        row = lax.broadcasted_iota(jnp.int32, (ROWS, slots), 0)
        result = jnp.zeros((ROWS, slots), F32)
        copy.wait()
        for t in range(steps_total):
            columns = lax.dot_general(
                pressure[t].reshape(cells, depth),
                chosen,
                (((0,), (0,)), ((), ())),
                preferred_element_type=F32,
            )
            picked = jnp.sum(jnp.where(level, columns, 0.0), axis=0, keepdims=True)
            result = jnp.where(row == t, picked, result)
        sample[...] = result

    samples = call(
        sample_kernel,
        struct((ROWS, slots), F32),
        scratch=[VMEM((steps_total, width_x, width_y, depth), BF), pltpu.SemaphoreType.DMA],
        specs=[whole, remain],
        micros=1.5,
        limit=8,
    )(source_cells.T, forward_field)
    state, samples = lax.optimization_barrier((adjoint_state, samples))
    samples = total_of(samples, "gx")

    def pack_kernel(state, speed, forward, cols, speed_cols, early, late, *outs):
        place = Place()
        for x in range(width_x):
            for b in range(blocks):
                at = pl.ds(b, width_y, stride=ROWS)
                here = slice(b * LANES, (b + 1) * LANES)
                for f in range(4):
                    cols[f, x, at, :] = state[0, f, x, :, here]
                speed_cols[x, at, :] = speed[x, :, here] * SCALE

        def load(f, x, y, n):
            ref = cols.at[f] if f < 4 else speed_cols
            return ref[x, column_rows(y, n), :]

        pack_faces(place, load, 5, width_x, width_y, outs[:2], outs[2:])

        mine_is_late = lax.axis_index("pair") == 0

        def one(n, carry):
            t, f = n // 4, lax.rem(n, 4)
            for is_late, ref, snap in ((True, late, t), (False, early, t + PER_ROUND)):
                number = snap * 4 + f
                for x in range(width_x):
                    for b in range(blocks):
                        ref[n, x, pl.ds(b, width_y, stride=ROWS), :] = forward[
                            snap, f, x, :, b * LANES : (b + 1) * LANES
                        ].astype(F32)
                for odd in (0, 1):
                    y = jnp.where(place.plus("gy", odd), width_y - 1, 0)
                    x = jnp.where(place.plus("gx", odd), width_x - 1, 0)
                    outs[2 + odd][rim_at + number] = ref[n, x].astype(BF)
                    value = ref[n, :, column_rows(y, 1), :].astype(BF)
                    to = rim_z_at + n * width_x

                    @pl.when(mine_is_late if is_late else jnp.logical_not(mine_is_late))
                    def _():
                        outs[odd][pl.ds(to, width_x)] = value

            return carry

        lax.fori_loop(0, 4 * PER_ROUND, one, 0)

    rim_z_at, rim_at = face_start(5, "gy") * width_x, face_start(5, "gx")
    packed = call(
        pack_kernel,
        [struct((4,) + tile, F32), struct(tile, F32)]
        + [struct((4 * PER_ROUND,) + tile, F32)] * 2
        + face_structs(5, forward_fields),
        micros=1.3,
        limit=12,
    )(state, sound_speed_sq, forward_field)
    cols, speed_cols, forward_early, forward_late = packed[:4]
    faces = packed[4:]
    z_first, x_first = first_hop(faces)

    def own_slopes(cols):
        def kernel(cols, out):
            altitude = Altitude()

            def one(f, carry):
                for x in range(width_x):
                    for y in range(width_y):
                        rows = column_rows(y, 1)
                        out[f, x, rows, :] = altitude(cols[f, x, rows, :])
                return carry

            lax.fori_loop(0, 4, one, 0)

        return call(kernel, struct((4,) + tile, F32), micros=0.8, limit=8)(cols)

    own_dz = own_slopes(cols)

    def face_slopes(z):
        def kernel(z_even, z_odd, out):
            place, altitude = Place(), Altitude()

            def one(x, carry):
                for odd, ref in enumerate((z_even, z_odd)):
                    plus = place.plus("gy", odd)
                    for f, reach in enumerate((HALO - 1, 1, HALO - 2, HALO - 1)):
                        deep = face_depth(f, "gy")
                        for d in range(reach):
                            at = face_start(f, "gy") * width_x + x * deep
                            at += jnp.where(plus, d, deep - 1 - d)
                            out[odd, f, x, d] = altitude(ref[at].astype(F32))
                return carry

            lax.fori_loop(0, width_x, one, 0)

        out = struct((2, 4, width_x, HALO - 1, ROWS, LANES), F32)
        return call(kernel, out, micros=0.6, limit=8)(*z)

    def slope_kernel(early, late, sample, *outs):
        *outs, held = outs
        held[...] = sample[...]
        altitude = Altitude()

        def one(n, carry):
            for ref, out in zip((early, late), outs):
                for x in range(width_x):
                    for y in range(width_y):
                        rows = column_rows(y, 1)
                        out[n, x, rows, :] = altitude(ref[n, x, rows, :])
            return carry

        lax.fori_loop(0, 4 * PER_ROUND, one, 0)

    slopes_early, slopes_late, samples = call(
        slope_kernel,
        [struct((4 * PER_ROUND,) + tile, F32)] * 2 + [struct(samples.shape, F32)],
        micros=2.7,
        limit=8,
    )(forward_early, forward_late, samples)
    samples = total_of(samples, "gy")

    z_first, x_first, samples, slopes_early, slopes_late, own_dz = lax.optimization_barrier(
        (z_first, x_first, samples, slopes_early, slopes_late, own_dz)
    )
    hop, hop_odd, rim_z = second_hop(5, z_first, faces[2], True)

    def inject_kernel(counts, receiver, misfit, samples, out):
        local_x = receiver[0:1] - (lax.axis_index("gx") * width_x - HALO)
        local_y = receiver[1:2] - (lax.axis_index("gy") * width_y - HALO)
        inside = (local_x >= 0) & (local_x < ext_x) & (local_y >= 0) & (local_y < ext_y)
        live = lax.broadcasted_iota(jnp.int32, (1, slots), 1) < counts[0]
        where = jnp.where(inside & live, local_x * ext_y + local_y, -1)
        cells = ext_x * ext_y
        chosen = lax.broadcasted_iota(jnp.int32, (cells, slots), 0) == where
        level = lax.broadcasted_iota(jnp.int32, (depth, slots), 0) == receiver[2:3]
        level = jnp.where(level, 1.0, 0.0).astype(BF)
        for t in range(steps_total):
            amplitude = misfit[t : t + 1] * samples[t : t + 1]
            head = amplitude.astype(BF).astype(F32)
            result = jnp.zeros((cells, depth), F32)
            for part in (head, amplitude - head):
                spread = jnp.where(chosen, part, 0.0).astype(BF)
                result += lax.dot_general(
                    spread, level, (((1,), (1,)), ((), ())), preferred_element_type=F32
                )
            for g in range(cells // ROWS):
                for b in range(blocks):
                    out[t, pl.ds(g * ROWS * ROWS + b, ROWS, stride=ROWS), :] = result[
                        g * ROWS : (g + 1) * ROWS, b * LANES : (b + 1) * LANES
                    ]

    injected = call(
        inject_kernel,
        struct((steps_total, ext_x * ext_y * ROWS, LANES), F32),
        specs=[pl.BlockSpec(memory_space=pltpu.SMEM)] + [whole] * 3,
        micros=1.6,
    )(pair_counts, receiver_cells.T, residuals.T, samples)

    rim_scratch = [
        VMEM((2, 4 * PER_ROUND) + block, F32),
        VMEM((2, 4 * PER_ROUND) + block, F32),
    ]

    def forward_of(place, columns, first, z_even, z_odd, z_other, x_even, x_odd, rim_y, rim_x):
        from_pair = (lax.axis_index("pair") == 0) == (first == 0)
        for odd, z, x in ((0, z_even, x_even), (1, z_odd, x_odd)):
            side_x = jnp.where(place.plus("gx", odd), 1, 0)
            side_y = jnp.where(place.plus("gy", odd), 1, 0)
            for n in range(4 * PER_ROUND):
                value = x[rim_at + 4 * first + n].astype(F32)
                if odd:
                    value = jnp.where(place.has("gx", odd), value, 0.0)
                rim_x[side_x, n] = value
                own_z = z[pl.ds(rim_z_at + n * width_x, width_x)].astype(F32).reshape(block)
                other = z_other[4 * PER_ROUND * odd + n].astype(F32)
                value = jnp.where(from_pair, own_z, other)
                if odd:
                    value = jnp.where(place.has("gy", odd), value, 0.0)
                rim_y[side_y, n] = value

        def reader(snap):
            base = 4 * (snap - first)

            def column(f, x, y):
                if isinstance(x, int) and x in (-1, width_x):
                    return rim_x[int(x > 0), base + f, column_rows(y, 1), :]
                if y in (-1, width_y):
                    rows = x * ROWS if isinstance(x, int) else pl.multiple_of(x * ROWS, ROWS)
                    return rim_y[int(y > 0), base + f, pl.ds(rows, ROWS), :]
                return columns[base + f, x, column_rows(y, 1), :]

            return column

        return reader

    def run_round(place, number, wind, inject, buffers, state_dz, own_dz, after):
        altitude = Altitude()
        winds = []
        for i in range(3):
            rows = [wind[i : i + 1, b * LANES : (b + 1) * LANES] for b in range(blocks)]
            winds.append(jnp.concatenate(rows, axis=0) * SCALE)
        for s in range(PER_ROUND):
            step = number * PER_ROUND + s
            snap = steps_total - 1 - step
            old, new = buffers[s % 2], buffers[(s + 1) % 2]

            def injected_at(x, y):
                start = (x * ext_y + y) * ROWS
                if not isinstance(start, int):
                    start = pl.multiple_of(start, ROWS)
                return inject[snap, pl.ds(start, ROWS), :]

            radius = 2 * (PER_ROUND - 1 - s) + 1
            advance(
                place,
                altitude,
                old,
                new,
                state_dz,
                winds,
                injected_at,
                radius,
                None if s else own_dz,
                width_x,
                width_y,
            )
            after(altitude, s, snap, new)

    def own(ref, f, x, y, n):
        return ref[f, HALO + x, column_rows(HALO + y, n), :]

    def fill(place, buffer, speed, cols, speed_cols, z_in, x_in, c_in, firsts):
        def store(f, x, y, n, value):
            ref = buffer.at[f] if f < 4 else speed
            ref[x, column_rows(y, n), :] = value

        for f in range(4):
            for x in range(width_x):
                store(f, HALO + x, HALO, width_y, cols[f, x])
        fields = 4
        if speed_cols is not None:
            fields = 5
            for x in range(width_x):
                store(4, HALO + x, HALO, width_y, speed_cols[x])
        place_edges(place, store, fields, width_x, width_y, z_in, x_in, c_in, firsts)

    def first_kernel(wind, inject, cols, own_dz, face_dz, speed_cols, z0, z1, x1, c0, c1, *refs):
        early, late, speed, *faces, here, there, dz_az, dz_p = refs
        place = Place()
        corners_at = (rim_at + forward_fields, 0)
        fill(place, here, speed, cols, speed_cols, (z0, z1), (c0, x1), (c0, c1), corners_at)

        def after(altitude, s, snap, state):
            out = (early, late)[s]
            for f in range(4):
                for x in range(width_x):
                    out[f, x] = own(state, f, x, 0, width_y)

        run_round(place, 0, wind, inject, (here, there), (speed, dz_az, dz_p), (own_dz, face_dz), after)

        def load(f, x, y, n):
            return own(here, f, x, y, n)

        pack_faces(place, load, 4, width_x, width_y, faces[:2], faces[2:])

    first = call(
        first_kernel,
        [struct((4,) + tile, F32)] * 2 + [struct(ext, F32)] + face_structs(4),
        scratch=[VMEM((4,) + ext, F32)] * 2 + [VMEM(ext, F32)] * 2,
        micros=6.0,
        limit=28,
    )(
        wind_profile, injected, cols, own_dz, face_slopes(z_first), speed_cols, *z_first, x_first, hop, hop_odd
    )
    early, late, speed_ext = first[:3]
    z_second, x_second = first_hop(first[3:])

    late_dz = own_slopes(late)
    rim_z, late_dz = lax.optimization_barrier((rim_z, late_dz))
    rim_z = lax.ppermute(rim_z, "pair", [(0, 1), (1, 0)])
    rim = (*z_first, rim_z, hop, x_first)

    def early_kernel(early, late, columns, slopes, z0, z1, zp, c0, x1, total, rim_y, rim_x):
        place = Place()
        reader = forward_of(place, columns, PER_ROUND, z0, z1, zp, c0, x1, rim_y, rim_x)
        total[...] = jnp.zeros_like(total)
        for s, state in ((0, early), (1, late)):
            add_increment(
                lambda f, x, y: state[f, x, column_rows(y, 1), :],
                reader(steps_total - 1 - s),
                lambda f, x, y: slopes[
                    4 * (steps_total - 1 - s - PER_ROUND) + f, x, column_rows(y, 1), :
                ],
                total,
                width_x,
                width_y,
            )

    total = call(early_kernel, struct((4,) + tile, F32), scratch=rim_scratch, micros=2.3, limit=16)(
        early, late, forward_early, slopes_early, *rim
    )
    z_second, x_second, late_dz = lax.optimization_barrier((z_second, x_second, late_dz))
    again, again_odd = second_hop(4, z_second, first[5], False)

    half = depth // 2
    half_blocks = blocks // 2

    def second_kernel(
        wind, inject, cols, own_dz, face_dz, speed, total, columns, slopes, *refs
    ):
        rims, (z0, z1, x1, c0, c1), refs = refs[:5], refs[5:10], refs[10:]
        last, mine, other, scales, here, there, dz_az, dz_p, sums, rim_y, rim_x = refs
        place = Place()
        fill(place, here, None, cols, None, (z0, z1), (c0, x1), (c0, c1), (face_start(4, "gx"), 0))
        reader = forward_of(place, columns, 0, *rims, rim_y, rim_x)
        sums[...] = total[...]

        def after(altitude, s, snap, state):
            add_increment(
                lambda f, x, y: own(state, f, x, y, 1),
                reader(snap),
                lambda f, x, y: slopes[4 * snap + f, x, column_rows(y, 1), :],
                sums,
                width_x,
                width_y,
            )

        run_round(place, 1, wind, inject, (here, there), (speed, dz_az, dz_p), (own_dz, face_dz), after)
        me = lax.axis_index("pair")
        for f in range(4):
            for x in range(width_x):
                last[f, x] = own(here, f, x, 0, width_y)

        def sums_at(f, x, part, b):
            return sums[f, x, pl.ds(part * half_blocks + b, width_y, stride=ROWS), :]

        for f in range(4):
            for b in range(half_blocks):
                here_lanes = slice(b * LANES, (b + 1) * LANES)
                largest = jnp.abs(sums_at(f, 0, 1 - me, b))
                for x in range(1, width_x):
                    largest = jnp.maximum(largest, jnp.abs(sums_at(f, x, 1 - me, b)))
                largest = jnp.maximum(jnp.max(largest, axis=0, keepdims=True), 1e-30)
                scales[f : f + 1, here_lanes] = largest * (0.5 / 32767.0)
                inverse = 32767.0 / largest
                for x in range(0, width_x, 2):
                    two = [sums_at(f, x + i, 1 - me, b) * inverse for i in (0, 1)]
                    two = jnp.round(jnp.concatenate(two, axis=0))
                    other[f, x // 2, :, here_lanes] = two.astype(jnp.int32).astype(jnp.int16)
        for f in range(4):
            for x in range(width_x):
                mine[f, x] = sums[f, x]

    kernel_half = struct((4, width_x, width_y, half), F32)
    last, mine, other, scales = call(
        second_kernel,
        [
            struct((4,) + tile, F32),
            struct((4,) + tile, F32),
            struct((4, width_x // 2, 2 * width_y, half), jnp.int16),
            struct((4, half), F32),
        ],
        scratch=[VMEM((4,) + ext, F32)] * 2
        + [VMEM(ext, F32)] * 2
        + [VMEM((4,) + tile, F32)]
        + rim_scratch,
        micros=9.0,
        limit=30,
    )(
        wind_profile,
        injected,
        late,
        late_dz,
        face_slopes(z_second),
        speed_ext,
        total,
        forward_late,
        slopes_late,
        *rim,
        *z_second,
        x_second,
        again,
        again_odd,
    )
    across = [(0, 1), (1, 0)]
    other, scales = lax.ppermute(other, "pair", across), lax.ppermute(scales, "pair", across)

    def final_kernel(last, sums, final, mine):
        me = lax.axis_index("pair")
        for f in range(4):
            for x in range(width_x):
                for b in range(blocks):
                    final[0, f, x, :, b * LANES : (b + 1) * LANES] = last[
                        f, x, pl.ds(b, width_y, stride=ROWS), :
                    ]
                for b in range(half_blocks):
                    mine[f, x, :, b * LANES : (b + 1) * LANES] = (
                        0.5 * sums[f, x, pl.ds(me * half_blocks + b, width_y, stride=ROWS), :]
                    )

    final, mine = call(
        final_kernel, [struct(adjoint_state.shape, F32), kernel_half], micros=1.0, limit=8
    )(last, mine)

    def sum_kernel(mine, other, scales, out):
        for f in range(4):
            for x in range(0, width_x, 2):
                two = other[f, x // 2].astype(jnp.int32).astype(F32) * scales[f : f + 1]
                for i in (0, 1):
                    out[f, x + i] = mine[f, x + i] + two[i * width_y : (i + 1) * width_y]

    kernels = call(sum_kernel, kernel_half, micros=0.8, limit=8)(mine, other, scales)
    return (kernels, final)


def solution(mesh):
    assert mesh.shape["pair"] == 2 and mesh.shape["gx"] % 2 == 0 and mesh.shape["gy"] % 2 == 0
    in_specs = (
        P("gx", "gy", None),
        P(),
        P(None, None, "gx", "gy", None),
        P("pair", None, "gx", "gy", None),
        P("pair"),
        P("pair", None),
        P("pair", None),
        P("pair", None),
    )
    out_specs = (P(None, "gx", "gy", "pair"), P("pair", None, "gx", "gy", None))
    return jax.shard_map(shards, mesh=mesh, in_specs=in_specs, out_specs=out_specs, check_vma=False)
```

```python
import jax
import jax.numpy as jnp
from jax import lax
from jax.experimental import pallas as pl
from jax.experimental.pallas import tpu as pltpu
from jax.sharding import PartitionSpec as P

step_length = 0.25
SCALE = 0.5 * step_length
HALO = 4
PER_ROUND = 2
LANES = 128
ROWS = 8
VMEM = pltpu.VMEM
CORNER = [(i, j) for i in range(1, HALO) for j in range(1, HALO) if i + j <= HALO]
BF = jnp.bfloat16
F32 = jnp.float32


def swap_pairs(size, odd):
    partner = [((i - odd) ^ 1) + odd for i in range(size)]
    return [(i, j if 0 <= j < size else i) for i, j in enumerate(partner)]


def swapped(x, axis, odd):
    return lax.ppermute(x, axis, swap_pairs(lax.axis_size(axis), odd))


def total_of(x, axis):
    size = lax.axis_size(axis)
    parts = [lax.ppermute(x, axis, [(i, (i + k) % size) for i in range(size)]) for k in range(1, size)]
    return sum(parts, x)


def summed(x, axis, k):
    size = lax.axis_size(axis)
    assert size & (size - 1) == 0
    while k < size:
        x = x + lax.ppermute(x, axis, [(i, i ^ k) for i in range(size)])
        k *= 2
    return x


def call(kernel, outs, scratch=(), micros=1.0, specs=None, out_specs=None, limit=16):
    def run(*args):
        return pl.pallas_call(
            kernel,
            out_shape=outs,
            in_specs=specs or [pl.BlockSpec(memory_space=VMEM)] * len(args),
            out_specs=out_specs
            or jax.tree.map(lambda _: pl.BlockSpec(memory_space=VMEM), outs),
            scratch_shapes=list(scratch),
            compiler_params=pltpu.CompilerParams(vmem_limit_bytes=limit * 2**20),
            cost_estimate=pl.CostEstimate(
                flops=int(1.1e9 * micros), bytes_accessed=100_000, transcendentals=0
            ),
        )(*args)

    return run


def struct(shape, dtype):
    return jax.ShapeDtypeStruct(shape, dtype)


class Place:
    def __init__(self):
        self.index = {}
        self.size = {}
        for axis in ("gx", "gy"):
            self.index[axis] = lax.axis_index(axis)
            self.size[axis] = lax.axis_size(axis)

    def plus(self, axis, odd):
        return lax.rem(self.index[axis], 2) == odd

    def has(self, axis, odd):
        i = self.index[axis]
        if not odd:
            return None
        return jnp.logical_and(i > 0, i < self.size[axis] - 1)


def column_rows(y, n):
    start = y * ROWS
    if not isinstance(start, int):
        start = pl.multiple_of(start, ROWS)
    return pl.ds(start, n * ROWS)


def face_depth(f, axis):
    return HALO if f in (0, {"gx": 1, "gy": 2}[axis]) else HALO - 1


def face_start(f, axis):
    return sum(face_depth(g, axis) for g in range(f))


def pack_faces(place, load, fields, width_x, width_y, z_out, x_out):
    for odd in (0, 1):
        for f in range(fields):
            deep = face_depth(f, "gy")
            y0 = jnp.where(place.plus("gy", odd), width_y - deep, 0)
            for x in range(width_x):
                value = load(f, x, y0, deep).reshape(deep, ROWS, LANES)
                at = face_start(f, "gy") * width_x + x * deep
                z_out[odd][pl.ds(at, deep)] = value.astype(BF)
            deep = face_depth(f, "gx")
            x0 = jnp.where(place.plus("gx", odd), width_x - deep, 0)
            for j in range(deep):
                value = load(f, x0 + j, 0, width_y)
                x_out[odd][face_start(f, "gx") + j] = value.astype(BF)


def corner_blocks(fields, width_y):
    return -(-2 * fields * len(CORNER) // width_y)


def corner_place(fields, odd_y, f, k, width_y):
    n = (odd_y * fields + f) * len(CORNER) + k
    return n // width_y, pl.ds(n % width_y * ROWS, 2 * ROWS)


def pack_corners(place, fields, width_x, width_y, z_in, out, first, odd_x):
    plus_x = place.plus("gx", odd_x)
    for odd_y in (0, 1):
        plus_y = place.plus("gy", odd_y)
        for f in range(fields):
            for k in range(0, len(CORNER), 2):
                two = []
                for i, j in CORNER[k : k + 2]:
                    x = jnp.where(plus_x, width_x - i, i - 1)
                    deep = face_depth(f, "gy")
                    y = jnp.where(plus_y, j - 1, deep - j)
                    at = face_start(f, "gy") * width_x + x * deep + y
                    two.append(z_in[odd_y][at].astype(F32))
                block, rows = corner_place(fields, odd_y, f, k, width_y)
                out[first + block, rows, :] = jnp.concatenate(two, axis=0).astype(BF)


def place_edges(place, store, fields, width_x, width_y, z_in, x_in, c_in, firsts):
    def masked(value, *conditions):
        value = value.astype(F32)
        for condition in conditions:
            if condition is not None:
                value = jnp.where(condition, value, 0.0)
        return value

    for odd in (0, 1):
        for f in range(fields):
            deep = face_depth(f, "gy")
            y0 = jnp.where(place.plus("gy", odd), width_y + HALO, HALO - deep)
            for x in range(width_x):
                at = face_start(f, "gy") * width_x + x * deep
                value = masked(z_in[odd][pl.ds(at, deep)], place.has("gy", odd))
                store(f, HALO + x, y0, deep, value.reshape(deep * ROWS, LANES))
            deep = face_depth(f, "gx")
            x0 = jnp.where(place.plus("gx", odd), width_x + HALO, HALO - deep)
            for j in range(deep):
                value = masked(x_in[odd][face_start(f, "gx") + j], place.has("gx", odd))
                store(f, x0 + j, HALO, width_y, value)
    for odd_x in (0, 1):
        plus_x = place.plus("gx", odd_x)
        for odd_y in (0, 1):
            plus_y = place.plus("gy", odd_y)
            for f in range(fields):
                for k in range(0, len(CORNER), 2):
                    block, rows = corner_place(fields, odd_y, f, k, width_y)
                    two = c_in[odd_x][firsts[odd_x] + block, rows, :].astype(F32)
                    two = [two[:ROWS], two[ROWS:]]
                    for value, (i, j) in zip(two, CORNER[k : k + 2]):
                        x = jnp.where(plus_x, HALO + width_x - 1 + i, HALO - i)
                        y = jnp.where(plus_y, HALO + width_y - 1 + j, HALO - j)
                        value = masked(value, place.has("gx", odd_x), place.has("gy", odd_y))
                        store(f, x, y, 1, value)


class Altitude:
    def __init__(self):
        lane = lax.broadcasted_iota(jnp.int32, (ROWS, LANES), 1)
        row = lax.broadcasted_iota(jnp.int32, (ROWS, LANES), 0)
        self.last_lane = lane == LANES - 1
        self.first_lane = lane == 0
        self.last_row = row == ROWS - 1
        self.first_row = row == 0

    def __call__(self, v):
        up = pltpu.roll(v, LANES - 1, 1)
        carried = jnp.where(self.last_row, 0.0, pltpu.roll(up, ROWS - 1, 0))
        up = jnp.where(self.last_lane, carried, up)
        down = pltpu.roll(v, 1, 1)
        carried = jnp.where(self.first_row, 0.0, pltpu.roll(down, 1, 0))
        down = jnp.where(self.first_lane, carried, down)
        return up - down


def over_diamond(radius, width_x, width_y, row, sides):
    def own(i, carry):
        row(HALO + i, HALO - radius, width_y + 2 * radius, None)
        return carry

    lax.fori_loop(0, width_x, own, 0)
    for d in range(1, radius + 1):
        rest = radius - d
        row(HALO - d, HALO - rest, width_y + 2 * rest, sides[0])
        row(HALO + width_x - 1 + d, HALO - rest, width_y + 2 * rest, sides[1])


def advance(
    place, altitude, old, new, state_dz, wind, inject, radius, own_dz, width_x, width_y
):
    east, north, vertical = wind
    speed, dz_az, dz_p = state_dz
    sides = {
        axis: [
            jnp.where(place.index[axis] == edge, 0.0, 1.0) for edge in (0, place.size[axis] - 1)
        ]
        for axis in ("gx", "gy")
    }

    def at(ref, x, y):
        return ref[x, column_rows(y, 1), :]

    def inside(value, kept, y):
        if y < HALO or y >= HALO + width_y:
            side = sides["gy"][int(y > HALO)]
            kept = side if kept is None else kept * side
        return value if kept is None else value * kept

    p, ax, ay, az = (old.at[f] for f in range(4))

    def slope(f, value, x, y, kept):
        if own_dz is None or kept is not None:
            return altitude(value)
        if HALO <= y < HALO + width_y:
            return own_dz[0][f, x - HALO, column_rows(y - HALO, 1), :]
        lower = jnp.where(place.plus("gy", 0), 1, 0)
        if y < HALO:
            return own_dz[1][lower, f, x - HALO, HALO - 1 - y]
        return own_dz[1][1 - lower, f, x - HALO, y - HALO - width_y]

    def p_row(x, y0, n, kept):
        ps = [at(p, x, y0 + k - 1) for k in range(n + 2)]
        ays = [at(ay, x, y0 + k - 1) for k in range(n + 2)]
        for k in range(n):
            y = y0 + k
            up = slope(3, at(az, x, y), x, y, kept)
            dz_az[x, column_rows(y, 1), :] = up
            up_p = at(dz_p, x, y) if own_dz is None else slope(0, ps[k + 1], x, y, kept)
            div = (at(ax, x + 1, y) - at(ax, x - 1, y)) + (ays[k + 2] - ays[k]) + up
            value = (
                at(speed, x, y) * div
                + east * (at(p, x + 1, y) - at(p, x - 1, y))
                + north * (ps[k + 2] - ps[k])
                + vertical * up_p
            )
            value = ps[k + 1] + value + inject(x, y)
            new[0, x, column_rows(y, 1), :] = inside(value, kept, y)

    over_diamond(radius, width_x, width_y, p_row, sides["gx"])
    pn = new.at[0]

    def a_row(x, y0, n, kept):
        ps = [at(pn, x, y0 + k - 1) for k in range(n + 2)]
        away = radius - 1 - (HALO - y0)
        for f, a in ((1, ax), (2, ay), (3, az)):
            if radius == 1:
                deep = 0
            elif f == 1:
                deep = radius - 2 if not away else radius - 1 - away
            elif f == 2:
                deep = radius - 1 - away if away < radius - 1 else -1
            else:
                deep = radius - 2 - away
            if deep < 0:
                continue
            start = HALO - deep - y0
            vs = [at(a, x, y0 + k - 1) for k in range(n + 2)]
            for k in range(start, n - start):
                y = y0 + k
                if f == 1:
                    grad = at(pn, x + 1, y) - at(pn, x - 1, y)
                elif f == 2:
                    grad = ps[k + 2] - ps[k]
                else:
                    grad = altitude(ps[k + 1])
                    if radius > 1:
                        dz_p[x, column_rows(y, 1), :] = grad
                up = at(dz_az, x, y) if f == 3 else slope(f, vs[k + 1], x, y, kept)
                value = (
                    SCALE * grad
                    + east * (at(a, x + 1, y) - at(a, x - 1, y))
                    + north * (vs[k + 2] - vs[k])
                    + vertical * up
                )
                new[f, x, column_rows(y, 1), :] = inside(vs[k + 1] + value, kept, y)

    over_diamond(radius - 1, width_x, width_y, a_row, sides["gx"])


def add_increment(state, forward, forward_dz, total, width_x, width_y):
    def row(i):
        for k in range(width_y):
            p, ax, ay, az = (state(f, i, k) for f in range(4))
            dx = [forward(f, i + 1, k) - forward(f, i - 1, k) for f in range(4)]
            dy = [forward(f, i, k + 1) - forward(f, i, k - 1) for f in range(4)]
            dz = [forward_dz(f, i, k) for f in range(4)]
            rows = column_rows(k, 1)
            total[0, i, rows, :] += p * (dx[1] + dy[2] + dz[3])
            for n, d in ((1, dx), (2, dy), (3, dz)):
                total[n, i, rows, :] += p * d[0] + ax * d[1] + ay * d[2] + az * d[3]

    def inner(i, carry):
        row(i)
        return carry

    row(0)
    lax.fori_loop(1, width_x - 1, inner, 0)
    row(width_x - 1)


def shards(
    sound_speed_sq,
    wind_profile,
    forward_field,
    adjoint_state,
    pair_counts,
    source_cells,
    receiver_cells,
    residuals,
):
    steps_total = forward_field.shape[0]
    width_x, width_y, depth = sound_speed_sq.shape
    slots = residuals.shape[0]
    ext_x, ext_y = width_x + 2 * HALO, width_y + 2 * HALO
    blocks = depth // LANES
    assert blocks == ROWS and steps_total == 2 * PER_ROUND and slots % (2 * LANES) == 0 and slots <= 8 * LANES
    assert width_x == width_y and width_x % 2 == 0
    tile = (width_x, width_y * ROWS, LANES)
    ext = (ext_x, ext_y * ROWS, LANES)
    block = (width_y * ROWS, LANES)
    forward_fields = 4 * steps_total

    def face_structs(fields, more=0):
        columns = face_start(fields, "gy") + more // 2
        z = struct((columns * width_x, ROWS, LANES), BF)
        x = [struct((face_start(fields, "gx") + more,) + block, BF)] * 2
        return [z, z, *x]

    def first_hop(faces):
        z_even, z_odd, _, x_odd = faces
        z = [swapped(z_even, "gy", 0), swapped(z_odd, "gy", 1)]
        return z, swapped(x_odd, "gx", 1)

    def second_hop(fields, z, faces, first):
        ahead = faces.shape[0]
        corners = corner_blocks(fields, width_y)

        def corner_kernel(z_even, z_odd, faces, even, odd, *rim):
            place = Place()
            even[:ahead] = faces[...]
            z = (z_even, z_odd)
            pack_corners(place, fields, width_x, width_y, z, even, ahead, 0)
            pack_corners(place, fields, width_x, width_y, z, odd, 0, 1)
            for out in rim:
                for odd_y, ref in enumerate(z):
                    for n in range(4 * PER_ROUND):
                        value = ref[pl.ds(rim_z_at + n * width_x, width_x)].reshape(block)
                        out[4 * PER_ROUND * odd_y + n] = value

        outs = [struct((n + corners,) + block, BF) for n in (ahead, 0)]
        if first:
            outs.append(struct((8 * PER_ROUND,) + block, BF))
        even, odd, *rim = call(corner_kernel, outs, micros=0.3, limit=8)(*z, faces)
        rim = [lax.ppermute(r, "pair", [(0, 1), (1, 0)]) for r in rim]
        return [swapped(even, "gx", 0), swapped(odd, "gx", 1), *rim]

    whole = pl.BlockSpec(memory_space=VMEM)
    remain = pl.BlockSpec(memory_space=pltpu.HBM)

    def sample_kernel(source, forward, sample, pressure, done):
        copy = pltpu.make_async_copy(forward.at[:, 0], pressure, done)
        copy.start()
        local_x = source[0:1] - lax.axis_index("gx") * width_x
        local_y = source[1:2] - lax.axis_index("gy") * width_y
        inside = (local_x >= 0) & (local_x < width_x) & (local_y >= 0) & (local_y < width_y)
        where = jnp.where(inside, local_x * width_y + local_y, -1)
        cells = width_x * width_y
        chosen = lax.broadcasted_iota(jnp.int32, (cells, slots), 0) == where
        chosen = jnp.where(chosen, 1.0, 0.0).astype(BF)
        level = lax.broadcasted_iota(jnp.int32, (depth, slots), 0) == source[2:3]
        row = lax.broadcasted_iota(jnp.int32, (ROWS, slots), 0)
        result = jnp.zeros((ROWS, slots), F32)
        copy.wait()
        for t in range(steps_total):
            columns = lax.dot_general(
                pressure[t].reshape(cells, depth),
                chosen,
                (((0,), (0,)), ((), ())),
                preferred_element_type=F32,
            )
            picked = jnp.sum(jnp.where(level, columns, 0.0), axis=0, keepdims=True)
            result = jnp.where(row == t, picked, result)
        sample[...] = result

    samples = call(
        sample_kernel,
        struct((ROWS, slots), F32),
        scratch=[VMEM((steps_total, width_x, width_y, depth), BF), pltpu.SemaphoreType.DMA],
        specs=[whole, remain],
        micros=1.5,
        limit=8,
    )(source_cells.T, forward_field)
    state, samples = lax.optimization_barrier((adjoint_state, samples))
    samples = total_of(samples, "gx")

    def pack_kernel(state, speed, forward, cols, speed_cols, early, late, *outs):
        place = Place()
        for x in range(width_x):
            for b in range(blocks):
                at = pl.ds(b, width_y, stride=ROWS)
                here = slice(b * LANES, (b + 1) * LANES)
                for f in range(4):
                    cols[f, x, at, :] = state[0, f, x, :, here]
                speed_cols[x, at, :] = speed[x, :, here] * SCALE

        def load(f, x, y, n):
            ref = cols.at[f] if f < 4 else speed_cols
            return ref[x, column_rows(y, n), :]

        pack_faces(place, load, 5, width_x, width_y, outs[:2], outs[2:])

        mine_is_late = lax.axis_index("pair") == 0

        def one(n, carry):
            t, f = n // 4, lax.rem(n, 4)
            for is_late, ref, snap in ((True, late, t), (False, early, t + PER_ROUND)):
                number = snap * 4 + f
                for x in range(width_x):
                    for b in range(blocks):
                        ref[n, x, pl.ds(b, width_y, stride=ROWS), :] = forward[
                            snap, f, x, :, b * LANES : (b + 1) * LANES
                        ].astype(F32)
                for odd in (0, 1):
                    y = jnp.where(place.plus("gy", odd), width_y - 1, 0)
                    x = jnp.where(place.plus("gx", odd), width_x - 1, 0)
                    outs[2 + odd][rim_at + number] = ref[n, x].astype(BF)
                    value = ref[n, :, column_rows(y, 1), :].astype(BF)
                    to = rim_z_at + n * width_x

                    @pl.when(mine_is_late if is_late else jnp.logical_not(mine_is_late))
                    def _():
                        outs[odd][pl.ds(to, width_x)] = value

            return carry

        lax.fori_loop(0, 4 * PER_ROUND, one, 0)

    rim_z_at, rim_at = face_start(5, "gy") * width_x, face_start(5, "gx")
    packed = call(
        pack_kernel,
        [struct((4,) + tile, F32), struct(tile, F32)]
        + [struct((4 * PER_ROUND,) + tile, F32)] * 2
        + face_structs(5, forward_fields),
        micros=1.3,
        limit=12,
    )(state, sound_speed_sq, forward_field)
    cols, speed_cols, forward_early, forward_late = packed[:4]
    faces = packed[4:]
    z_first, x_first = first_hop(faces)

    def own_slopes(cols):
        def kernel(cols, out):
            altitude = Altitude()

            def one(f, carry):
                for x in range(width_x):
                    for y in range(width_y):
                        rows = column_rows(y, 1)
                        out[f, x, rows, :] = altitude(cols[f, x, rows, :])
                return carry

            lax.fori_loop(0, 4, one, 0)

        return call(kernel, struct((4,) + tile, F32), micros=0.8, limit=8)(cols)

    own_dz = own_slopes(cols)

    def face_slopes(z):
        def kernel(z_even, z_odd, out):
            place, altitude = Place(), Altitude()

            def one(x, carry):
                for odd, ref in enumerate((z_even, z_odd)):
                    plus = place.plus("gy", odd)
                    for f, reach in enumerate((HALO - 1, 1, HALO - 2, HALO - 1)):
                        deep = face_depth(f, "gy")
                        for d in range(reach):
                            at = face_start(f, "gy") * width_x + x * deep
                            at += jnp.where(plus, d, deep - 1 - d)
                            out[odd, f, x, d] = altitude(ref[at].astype(F32))
                return carry

            lax.fori_loop(0, width_x, one, 0)

        out = struct((2, 4, width_x, HALO - 1, ROWS, LANES), F32)
        return call(kernel, out, micros=0.6, limit=8)(*z)

    def slope_kernel(early, late, sample, *outs):
        *outs, held = outs
        held[...] = sample[...]
        altitude = Altitude()

        def one(n, carry):
            for ref, out in zip((early, late), outs):
                for x in range(width_x):
                    for y in range(width_y):
                        rows = column_rows(y, 1)
                        out[n, x, rows, :] = altitude(ref[n, x, rows, :])
            return carry

        lax.fori_loop(0, 4 * PER_ROUND, one, 0)

    slopes_early, slopes_late, samples = call(
        slope_kernel,
        [struct((4 * PER_ROUND,) + tile, F32)] * 2 + [struct(samples.shape, F32)],
        micros=2.7,
        limit=8,
    )(forward_early, forward_late, samples)
    samples = total_of(samples, "gy")

    z_first, x_first, samples, slopes_early, slopes_late, own_dz = lax.optimization_barrier(
        (z_first, x_first, samples, slopes_early, slopes_late, own_dz)
    )
    hop, hop_odd, rim_z = second_hop(5, z_first, faces[2], True)

    def inject_kernel(counts, receiver, misfit, samples, out):
        local_x = receiver[0:1] - (lax.axis_index("gx") * width_x - HALO)
        local_y = receiver[1:2] - (lax.axis_index("gy") * width_y - HALO)
        inside = (local_x >= 0) & (local_x < ext_x) & (local_y >= 0) & (local_y < ext_y)
        live = lax.broadcasted_iota(jnp.int32, (1, slots), 1) < counts[0]
        where = jnp.where(inside & live, local_x * ext_y + local_y, -1)
        cells = ext_x * ext_y
        chosen = lax.broadcasted_iota(jnp.int32, (cells, slots), 0) == where
        level = lax.broadcasted_iota(jnp.int32, (depth, slots), 0) == receiver[2:3]
        level = jnp.where(level, 1.0, 0.0).astype(BF)
        for t in range(steps_total):
            amplitude = misfit[t : t + 1] * samples[t : t + 1]
            head = amplitude.astype(BF).astype(F32)
            result = jnp.zeros((cells, depth), F32)
            for part in (head, amplitude - head):
                spread = jnp.where(chosen, part, 0.0).astype(BF)
                result += lax.dot_general(
                    spread, level, (((1,), (1,)), ((), ())), preferred_element_type=F32
                )
            for g in range(cells // ROWS):
                for b in range(blocks):
                    out[t, pl.ds(g * ROWS * ROWS + b, ROWS, stride=ROWS), :] = result[
                        g * ROWS : (g + 1) * ROWS, b * LANES : (b + 1) * LANES
                    ]

    injected = call(
        inject_kernel,
        struct((steps_total, ext_x * ext_y * ROWS, LANES), F32),
        specs=[pl.BlockSpec(memory_space=pltpu.SMEM)] + [whole] * 3,
        micros=1.6,
    )(pair_counts, receiver_cells.T, residuals.T, samples)

    rim_scratch = [
        VMEM((2, 4 * PER_ROUND) + block, F32),
        VMEM((2, 4 * PER_ROUND) + block, F32),
    ]

    def forward_of(place, columns, first, z_even, z_odd, z_other, x_even, x_odd, rim_y, rim_x):
        from_pair = (lax.axis_index("pair") == 0) == (first == 0)
        for odd, z, x in ((0, z_even, x_even), (1, z_odd, x_odd)):
            side_x = jnp.where(place.plus("gx", odd), 1, 0)
            side_y = jnp.where(place.plus("gy", odd), 1, 0)
            for n in range(4 * PER_ROUND):
                value = x[rim_at + 4 * first + n].astype(F32)
                if odd:
                    value = jnp.where(place.has("gx", odd), value, 0.0)
                rim_x[side_x, n] = value
                own_z = z[pl.ds(rim_z_at + n * width_x, width_x)].astype(F32).reshape(block)
                other = z_other[4 * PER_ROUND * odd + n].astype(F32)
                value = jnp.where(from_pair, own_z, other)
                if odd:
                    value = jnp.where(place.has("gy", odd), value, 0.0)
                rim_y[side_y, n] = value

        def reader(snap):
            base = 4 * (snap - first)

            def column(f, x, y):
                if isinstance(x, int) and x in (-1, width_x):
                    return rim_x[int(x > 0), base + f, column_rows(y, 1), :]
                if y in (-1, width_y):
                    rows = x * ROWS if isinstance(x, int) else pl.multiple_of(x * ROWS, ROWS)
                    return rim_y[int(y > 0), base + f, pl.ds(rows, ROWS), :]
                return columns[base + f, x, column_rows(y, 1), :]

            return column

        return reader

    def run_round(place, number, wind, inject, buffers, state_dz, own_dz, after):
        altitude = Altitude()
        winds = []
        for i in range(3):
            rows = [wind[i : i + 1, b * LANES : (b + 1) * LANES] for b in range(blocks)]
            winds.append(jnp.concatenate(rows, axis=0) * SCALE)
        for s in range(PER_ROUND):
            step = number * PER_ROUND + s
            snap = steps_total - 1 - step
            old, new = buffers[s % 2], buffers[(s + 1) % 2]

            def injected_at(x, y):
                start = (x * ext_y + y) * ROWS
                if not isinstance(start, int):
                    start = pl.multiple_of(start, ROWS)
                return inject[snap, pl.ds(start, ROWS), :]

            radius = 2 * (PER_ROUND - 1 - s) + 1
            advance(
                place,
                altitude,
                old,
                new,
                state_dz,
                winds,
                injected_at,
                radius,
                None if s else own_dz,
                width_x,
                width_y,
            )
            after(altitude, s, snap, new)

    def own(ref, f, x, y, n):
        return ref[f, HALO + x, column_rows(HALO + y, n), :]

    def fill(place, buffer, speed, cols, speed_cols, z_in, x_in, c_in, firsts):
        def store(f, x, y, n, value):
            ref = buffer.at[f] if f < 4 else speed
            ref[x, column_rows(y, n), :] = value

        for f in range(4):
            for x in range(width_x):
                store(f, HALO + x, HALO, width_y, cols[f, x])
        fields = 4
        if speed_cols is not None:
            fields = 5
            for x in range(width_x):
                store(4, HALO + x, HALO, width_y, speed_cols[x])
        place_edges(place, store, fields, width_x, width_y, z_in, x_in, c_in, firsts)

    def first_kernel(wind, inject, cols, own_dz, face_dz, speed_cols, z0, z1, x1, c0, c1, *refs):
        early, late, speed, *faces, here, there, dz_az, dz_p = refs
        place = Place()
        corners_at = (rim_at + forward_fields, 0)
        fill(place, here, speed, cols, speed_cols, (z0, z1), (c0, x1), (c0, c1), corners_at)

        def after(altitude, s, snap, state):
            out = (early, late)[s]
            for f in range(4):
                for x in range(width_x):
                    out[f, x] = own(state, f, x, 0, width_y)

        run_round(place, 0, wind, inject, (here, there), (speed, dz_az, dz_p), (own_dz, face_dz), after)

        def load(f, x, y, n):
            return own(here, f, x, y, n)

        pack_faces(place, load, 4, width_x, width_y, faces[:2], faces[2:])

    first = call(
        first_kernel,
        [struct((4,) + tile, F32)] * 2 + [struct(ext, F32)] + face_structs(4),
        scratch=[VMEM((4,) + ext, F32)] * 2 + [VMEM(ext, F32)] * 2,
        micros=6.0,
        limit=28,
    )(
        wind_profile, injected, cols, own_dz, face_slopes(z_first), speed_cols, *z_first, x_first, hop, hop_odd
    )
    early, late, speed_ext = first[:3]
    z_second, x_second = first_hop(first[3:])

    rim = (*z_first, rim_z, hop, x_first)

    def early_kernel(early, late, columns, slopes, z0, z1, zp, c0, x1, total, rim_y, rim_x):
        place = Place()
        reader = forward_of(place, columns, PER_ROUND, z0, z1, zp, c0, x1, rim_y, rim_x)
        total[...] = jnp.zeros_like(total)
        for s, state in ((0, early), (1, late)):
            add_increment(
                lambda f, x, y: state[f, x, column_rows(y, 1), :],
                reader(steps_total - 1 - s),
                lambda f, x, y: slopes[
                    4 * (steps_total - 1 - s - PER_ROUND) + f, x, column_rows(y, 1), :
                ],
                total,
                width_x,
                width_y,
            )

    total = call(early_kernel, struct((4,) + tile, F32), scratch=rim_scratch, micros=2.3, limit=16)(
        early, late, forward_early, slopes_early, *rim
    )
    late_dz = own_slopes(late)
    z_second, x_second, late_dz = lax.optimization_barrier((z_second, x_second, late_dz))
    again, again_odd = second_hop(4, z_second, first[5], False)

    half = depth // 2
    half_blocks = blocks // 2

    def second_kernel(
        wind, inject, cols, own_dz, face_dz, speed, total, columns, slopes, *refs
    ):
        rims, (z0, z1, x1, c0, c1), refs = refs[:5], refs[5:10], refs[10:]
        last, mine, other, scales, here, there, dz_az, dz_p, sums, rim_y, rim_x = refs
        place = Place()
        fill(place, here, None, cols, None, (z0, z1), (c0, x1), (c0, c1), (face_start(4, "gx"), 0))
        reader = forward_of(place, columns, 0, *rims, rim_y, rim_x)
        sums[...] = total[...]

        def after(altitude, s, snap, state):
            add_increment(
                lambda f, x, y: own(state, f, x, y, 1),
                reader(snap),
                lambda f, x, y: slopes[4 * snap + f, x, column_rows(y, 1), :],
                sums,
                width_x,
                width_y,
            )

        run_round(place, 1, wind, inject, (here, there), (speed, dz_az, dz_p), (own_dz, face_dz), after)
        me = lax.axis_index("pair")
        for f in range(4):
            for x in range(width_x):
                last[f, x] = own(here, f, x, 0, width_y)

        def sums_at(f, x, part, b):
            return sums[f, x, pl.ds(part * half_blocks + b, width_y, stride=ROWS), :]

        for f in range(4):
            for b in range(half_blocks):
                here_lanes = slice(b * LANES, (b + 1) * LANES)
                largest = jnp.abs(sums_at(f, 0, 1 - me, b))
                for x in range(1, width_x):
                    largest = jnp.maximum(largest, jnp.abs(sums_at(f, x, 1 - me, b)))
                largest = jnp.maximum(jnp.max(largest, axis=0, keepdims=True), 1e-30)
                scales[f : f + 1, here_lanes] = largest * (0.5 / 32767.0)
                inverse = 32767.0 / largest
                for x in range(0, width_x, 2):
                    two = [sums_at(f, x + i, 1 - me, b) * inverse for i in (0, 1)]
                    two = jnp.round(jnp.concatenate(two, axis=0))
                    other[f, x // 2, :, here_lanes] = two.astype(jnp.int32).astype(jnp.int16)
        for f in range(4):
            for x in range(width_x):
                mine[f, x] = sums[f, x]

    kernel_half = struct((4, width_x, width_y, half), F32)
    last, mine, other, scales = call(
        second_kernel,
        [
            struct((4,) + tile, F32),
            struct((4,) + tile, F32),
            struct((4, width_x // 2, 2 * width_y, half), jnp.int16),
            struct((4, half), F32),
        ],
        scratch=[VMEM((4,) + ext, F32)] * 2
        + [VMEM(ext, F32)] * 2
        + [VMEM((4,) + tile, F32)]
        + rim_scratch,
        micros=9.0,
        limit=30,
    )(
        wind_profile,
        injected,
        late,
        late_dz,
        face_slopes(z_second),
        speed_ext,
        total,
        forward_late,
        slopes_late,
        *rim,
        *z_second,
        x_second,
        again,
        again_odd,
    )
    across = [(0, 1), (1, 0)]
    other, scales = lax.ppermute(other, "pair", across), lax.ppermute(scales, "pair", across)

    def final_kernel(last, sums, final, mine):
        me = lax.axis_index("pair")
        for f in range(4):
            for x in range(width_x):
                for b in range(blocks):
                    final[0, f, x, :, b * LANES : (b + 1) * LANES] = last[
                        f, x, pl.ds(b, width_y, stride=ROWS), :
                    ]
                for b in range(half_blocks):
                    mine[f, x, :, b * LANES : (b + 1) * LANES] = (
                        0.5 * sums[f, x, pl.ds(me * half_blocks + b, width_y, stride=ROWS), :]
                    )

    final, mine = call(
        final_kernel, [struct(adjoint_state.shape, F32), kernel_half], micros=1.0, limit=8
    )(last, mine)

    def sum_kernel(mine, other, scales, out):
        for f in range(4):
            for x in range(0, width_x, 2):
                two = other[f, x // 2].astype(jnp.int32).astype(F32) * scales[f : f + 1]
                for i in (0, 1):
                    out[f, x + i] = mine[f, x + i] + two[i * width_y : (i + 1) * width_y]

    kernels = call(sum_kernel, kernel_half, micros=0.8, limit=8)(mine, other, scales)
    return (kernels, final)


def solution(mesh):
    assert mesh.shape["pair"] == 2 and mesh.shape["gx"] % 2 == 0 and mesh.shape["gy"] % 2 == 0
    in_specs = (
        P("gx", "gy", None),
        P(),
        P(None, None, "gx", "gy", None),
        P("pair", None, "gx", "gy", None),
        P("pair"),
        P("pair", None),
        P("pair", None),
        P("pair", None),
    )
    out_specs = (P(None, "gx", "gy", "pair"), P("pair", None, "gx", "gy", None))
    return jax.shard_map(shards, mesh=mesh, in_specs=in_specs, out_specs=out_specs, check_vma=False)
```
